32 devices in a mesh: dp: 8 (over z, x), tensor: 4 (over y, core).
Axes of the slice: x: 2, y: 2, z: 4, core: 2. Of those that a mesh axis runs over, the one named last changes fastest.
Arguments:
- tokens: bfloat16 [32768, 384], P(('dp', 'tensor')), may hold values from -6 to 6
- cotangent: bfloat16 [32768, 384], P(('dp', 'tensor')), may hold values from -6 to 6
- shapes: int32 [64, 2, 33], P('dp'), may hold values from 0 to 14, as said below
- head_mask: int32 [8], P('tensor'), may hold values from 0 to 1, as said below
- w_expand: bfloat16 [384, 1536], P(None, 'tensor'), may hold values from -0.3125 to 0.3125
- w_depth: bfloat16 [9, 1536], P(None, 'tensor'), may hold values from -2 to 2
- w_project: bfloat16 [1536, 384], P('tensor'), may hold values from -0.15625 to 0.15625
- gain_conv: float32 [384], replicated, may hold values from 0.1 to 1.9
- gain_attn: float32 [384], replicated, may hold values from 0.1 to 1.9
- w_qkv: bfloat16 [384, 3, 512], P(None, None, 'tensor'), may hold values from -0.3125 to 0.3125
- w_out: bfloat16 [512, 384], P('tensor'), may hold values from -1 to 1
- gain_mlp: float32 [384], replicated, may hold values from 0.1 to 1.9
- w_up: bfloat16 [384, 1536], P(None, 'tensor'), may hold values from -0.3125 to 0.3125
- w_down: bfloat16 [1536, 384], P('tensor'), may hold values from -0.15625 to 0.15625
Outputs:
- out_tokens: bfloat16 [32768, 384], P(('dp', 'tensor'))
- grad_tokens: bfloat16 [32768, 384], P(('dp', 'tensor'))
- grad_expand: float32 [384, 1536], P(None, 'tensor')
- grad_depth: float32 [9, 1536], P(None, 'tensor')
- grad_project: float32 [1536, 384], P('tensor')
- grad_gain_conv: float32 [384], replicated
- grad_gain_attn: float32 [384], replicated
- grad_qkv: float32 [384, 3, 512], P(None, None, 'tensor')
- grad_out: float32 [512, 384], P('tensor')
- grad_gain_mlp: float32 [384], replicated
- grad_up: float32 [384, 1536], P(None, 'tensor')
- grad_down: float32 [1536, 384], P('tensor')
The draws below stay inside these ranges and needn't reach their ends.
Inputs may be any that keep to these rules, and one draw needn't show every extreme that they name: `shapes`: in every pack the used slots come first and their images fill the pack's 512 tokens exactly; an unused slot has 0 rows and 0 columns, and every pack has one. Slot 0 of every pack has 14 rows. Every image but a pack's last two has 4 to 14 patches a side; the last two may be narrower, one of them a single row. `head_mask`: exactly 6 of the 8 entries are 1, the others 0.
All inputs are finite; a program needn't handle non-finite values.
Results may differ from the reference program's by a relative error of at most 0.02.
Values may be sent and summed in bfloat16 or wider, within the bound.
No kernel may reach another device: no remote copies, remote signals or barrier semaphores. Data moves between devices by JAX's collectives and lax.ppermute only.
A program may use at most 192 MiB of HBM per device.

```python
import math
import jax
import jax.numpy as jnp
from jax import lax

D = 384
EXP = 1536
HID = 1536
HEADS = 8
HSZ = 64
ACTIVE = 6
PACK = 512
SIDE_LO = 4
SIDE_HI = 14
IMG_SLOTS = 33
TOKENS = 32768
NPACK = 64


def draw_shapes(key, part):
    key = jax.random.fold_in(key, 11)
    side_keys = jax.random.split(key, 2)
    heights = jax.random.randint(side_keys[0], (NPACK, IMG_SLOTS), SIDE_LO, SIDE_HI + 1, dtype=jnp.int32)
    widths = jax.random.randint(side_keys[1], (NPACK, IMG_SLOTS), SIDE_LO, SIDE_HI + 1, dtype=jnp.int32)
    slot_ids = jnp.arange(IMG_SLOTS, dtype=jnp.int32)
    heights = jnp.where(slot_ids[None, :] == 0, SIDE_HI, heights).astype(jnp.int32)
    sizes = heights * widths
    ends = jnp.cumsum(sizes, axis=1).astype(jnp.int32)
    kept = ends <= PACK
    used_tokens = jnp.sum(jnp.where(kept, sizes, 0), axis=1).astype(jnp.int32)
    remain = (PACK - used_tokens).astype(jnp.int32)
    kept_count = jnp.sum(kept.astype(jnp.int32), axis=1).astype(jnp.int32)
    rows_fill = (remain // SIDE_HI).astype(jnp.int32)
    rest = (remain - rows_fill * SIDE_HI).astype(jnp.int32)
    first_slot = kept_count
    second_slot = (kept_count + (rows_fill > 0).astype(jnp.int32)).astype(jnp.int32)
    block_fill = (slot_ids[None, :] == first_slot[:, None]) & (rows_fill[:, None] > 0)
    row_fill = (slot_ids[None, :] == second_slot[:, None]) & (rest[:, None] > 0)
    heights = jnp.where(kept, heights, jnp.where(block_fill, rows_fill[:, None], jnp.where(row_fill, 1, 0)))
    widths = jnp.where(kept, widths, jnp.where(block_fill, SIDE_HI, jnp.where(row_fill, rest[:, None], 0)))
    return jnp.stack([heights, widths], axis=1).astype(jnp.int32)


def draw_head_mask(key, part):
    key = jax.random.fold_in(key, 23)
    order = jax.random.permutation(key, HEADS)
    return (order < ACTIVE).astype(jnp.int32)


def levels(rng, shape, cuts, least, largest):
    def one(position, blocks):
        steps = jax.random.uniform(jax.random.fold_in(jax.random.fold_in(rng, 6), position), (blocks,), jnp.float32, least / len(cuts), largest / len(cuts))
        return jnp.repeat(jnp.exp(steps), shape[position] // blocks).reshape((-1,) + (1,) * (len(shape) - position - 1))

    factor_of = one(*cuts[0])
    for cut in cuts[1:]:
        factor_of = factor_of * one(*cut)
    return factor_of


def gaussian(stream_key, dims, deviation, reach, cuts=(), kind=jnp.bfloat16):
    array = deviation * jax.random.normal(stream_key, dims, jnp.float32)
    if cuts:
        array = array * levels(stream_key, dims, cuts, -0.22, 0.18)
    return jnp.clip(array, -reach, reach).astype(kind)


def setup_inputs(seed: int = 0) -> dict:
    splits = jax.random.split(jax.random.key(seed), 15)
    tokens = gaussian(splits[0], (TOKENS, D), 1.0, 6.0, ((0, 32),))
    cotangent = gaussian(splits[1], (TOKENS, D), 1.0, 6.0, ((0, 32),))
    shapes = draw_shapes(jax.random.fold_in(splits[14], 71), 0)
    head_mask = draw_head_mask(jax.random.fold_in(splits[14], 71), 0)
    w_expand = gaussian(splits[4], (D, EXP), D ** -0.5, 0.3125, ((1, 4),))
    w_depth = gaussian(splits[5], (9, EXP), 9 ** -0.5, 2.0, ((1, 4),))
    w_project = gaussian(splits[6], (EXP, D), EXP ** -0.5, 0.15625, ((0, 4),))
    gain_conv = jnp.clip(1.0 + 0.18 * jax.random.normal(splits[7], (D,), jnp.float32), 0.1, 1.9)
    gain_attn = jnp.clip(1.0 + 0.18 * jax.random.normal(splits[8], (D,), jnp.float32), 0.1, 1.9)
    w_qkv = gaussian(splits[9], (D, 3, HEADS * HSZ), D ** -0.5, 0.3125, ((2, 4),))
    w_out = gaussian(splits[10], (HEADS * HSZ, D), (HEADS * HSZ // 16) ** -0.5, 1.0, ((0, 4),))
    gain_mlp = jnp.clip(1.0 + 0.18 * jax.random.normal(splits[11], (D,), jnp.float32), 0.1, 1.9)
    w_up = gaussian(splits[12], (D, HID), D ** -0.5, 0.3125, ((1, 4),))
    w_down = gaussian(splits[13], (HID, D), HID ** -0.5, 0.15625, ((0, 4),))
    return dict(tokens=tokens, cotangent=cotangent, shapes=shapes, head_mask=head_mask, w_expand=w_expand, w_depth=w_depth, w_project=w_project, gain_conv=gain_conv, gain_attn=gain_attn, w_qkv=w_qkv, w_out=w_out, gain_mlp=gain_mlp, w_up=w_up, w_down=w_down)


@jax.custom_vjp
def low(v):
    return lax.optimization_barrier(v.astype(jnp.bfloat16)).astype(jnp.float32)

@jax.custom_vjp
def low_back(v):
    return v

def low_keep(v):
    return (low(v), None)

def low_pass(kept, grad):
    return (grad,)

def back_keep(v):
    return (v, None)

def back_low(kept, grad):
    return (low(grad),)
low.defvjp(low_keep, low_pass)
low_back.defvjp(back_keep, back_low)
epsilon = 1e-05
masked_score = -1e+30

def normalize(values, scale_gain):
    row_mean = lax.optimization_barrier(jnp.mean(values, axis=-1, keepdims=True))
    centred = values - row_mean
    spread = lax.optimization_barrier(jnp.mean(centred * centred, axis=-1, keepdims=True))
    return centred * lax.rsqrt(spread + epsilon) * scale_gain

def gelu_exact(values):
    return jax.nn.gelu(values, approximate=False)

def pick_rows(source, where_from):
    return source[where_from]

def geometry(shapes, pack_len):
    heights = shapes[:, 0, :].astype(jnp.int32)
    widths = shapes[:, 1, :].astype(jnp.int32)
    sizes = heights * widths
    ends = jnp.cumsum(sizes, axis=1).astype(jnp.int32)
    starts = (ends - sizes).astype(jnp.int32)
    places = jnp.arange(pack_len, dtype=jnp.int32)
    segment = lax.optimization_barrier(jnp.sum((ends[:, None, :] <= places[None, :, None]).astype(jnp.int32), axis=2)).astype(jnp.int32)
    slot_ids = jnp.arange(shapes.shape[2], dtype=jnp.int32)
    picked = (segment[:, :, None] == slot_ids[None, None, :]).astype(jnp.int32)
    image_start = lax.optimization_barrier(jnp.sum(picked * starts[:, None, :], axis=2)).astype(jnp.int32)
    height = lax.optimization_barrier(jnp.sum(picked * heights[:, None, :], axis=2)).astype(jnp.int32)
    image_width = lax.optimization_barrier(jnp.sum(picked * widths[:, None, :], axis=2)).astype(jnp.int32)
    safe_width = jnp.maximum(image_width, 1)
    offset = places[None, :] - image_start
    grid_row = (offset // safe_width).astype(jnp.int32)
    grid_col = (offset - grid_row * safe_width).astype(jnp.int32)
    near_list = []
    inside_list = []
    for tap_index in range(9):
        step_down = tap_index // 3 - 1
        step_right = tap_index % 3 - 1
        inside = (grid_row + step_down >= 0) & (grid_row + step_down < height) & (grid_col + step_right >= 0) & (grid_col + step_right < image_width)
        target = jnp.where(inside, places[None, :] + step_down * image_width + step_right, places[None, :])
        near_list.append(target.astype(jnp.int32))
        inside_list.append(inside.astype(jnp.float32))
    return (segment, jnp.stack(near_list, 1), jnp.stack(inside_list, 1))

def depth_mix(packed, kernel, neighbour, inside_mask):
    total_mix = jnp.zeros(packed.shape, jnp.float32)
    for tap_index in range(9):
        taken = jax.vmap(pick_rows)(packed, neighbour[:, tap_index, :])
        total_mix = total_mix + kernel[tap_index] * inside_mask[:, tap_index, :, None] * taken
    return total_mix

def dot_high(left_side, right_side):
    return jnp.dot(left_side, right_side, precision=lax.Precision.HIGHEST, preferred_element_type=jnp.float32)

def attend_pack(operands):
    queries, keys_in, values_in, segment = operands
    raw_scores = jnp.einsum('qhd,khd->hqk', queries, keys_in, precision=lax.Precision.HIGHEST) * HSZ ** (-0.5)
    scores = low_back(raw_scores)
    same_image = segment[:, None] == segment[None, :]
    scores = jnp.where(same_image[None], scores, masked_score)
    highest = lax.optimization_barrier(jnp.max(scores, axis=-1, keepdims=True))
    log_totals = highest + jnp.log(lax.optimization_barrier(jnp.sum(jnp.exp(scores - highest), axis=-1, keepdims=True)))
    probs = low(jnp.exp(scores - log_totals))
    return jnp.einsum('hqk,khd->qhd', probs, values_in, precision=lax.Precision.HIGHEST)

def forward(token_rows, weights, segment, neighbour, inside_mask, mask_float):
    expand_w, depth_w, project_w, gain_c, gain_a, qkv_w, out_w, gain_m, up_w, down_w = weights
    rows_here = token_rows.shape[0]
    pack_count = rows_here // PACK
    expanded = low_back(dot_high(token_rows, expand_w))
    mixed = depth_mix(expanded.reshape(pack_count, PACK, EXP), depth_w, neighbour, inside_mask).reshape(rows_here, EXP)
    acted = low(mixed * jax.nn.sigmoid(mixed))
    projected = low_back(dot_high(acted, project_w))
    residual_one = token_rows + normalize(projected, gain_c)
    attn_in = low(normalize(residual_one, gain_a))
    qkv_flat = qkv_w.reshape(D, 3 * HEADS * HSZ)
    projections = low(low_back(dot_high(attn_in, qkv_flat)))
    split_heads = projections.reshape(pack_count, PACK, 3, HEADS, HSZ)
    heads_out = lax.map(jax.checkpoint(attend_pack), (split_heads[:, :, 0], split_heads[:, :, 1], split_heads[:, :, 2], segment))
    merged = low(low_back((heads_out * mask_float[None, None, :, None]).reshape(rows_here, HEADS * HSZ)))
    residual_two = residual_one + low_back(dot_high(merged, out_w))
    mlp_in = low(normalize(residual_two, gain_m))
    hidden_pre = low_back(dot_high(mlp_in, up_w))
    hidden_act = low(gelu_exact(hidden_pre))
    return residual_two + low_back(dot_high(hidden_act, down_w))

def reference(tokens, cotangent, shapes, head_mask, w_expand, w_depth, w_project, gain_conv, gain_attn, w_qkv, w_out, gain_mlp, w_up, w_down):
    params = (w_expand.astype(jnp.float32), w_depth.astype(jnp.float32), w_project.astype(jnp.float32), gain_conv.astype(jnp.float32), gain_attn.astype(jnp.float32), w_qkv.astype(jnp.float32), w_out.astype(jnp.float32), gain_mlp.astype(jnp.float32), w_up.astype(jnp.float32), w_down.astype(jnp.float32))
    mask_float = head_mask.astype(jnp.float32)
    pack_total = shapes.shape[0]
    group_packs = math.gcd(pack_total, max(1, 4096 // PACK))
    steps_count = pack_total // group_packs
    rows_group = group_packs * PACK
    segment, neighbour, inside_mask = geometry(shapes, PACK)
    blocks = (tokens.astype(jnp.float32).reshape(steps_count, rows_group, D), cotangent.astype(jnp.float32).reshape(steps_count, rows_group, D), segment.reshape(steps_count, group_packs, PACK), neighbour.reshape(steps_count, group_packs, 9, PACK), inside_mask.reshape(steps_count, group_packs, 9, PACK))

    def one_group(running_totals, pieces):
        token_rows, cot_rows, seg_rows, near_rows, inside_rows = pieces

        def forward_rows(rows_in, weights):
            return forward(rows_in, weights, seg_rows, near_rows, inside_rows, mask_float)
        result, pullback = jax.vjp(forward_rows, token_rows, params)
        grad_rows, grad_weights = pullback(cot_rows)
        running_totals = jax.tree.map(lambda running, fresh: running + fresh, running_totals, grad_weights)
        return (running_totals, (result.astype(jnp.bfloat16), grad_rows.astype(jnp.bfloat16)))
    start_totals = tuple((jnp.zeros(weight.shape, jnp.float32) for weight in params))
    final_totals, (out_rows, grad_rows) = lax.scan(one_group, start_totals, blocks)
    return (out_rows.reshape(tokens.shape), grad_rows.reshape(tokens.shape), final_totals[0], final_totals[1], final_totals[2], final_totals[3], final_totals[4], final_totals[5], final_totals[6], final_totals[7], final_totals[8], final_totals[9])
```

```python
import jax
import jax.numpy as jnp
from jax import lax
from jax.sharding import PartitionSpec as P

HSZ = 64
PACK = 512

epsilon = 1e-05
masked_score = -1e30
f32 = jnp.float32
bf16 = jnp.bfloat16


def normalize(values, scale_gain):
    row_mean = jnp.mean(values, axis=-1, keepdims=True)
    centred = values - row_mean
    spread = jnp.mean(centred * centred, axis=-1, keepdims=True)
    return centred * lax.rsqrt(spread + epsilon) * scale_gain


def gelu_exact(values):
    return jax.nn.gelu(values, approximate=False)


def geometry(shapes, pack_len):
    heights = shapes[:, 0, :]
    widths = shapes[:, 1, :]
    sizes = heights * widths
    ends = jnp.cumsum(sizes, axis=1)
    starts = ends - sizes
    places = jnp.arange(pack_len, dtype=jnp.int32)
    segment = jnp.sum((ends[:, None, :] <= places[None, :, None]).astype(jnp.int32), axis=2)
    slot_ids = jnp.arange(shapes.shape[2], dtype=jnp.int32)
    picked = (segment[:, :, None] == slot_ids[None, None, :]).astype(jnp.int32)
    image_start = jnp.sum(picked * starts[:, None, :], axis=2)
    height = jnp.sum(picked * heights[:, None, :], axis=2)
    image_width = jnp.sum(picked * widths[:, None, :], axis=2)
    safe_width = jnp.maximum(image_width, 1)
    offset = places[None, :] - image_start
    grid_row = offset // safe_width
    grid_col = offset - grid_row * safe_width
    above = grid_row >= 1
    mover = (
        (places[None, :, None] - image_width[:, :, None] == places[None, None, :]) & above[:, :, None]
    ).astype(bf16)
    left = (grid_col >= 1).astype(f32)
    right = (grid_col + 1 < image_width).astype(f32)
    return segment, mover, left, right


def slide(packed, step):
    filler = jnp.zeros((packed.shape[0], 1, packed.shape[2]), packed.dtype)
    if step > 0:
        return jnp.concatenate([packed[:, 1:], filler], axis=1)
    return jnp.concatenate([filler, packed[:, :-1]], axis=1)


def moved(packed, mover):
    low = packed.astype(bf16)
    up = jnp.einsum("ptu,puc->ptc", mover, low, preferred_element_type=f32)
    down = jnp.einsum("put,puc->ptc", mover, low, preferred_element_type=f32)
    return [up, packed, down]


def mix(rows, kernel, left, right):
    cols = [sum(rows[a] * kernel[3 * a + b] for a in range(3)) for b in range(3)]
    return cols[1] + left[:, :, None] * slide(cols[0], -1) + right[:, :, None] * slide(cols[2], 1)


def mm(a, b):
    return jnp.dot(a, b, preferred_element_type=f32)


def mm_t(a, b):
    return lax.dot_general(a, b, (((1,), (1,)), ((), ())), preferred_element_type=f32)


def t_mm(a, b):
    return lax.dot_general(a, b, (((0,), (0,)), ((), ())), preferred_element_type=f32)


def masked_scores(queries, keys_in, segment):
    scores = jnp.einsum("phqd,phkd->phqk", queries, keys_in, preferred_element_type=f32) * HSZ**-0.5
    same_image = segment[:, :, None] == segment[:, None, :]
    return jnp.where(same_image[:, None], scores, masked_score)


def per_device(
    tokens, cotangent, shapes, head_mask, w_expand, w_depth, w_project, gain_conv, gain_attn, w_qkv, w_out,
    gain_mlp, w_up, w_down,
):
    rows, width = tokens.shape
    packs = rows // PACK
    tensor_size = lax.axis_size("tensor")
    dp_size = lax.axis_size("dp")
    me_tensor = lax.axis_index("tensor")
    me_dp = lax.axis_index("dp")

    def swap_tensor(x, bit):
        return lax.ppermute(x, "tensor", [(i, i ^ bit) for i in range(tensor_size)])

    def swap_dp(x, bit):
        return lax.ppermute(x, "dp", [(i, i ^ bit) for i in range(dp_size)])

    def gather(x):
        far = swap_tensor(x, 2)
        return [x, swap_tensor(x, 1), far, swap_tensor(far, 1)]

    def add(a, b):
        return (a.astype(f32) + b.astype(f32)).astype(a.dtype)

    def reduce_blocks(blocks):
        pair = swap_tensor(jnp.concatenate([blocks[1], blocks[3]]), 1)
        n = blocks[0].shape[0]
        near = add(blocks[0], pair[:n])
        far = swap_tensor(add(blocks[2], pair[n:]), 2)
        x = add(near, far)
        bits = [1 << b for b in range(dp_size.bit_length() - 1)]
        halved = []
        for bit in bits:
            if x.shape[0] % 2:
                x = add(x, swap_dp(x, bit))
                continue
            halved.append(bit)
            mine = ((me_dp & bit) != 0).astype(jnp.int32)
            half = x.shape[0] // 2
            send = lax.dynamic_slice_in_dim(x, (1 - mine) * half, half, 0)
            keep = lax.dynamic_slice_in_dim(x, mine * half, half, 0)
            x = add(keep, swap_dp(send, bit))
        for bit in reversed(halved):
            other = swap_dp(x, bit)
            mine = (me_dp & bit) != 0
            x = jnp.concatenate([jnp.where(mine, other, x), jnp.where(mine, x, other)])
        return x

    own_shapes = lax.dynamic_slice_in_dim(shapes, me_tensor * packs, packs, 0)
    segment, mover, left, right = geometry(own_shapes, PACK)

    we = jnp.concatenate(gather(w_expand), axis=1)
    wd = jnp.concatenate(gather(w_depth), axis=1).astype(f32)
    wp = jnp.concatenate(gather(w_project), axis=0)
    wq = jnp.concatenate(gather(w_qkv.reshape(width, -1, 2, HSZ)), axis=2)
    wo = jnp.concatenate(gather(w_out), axis=0)
    wu = jnp.concatenate(gather(w_up), axis=1)
    wn = jnp.concatenate(gather(w_down), axis=0)
    mask = jnp.concatenate(gather(head_mask), axis=0).astype(f32)
    heads = mask.shape[0]
    wq = wq.reshape(width, 3 * heads * HSZ)

    channels = we.shape[1]
    expanded = mm(tokens, we).reshape(packs, PACK, channels)
    mixed = mix(moved(expanded, mover), wd, left, right).reshape(rows, channels)
    q = jax.nn.sigmoid(mixed)
    acted = (mixed * q).astype(bf16)
    projected = mm(acted, wp)
    conv_out, conv_pull = jax.vjp(normalize, projected, gain_conv)
    residual_one = tokens.astype(f32) + conv_out
    attn_in, attn_pull = jax.vjp(normalize, residual_one, gain_attn)
    attn_low = attn_in.astype(bf16)

    qkv = mm(attn_low, wq).astype(bf16).reshape(packs, PACK, 3, heads, HSZ).transpose(2, 0, 3, 1, 4)
    queries, keys_in, values_in = qkv[0], qkv[1], qkv[2]
    scores = masked_scores(queries, keys_in, segment)
    probs = jax.nn.softmax(scores, axis=-1)
    probs_low = probs.astype(bf16)
    heads_out = jnp.einsum("phqk,phkd->pqhd", probs_low, values_in, preferred_element_type=f32)
    merged = (heads_out * mask[None, None, :, None]).astype(bf16).reshape(rows, heads * HSZ)
    residual_two = residual_one + mm(merged, wo)
    mlp_in, mlp_pull = jax.vjp(normalize, residual_two, gain_mlp)
    mlp_low = mlp_in.astype(bf16)
    hidden_pre = mm(mlp_low, wu)
    hidden_act, gelu_pull = jax.vjp(gelu_exact, hidden_pre)
    hidden_low = hidden_act.astype(bf16)
    out_tokens = (residual_two + mm(hidden_low, wn)).astype(bf16)

    def split(x):
        return [x[:, i * (x.shape[1] // 4) : (i + 1) * (x.shape[1] // 4)].astype(bf16) for i in range(4)]

    grad_down = split(t_mm(cotangent, hidden_low))
    grad_pre = gelu_pull(mm_t(cotangent, wn))[0].astype(bf16)
    grad_up = split(t_mm(mlp_low, grad_pre))
    mlp_sum = reduce_blocks([jnp.concatenate([a, b]) for a, b in zip(grad_down, grad_up)])
    grad_two_part, grad_gain_mlp = mlp_pull(mm_t(grad_pre, wu))
    grad_two = cotangent.astype(f32) + grad_two_part
    grad_two_low = grad_two.astype(bf16)
    grad_out = split(t_mm(grad_two_low, merged))
    grad_merged = mm_t(grad_two_low, wo).astype(bf16)
    grad_heads = grad_merged.reshape(packs, PACK, heads, HSZ) * mask.astype(bf16)[None, None, :, None]
    grad_heads = grad_heads.transpose(0, 2, 1, 3)
    grad_probs = jnp.einsum("phqd,phkd->phqk", grad_heads, values_in, preferred_element_type=f32)
    centre = jnp.sum(probs * grad_probs, axis=-1, keepdims=True)
    grad_scores = (probs * (grad_probs - centre)).astype(bf16)
    gq = jnp.einsum("phqk,phkd->pqhd", grad_scores, keys_in, preferred_element_type=f32) * HSZ**-0.5
    gk = jnp.einsum("phqk,phqd->pkhd", grad_scores, queries, preferred_element_type=f32) * HSZ**-0.5
    gv = jnp.einsum("phqk,phqd->pkhd", probs_low, grad_heads, preferred_element_type=f32)
    grad_proj = jnp.stack([gq, gk, gv], axis=2).astype(bf16).reshape(rows, -1)
    grad_qkv = t_mm(attn_low, grad_proj).reshape(width, 3, 4, heads * HSZ // 4).astype(bf16)
    attn_sum = reduce_blocks(
        [jnp.concatenate([grad_qkv[:, 0, i], grad_qkv[:, 1, i], grad_qkv[:, 2, i], grad_out[i]]) for i in range(4)]
    )
    grad_one_part, grad_gain_attn = attn_pull(mm_t(grad_proj, wq))
    grad_one = grad_two + grad_one_part
    grad_projected, grad_gain_conv = conv_pull(grad_one)
    grad_proj_low = grad_projected.astype(bf16)
    grad_project = split(t_mm(grad_proj_low, acted))
    grad_acted = mm_t(grad_proj_low, wp)
    grad_mixed = (grad_acted * q * (1.0 + mixed * (1.0 - q))).reshape(packs, PACK, channels)
    grad_rows = moved(grad_mixed, mover)
    from_left = left[:, :, None] * slide(expanded, -1)
    from_right = right[:, :, None] * slide(expanded, 1)
    grad_depth = jnp.stack(
        [
            jnp.sum(grad_rows[2 - a] * part, axis=(0, 1))
            for a in range(3)
            for part in (from_left, expanded, from_right)
        ]
    )
    grad_expanded = mix(grad_rows, wd[::-1], left, right).reshape(rows, channels).astype(bf16)
    grad_expand = split(t_mm(tokens, grad_expanded))
    gains = jnp.stack([grad_gain_conv, grad_gain_attn, grad_gain_mlp])
    for bit in (1, 2):
        gains = gains + swap_tensor(gains, bit)
    for b in range(dp_size.bit_length() - 1):
        gains = gains + swap_dp(gains, 1 << b)
    tail = jnp.zeros((16 - 9, width), bf16)
    conv_sum = reduce_blocks(
        [
            jnp.concatenate([a, b, c, tail])
            for a, b, c in zip(grad_expand, grad_project, split(grad_depth))
        ]
    )
    grad_tokens = (grad_one + mm_t(grad_expanded, we)).astype(bf16)

    mlp_sum, attn_sum, conv_sum = (s.astype(f32) for s in (mlp_sum, attn_sum, conv_sum))
    w = width
    part = w_out.shape[0]
    out_qkv = jnp.stack([attn_sum[:w], attn_sum[w : 2 * w], attn_sum[2 * w : 3 * w]], axis=1)
    return (
        out_tokens,
        grad_tokens,
        conv_sum[:w],
        conv_sum[2 * w : 2 * w + 9],
        conv_sum[w : 2 * w].T,
        gains[0],
        gains[1],
        out_qkv,
        attn_sum[3 * w :].T,
        gains[2],
        mlp_sum[w:],
        mlp_sum[:w].T,
    )


def solution(mesh):
    rows = P(("dp", "tensor"), None)
    cols = P(None, "tensor")
    down = P("tensor", None)
    return jax.shard_map(
        per_device,
        mesh=mesh,
        in_specs=(
            rows, rows, P("dp", None, None), P("tensor"), cols, cols, down, P(), P(), P(None, None, "tensor"), down,
            P(), cols, down,
        ),
        out_specs=(rows, rows, cols, cols, down, P(), P(), P(None, None, "tensor"), down, P(), cols, down),
        check_vma=False,
    )
```

```python
import functools
import jax
import jax.numpy as jnp
from jax import lax
from jax.experimental import pallas as pl
from jax.experimental.pallas import tpu as pltpu
from jax.sharding import PartitionSpec as P

HSZ = 64
PACK = 512
WINDOWS = (0, 240, 256)
SPAN = 256
UP_ROWS = (0, 256, 496, 512)
DOWN_ROWS = (0, 240, 480, 512)

epsilon = 1e-05
f32 = jnp.float32
bf16 = jnp.bfloat16


def mm(a, b):
    return jnp.dot(a, b, preferred_element_type=f32)


def mm_t(a, b):
    return lax.dot_general(a, b, (((1,), (1,)), ((), ())), preferred_element_type=f32)


def t_mm(a, b):
    return lax.dot_general(a, b, (((0,), (0,)), ((), ())), preferred_element_type=f32)


def standard(values):
    centred = values - jnp.mean(values, axis=-1, keepdims=True)
    inverse = lax.rsqrt(jnp.mean(centred * centred, axis=-1, keepdims=True) + epsilon)
    return centred * inverse, inverse


def standard_back(grad, unit, inverse):
    mean_grad = jnp.mean(grad, axis=-1, keepdims=True)
    mean_both = jnp.mean(grad * unit, axis=-1, keepdims=True)
    return (grad - mean_grad - unit * mean_both) * inverse


def geometry_kernel(shape_ref, mover_ref, side_ref, segment_ref, segment_row_ref):
    sides = shape_ref[0]
    height_slots = sides[0:1]
    width_slots = sides[1:2]
    sizes = jnp.broadcast_to(height_slots * width_slots, (8, 128))
    before = lax.broadcasted_iota(jnp.int32, (128, 128), 0)
    after = lax.broadcasted_iota(jnp.int32, (128, 128), 1)
    ends = mm(sizes.astype(bf16), (before <= after).astype(bf16))[0:1]
    starts = ends - height_slots * width_slots
    places = lax.broadcasted_iota(jnp.int32, (PACK, 128), 0).astype(f32)
    here = ((starts <= places) & (places < ends)).astype(f32)
    image_start = jnp.sum(here * starts, axis=1, keepdims=True)
    height = jnp.sum(here * height_slots, axis=1, keepdims=True)
    width = jnp.sum(here * width_slots, axis=1, keepdims=True)
    place = places[:, 0:1]
    offset = place - image_start
    safe = jnp.maximum(width, 1.0)
    grid_row = jnp.floor((offset + 0.5) / safe)
    grid_col = offset - grid_row * safe
    above = jnp.where(grid_row >= 1.0, place - width, -1.0)
    below = jnp.where(grid_row + 1.0 < height, place + width, -1.0)
    lanes = lax.broadcasted_iota(jnp.int32, (1, SPAN), 1).astype(f32)
    for part in range(3):
        base = lanes + WINDOWS[part]
        for which, (target, bounds) in enumerate(((above, UP_ROWS), (below, DOWN_ROWS))):
            low, high = bounds[part], bounds[part + 1]
            hit = (target[low:high] == base).astype(f32).astype(bf16)
            mover_ref[which * PACK + low : which * PACK + high] = hit
    side_ref[:, 0:128] = jnp.broadcast_to((grid_col >= 1.0).astype(f32), (PACK, 128))
    side_ref[:, 128:256] = jnp.broadcast_to((grid_col + 1.0 < width).astype(f32), (PACK, 128))
    segment = jnp.broadcast_to(image_start, (PACK, 128))
    segment_ref[...] = segment
    segment_row_ref[0] = segment.T[0:8]


def move(mover_ref, which, low):
    bounds = DOWN_ROWS if which else UP_ROWS
    parts = []
    for part in range(3):
        hit = mover_ref[which * PACK + bounds[part] : which * PACK + bounds[part + 1]]
        parts.append(mm(hit, low[WINDOWS[part] : WINDOWS[part] + SPAN]))
    return jnp.concatenate(parts, axis=0)


def before_row(values):
    return pltpu.roll(values, 1, 0)


def after_row(values):
    return pltpu.roll(values, values.shape[0] - 1, 0)


def conv_forward_kernel(count, final, *refs):
    refs = list(refs)
    token_ref, mover_ref, side_ref = refs[:3]
    weight_refs = refs[3 : 3 + count]
    rest = refs[3 + count :]
    if final:
        partial_ref, gain_conv_ref, gain_attn_ref = rest[:3]
        rest = rest[3:]
    expanded_refs = rest[:count]
    mixed_refs = rest[count : 2 * count]
    projected_ref = rest[2 * count]
    tokens = token_ref[...]
    width = tokens.shape[1]
    channels = weight_refs[0].shape[1]
    total = partial_ref[...] if final else None
    for weight_ref, expanded_ref, mixed_ref in zip(weight_refs, expanded_refs, mixed_refs):
        expanded = mm(tokens, weight_ref[0:width])
        expanded_ref[...] = expanded.astype(bf16)
        taps = weight_ref[width + channels : width + channels + 16].astype(f32)
        pieces = []
        for tile in range(channels // 128):
            lanes = slice(tile * 128, tile * 128 + 128)
            mid = expanded[:, lanes]
            left = before_row(mid) * side_ref[:, 0:128]
            right = after_row(mid) * side_ref[:, 128:256]
            lines = [
                left * taps[3 * a : 3 * a + 1, lanes]
                + mid * taps[3 * a + 1 : 3 * a + 2, lanes]
                + right * taps[3 * a + 2 : 3 * a + 3, lanes]
                for a in range(3)
            ]
            pieces.append(lines)
        line_up = jnp.concatenate([p[0].astype(bf16) for p in pieces], axis=1)
        line_mid = jnp.concatenate([p[1] for p in pieces], axis=1)
        line_down = jnp.concatenate([p[2].astype(bf16) for p in pieces], axis=1)
        mixed = move(mover_ref, 0, line_up) + move(mover_ref, 1, line_down) + line_mid
        mixed_ref[...] = mixed.astype(bf16)
        acted = (mixed * jax.nn.sigmoid(mixed)).astype(bf16)
        product = mm(acted, weight_ref[width : width + channels])
        total = product if total is None else total + product
    projected_ref[...] = total
    if final:
        residual_ref, attn_ref = rest[2 * count + 1 :]
        unit, _ = standard(total)
        residual = tokens.astype(f32) + unit * gain_conv_ref[...]
        residual_ref[...] = residual
        unit, _ = standard(residual)
        attn_ref[...] = (unit * gain_attn_ref[...]).astype(bf16)


def attention_forward_kernel(mask_ref, attn_ref, residual_ref, segment_ref, segment_row_ref, gain_ref, *refs):
    weight_refs = refs[:4]
    qkv_refs = refs[4:8]
    probs_ref, merged_ref, residual_two_ref, mlp_ref = refs[8:]
    attn = attn_ref[...]
    width = attn.shape[1]
    first = lax.broadcasted_iota(jnp.int32, (1, 128), 1) < HSZ
    total = residual_ref[...]
    row_segment = segment_row_ref[0, 0:1]
    for pair in range(4):
        projections = mm(attn, weight_refs[pair][0:width]).astype(bf16)
        qkv_refs[pair][...] = projections
        keys = projections[:, 128:256]
        values = projections[:, 256:384]
        merged_ref[:, pair * 128 : pair * 128 + 128] = jnp.zeros((PACK, 128), bf16)
        for side in range(2):
            head = 2 * pair + side
            lanes = first if side == 0 else ~first

            @pl.when(mask_ref[head] != 0)
            def _():
                queries = projections[:, 0:128] * jnp.where(lanes, HSZ**-0.5, 0.0).astype(bf16)
                for block in range(PACK // 128):
                    rows = slice(block * 128, block * 128 + 128)
                    scores = mm_t(queries[rows], keys)
                    same = segment_ref[rows, 0:1] == row_segment
                    scores = jnp.where(same, scores, -1e30)
                    weights = jnp.exp(scores - jnp.max(scores, axis=1, keepdims=True))
                    probs = weights * (1.0 / jnp.sum(weights, axis=1, keepdims=True))
                    probs = probs.astype(bf16)
                    probs_ref[0, head, rows] = probs
                    out = mm(probs, values).astype(bf16)
                    merged_ref[rows, pair * 128 : pair * 128 + 128] += jnp.where(lanes, out, 0).astype(bf16)

        total += mm(merged_ref[:, pair * 128 : pair * 128 + 128], weight_refs[pair][width : width + 128])
    residual_two_ref[...] = total
    unit, _ = standard(total)
    mlp_ref[...] = (unit * gain_ref[...]).astype(bf16)


def gelu_parts(values):
    size = jnp.abs(values)
    t = 1.0 / (1.0 + size * (0.3275911 * 0.7071067811865476))
    bell = jnp.exp(values * values * -0.5)
    poly = t * (
        0.5 * 0.254829592
        + t * (0.5 * -0.284496736 + t * (0.5 * 1.421413741 + t * (0.5 * -1.453152027 + t * (0.5 * 1.061405429))))
    )
    upper = poly * bell
    cdf = jnp.where(values >= 0, 1.0 - upper, upper)
    return values * cdf, cdf + values * bell * 0.3989422804014327


def mlp_kernel(mlp_ref, cotangent_ref, residual_ref, gain_ref, *refs):
    weight_refs = refs[:4]
    out_ref, grad_two_ref, gain_grad_ref = refs[4:7]
    grad_refs = refs[7:11]
    total_refs = refs[11:15]
    act_ref, pre_ref = refs[15:]
    step = pl.program_id(0)
    mlp = mlp_ref[...]
    cotangent = cotangent_ref[...]
    width = mlp.shape[1]
    mlp_t = mlp.T
    cotangent_t = cotangent.T
    out = residual_ref[...]
    grad_in = None
    for block in range(4):
        up = weight_refs[block][0:width]
        down = weight_refs[block][width:]
        for rows in range(0, PACK, 128):
            rows = slice(rows, rows + 128)
            pre = mm(mlp[rows], up)
            grad_hidden = mm_t(cotangent[rows], down)
            act, slope = gelu_parts(pre)
            act_ref[rows] = act.astype(bf16)
            pre_ref[rows] = (grad_hidden * slope).astype(bf16)
        act = act_ref[...]
        grad_pre = pre_ref[...]
        out = out + mm(act, down)
        product = mm_t(grad_pre, up)
        grad_in = product if grad_in is None else grad_in + product
        grad_up = mm(mlp_t, grad_pre)
        grad_down = mm(cotangent_t, act)

        @pl.when(step == 0)
        def _():
            total_refs[block][0:width] = grad_up
            total_refs[block][width:] = grad_down

        @pl.when(step != 0)
        def _():
            total_refs[block][0:width] += grad_up
            total_refs[block][width:] += grad_down

        @pl.when(step == pl.num_programs(0) - 1)
        def _():
            grad_refs[block][...] = total_refs[block][...].astype(bf16)

    out_ref[...] = out.astype(bf16)
    unit, inverse = standard(residual_ref[...])
    gain_part = jnp.sum((grad_in * unit).reshape(PACK // 8, 8, width), axis=0)

    @pl.when(step == 0)
    def _():
        gain_grad_ref[...] = gain_part

    @pl.when(step != 0)
    def _():
        gain_grad_ref[...] += gain_part

    grad_two_ref[...] = cotangent.astype(f32) + standard_back(grad_in * gain_ref[...], unit, inverse)


def attention_backward_kernel(
    mask_ref, grad_two_ref, attn_ref, residual_ref, projected_ref, merged_ref, probs_ref, gain_attn_ref, gain_conv_ref,
    *refs,
):
    weight_refs = refs[:4]
    qkv_refs = refs[4:8]
    grad_one_ref, grad_projected_ref, gain_attn_grad_ref, gain_conv_grad_ref = refs[8:12]
    grad_refs = refs[12:16]
    total_refs = refs[16:20]
    grad_proj_ref, sum_ref, scores_ref = refs[20:]
    step = pl.program_id(0)
    grad_two = grad_two_ref[...]
    low = grad_two.astype(bf16)
    width = low.shape[1]
    attn_t = attn_ref[...].T
    first = lax.broadcasted_iota(jnp.int32, (1, 128), 1) < HSZ
    grad_in = None
    for pair in range(4):
        out_weight = weight_refs[pair][width : width + 128]
        merged = merged_ref[:, pair * 128 : pair * 128 + 128]
        grad_out = t_mm(merged, low)
        grad_merged = mm_t(low, out_weight).astype(bf16)
        delta_all = grad_merged.astype(f32) * merged.astype(f32)
        sum_ref[...] = jnp.zeros_like(sum_ref)
        for side in range(2):
            head = 2 * pair + side
            lanes = first if side == 0 else ~first

            @pl.when(mask_ref[head] != 0)
            def _():
                queries = qkv_refs[pair][:, 0:128]
                keys = qkv_refs[pair][:, 128:256]
                values = qkv_refs[pair][:, 256:384]
                keep = lanes.astype(f32).astype(bf16)
                grad_heads = grad_merged * keep
                delta = jnp.sum(jnp.where(lanes, delta_all, 0.0), axis=1, keepdims=True)
                for block in range(PACK // 128):
                    rows = slice(block * 128, block * 128 + 128)
                    grad_probs = mm_t(grad_heads[rows], values)
                    scores_ref[rows] = (probs_ref[0, head, rows].astype(f32) * (grad_probs - delta[rows])).astype(bf16)
                grad_scores = scores_ref[...]
                sum_ref[:, 0:128] += mm(grad_scores, keys * keep)
                sum_ref[:, 128:256] += t_mm(grad_scores, queries * keep)
                sum_ref[:, 256:384] += t_mm(probs_ref[0, head], grad_heads)

        grad_proj_ref[:, 0:256] = (sum_ref[:, 0:256] * HSZ**-0.5).astype(bf16)
        grad_proj_ref[:, 256:384] = sum_ref[:, 256:384].astype(bf16)
        grad_proj = grad_proj_ref[...]
        grad_qkv = mm(attn_t, grad_proj)
        product = mm_t(grad_proj, weight_refs[pair][0:width])
        grad_in = product if grad_in is None else grad_in + product

        @pl.when(step == 0)
        def _():
            total_refs[pair][0:width] = grad_qkv
            total_refs[pair][width:] = grad_out

        @pl.when(step != 0)
        def _():
            total_refs[pair][0:width] += grad_qkv
            total_refs[pair][width:] += grad_out

        @pl.when(step == pl.num_programs(0) - 1)
        def _():
            grad_refs[pair][...] = total_refs[pair][...].astype(bf16)

    unit, inverse = standard(residual_ref[...])
    attn_part = jnp.sum((grad_in * unit).reshape(PACK // 8, 8, width), axis=0)
    grad_one = grad_two + standard_back(grad_in * gain_attn_ref[...], unit, inverse)
    grad_one_ref[...] = grad_one
    unit, inverse = standard(projected_ref[...])
    conv_part = jnp.sum((grad_one * unit).reshape(PACK // 8, 8, width), axis=0)
    grad_projected_ref[...] = standard_back(grad_one * gain_conv_ref[...], unit, inverse).astype(bf16)

    @pl.when(step == 0)
    def _():
        gain_attn_grad_ref[...] = attn_part
        gain_conv_grad_ref[...] = conv_part

    @pl.when(step != 0)
    def _():
        gain_attn_grad_ref[...] += attn_part
        gain_conv_grad_ref[...] += conv_part


def conv_backward_kernel(count, grad_projected_ref, token_ref, mover_ref, side_ref, partial_ref, *refs):
    weight_refs = refs[:count]
    expanded_refs = refs[count : 2 * count]
    mixed_refs = refs[2 * count : 3 * count]
    out_ref = refs[3 * count]
    grad_refs = refs[3 * count + 1 : 4 * count + 1]
    total_refs = refs[4 * count + 1 :]
    step = pl.program_id(0)
    grad_projected = grad_projected_ref[...]
    tokens = token_ref[...]
    width = tokens.shape[1]
    channels = weight_refs[0].shape[1]
    projected_t = grad_projected.T
    token_t = tokens.T
    total = partial_ref[...]
    for weight_ref, expanded_ref, mixed_ref, grad_ref, total_ref in zip(
        weight_refs, expanded_refs, mixed_refs, grad_refs, total_refs
    ):
        mixed = mixed_ref[...].astype(f32)
        gate = jax.nn.sigmoid(mixed)
        acted = (mixed * gate).astype(bf16)
        grad_project = mm(projected_t, acted)
        grad_acted = mm_t(grad_projected, weight_ref[width : width + channels])
        grad_mixed = grad_acted * (gate * (1.0 + mixed * (1.0 - gate)))
        grad_low = grad_mixed.astype(bf16)
        grad_up = move(mover_ref, 0, grad_low)
        grad_down = move(mover_ref, 1, grad_low)
        taps = weight_ref[width + channels : width + channels + 16].astype(f32)
        grads = []
        depth = []
        for tile in range(channels // 128):
            lanes = slice(tile * 128, tile * 128 + 128)
            rows = [grad_up[:, lanes], grad_mixed[:, lanes], grad_down[:, lanes]]
            mid = expanded_ref[:, lanes].astype(f32)
            left_mask = side_ref[:, 0:128]
            right_mask = side_ref[:, 128:256]
            left = before_row(mid) * left_mask
            right = after_row(mid) * right_mask
            sums = [
                jnp.sum(rows[2 - a] * part, axis=0, keepdims=True) for a in range(3) for part in (left, mid, right)
            ]
            depth.append(jnp.concatenate(sums + [jnp.zeros((7, 128), f32)], axis=0))
            cols = [
                sum(rows[a] * taps[8 - 3 * a - b : 9 - 3 * a - b, lanes] for a in range(3)) for b in range(3)
            ]
            grads.append(
                (cols[1] + before_row(cols[0]) * left_mask + after_row(cols[2]) * right_mask).astype(bf16)
            )
        grad_expanded = jnp.concatenate(grads, axis=1)
        grad_depth = jnp.concatenate(depth, axis=1)
        grad_expand = mm(token_t, grad_expanded)
        total = total + mm_t(grad_expanded, weight_ref[0:width])

        @pl.when(step == 0)
        def _():
            total_ref[0:width] = grad_expand
            total_ref[width : 2 * width] = grad_project
            total_ref[2 * width :] = grad_depth

        @pl.when(step != 0)
        def _():
            total_ref[0:width] += grad_expand
            total_ref[width : 2 * width] += grad_project
            total_ref[2 * width :] += grad_depth

        @pl.when(step == pl.num_programs(0) - 1)
        def _():
            grad_ref[...] = total_ref[...].astype(bf16)

    out_ref[...] = total.astype(out_ref.dtype)


def whole(shape):
    zeros = (0,) * len(shape)
    return pl.BlockSpec(shape, lambda p: zeros)


def packed(columns):
    return pl.BlockSpec((PACK, columns), lambda p: (p, 0))


def params(megabytes=48):
    return pltpu.CompilerParams(dimension_semantics=("arbitrary",), vmem_limit_bytes=megabytes << 20)


smem = pl.BlockSpec(memory_space=pltpu.SMEM)


def shaped(shape, dtype):
    return jax.ShapeDtypeStruct(shape, dtype)


def run_geometry(shapes):
    packs = shapes.shape[0]
    sides = jnp.pad(shapes.astype(f32), ((0, 0), (0, 6), (0, 128 - shapes.shape[2])))
    return pl.pallas_call(
        geometry_kernel,
        grid=(packs,),
        in_specs=[pl.BlockSpec((1, 8, 128), lambda p: (p, 0, 0))],
        out_specs=[
            pl.BlockSpec((2 * PACK, SPAN), lambda p: (p, 0)),
            packed(256),
            packed(128),
            pl.BlockSpec((1, 8, PACK), lambda p: (p, 0, 0)),
        ],
        out_shape=[
            shaped((packs * 2 * PACK, SPAN), bf16),
            shaped((packs * PACK, 256), f32),
            shaped((packs * PACK, 128), f32),
            shaped((packs, 8, PACK), f32),
        ],
        compiler_params=params(),
        name="geometry",
    )(sides)


def run_conv_forward(tokens, mover, side, weights, partial=None, gains=()):
    rows, width = tokens.shape
    channels = weights[0].shape[1]
    count = len(weights)
    final = partial is not None
    in_specs = [packed(width), pl.BlockSpec((2 * PACK, SPAN), lambda p: (p, 0)), packed(256)]
    in_specs += [whole(w.shape) for w in weights]
    args = [tokens, mover, side, *weights]
    if final:
        in_specs += [packed(width), whole((1, width)), whole((1, width))]
        args += [partial, *gains]
    outs = [(channels, bf16)] * (2 * count) + [(width, f32)]
    if final:
        outs += [(width, f32), (width, bf16)]
    result = pl.pallas_call(
        functools.partial(conv_forward_kernel, count, final),
        grid=(rows // PACK,),
        in_specs=in_specs,
        out_specs=[packed(c) for c, _ in outs],
        out_shape=[shaped((rows, c), d) for c, d in outs],
        compiler_params=params(),
        name="conv_forward",
    )(*args)
    return result[:count], result[count : 2 * count], result[2 * count :]


def run_attention_forward(mask, attn, residual, segment, segment_row, gain, weights):
    rows, width = attn.shape
    packs = rows // PACK
    heads = mask.shape[0]
    outs = [(384, bf16)] * 4
    result = pl.pallas_call(
        attention_forward_kernel,
        grid=(packs,),
        in_specs=[smem, packed(width), packed(width), packed(128), pl.BlockSpec((1, 8, PACK), lambda p: (p, 0, 0)),
                  whole((1, width))] + [whole(w.shape) for w in weights],
        out_specs=[packed(384)] * 4
        + [
            pl.BlockSpec((1, heads, PACK, PACK), lambda p: (p, 0, 0, 0)),
            packed(heads * HSZ), packed(width), packed(width),
        ],
        out_shape=[shaped((rows, 384), bf16)] * 4
        + [
            shaped((packs, heads, PACK, PACK), bf16),
            shaped((rows, heads * HSZ), bf16), shaped((rows, width), f32), shaped((rows, width), bf16),
        ],
        compiler_params=params(),
        name="attention_forward",
    )(mask, attn, residual, segment, segment_row, gain, *weights)
    return result[:4], result[4:]


def run_mlp(mlp, cotangent, residual, gain, weights):
    rows, width = mlp.shape
    channels = weights[0].shape[1]
    result = pl.pallas_call(
        mlp_kernel,
        grid=(rows // PACK,),
        in_specs=[packed(width)] * 3 + [whole((1, width))] + [whole(w.shape) for w in weights],
        out_specs=[packed(width)] * 2 + [whole((8, width))] + [whole((2 * width, channels))] * 4,
        out_shape=[shaped((rows, width), bf16), shaped((rows, width), f32), shaped((8, width), f32)]
        + [shaped((2 * width, channels), bf16)] * 4,
        scratch_shapes=[pltpu.VMEM((2 * width, channels), f32)] * 4 + [pltpu.VMEM((PACK, channels), bf16)] * 2,
        compiler_params=params(),
        name="mlp_both",
    )(mlp, cotangent, residual, gain, *weights)
    return result[:3], result[3:]


def run_attention_backward(
    mask, grad_two, attn, residual, projected, merged, probs, gain_attn, gain_conv, weights, qkv
):
    rows, width = attn.shape
    packs = rows // PACK
    heads = mask.shape[0]
    result = pl.pallas_call(
        attention_backward_kernel,
        grid=(packs,),
        in_specs=[smem]
        + [packed(width)] * 4
        + [packed(heads * HSZ), pl.BlockSpec((1, heads, PACK, PACK), lambda p: (p, 0, 0, 0))]
        + [whole((1, width))] * 2
        + [whole(w.shape) for w in weights]
        + [packed(384)] * 4,
        out_specs=[packed(width)] * 2 + [whole((8, width))] * 2 + [whole((width + 128, 384))] * 4,
        out_shape=[shaped((rows, width), f32), shaped((rows, width), bf16)]
        + [shaped((8, width), f32)] * 2
        + [shaped((width + 128, 384), bf16)] * 4,
        scratch_shapes=[pltpu.VMEM((width + 128, 384), f32)] * 4
        + [pltpu.VMEM((PACK, 384), bf16), pltpu.VMEM((PACK, 384), f32), pltpu.VMEM((PACK, PACK), bf16)],
        compiler_params=params(),
        name="attention_backward",
    )(mask, grad_two, attn, residual, projected, merged, probs, gain_attn, gain_conv, *weights, *qkv)
    return result[:4], result[4:]


def run_conv_backward(grad_projected, tokens, mover, side, partial, weights, expanded, mixed, out_dtype):
    rows, width = tokens.shape
    channels = weights[0].shape[1]
    count = len(weights)
    grad_shape = (2 * width + 16, channels)
    result = pl.pallas_call(
        functools.partial(conv_backward_kernel, count),
        grid=(rows // PACK,),
        in_specs=[packed(width)] * 2
        + [pl.BlockSpec((2 * PACK, SPAN), lambda p: (p, 0)), packed(256), packed(width)]
        + [whole(w.shape) for w in weights]
        + [packed(channels)] * (2 * count),
        out_specs=[packed(width)] + [whole(grad_shape)] * count,
        out_shape=[shaped((rows, width), out_dtype)] + [shaped(grad_shape, bf16)] * count,
        scratch_shapes=[pltpu.VMEM(grad_shape, f32)] * count,
        compiler_params=params(),
        name="conv_backward",
    )(grad_projected, tokens, mover, side, partial, *weights, *expanded, *mixed)
    return result[0], result[1:]


def per_device(
    tokens, cotangent, shapes, head_mask, w_expand, w_depth, w_project, gain_conv, gain_attn, w_qkv, w_out,
    gain_mlp, w_up, w_down,
):
    rows, width = tokens.shape
    packs = rows // PACK
    channels = w_expand.shape[1]
    tensor_size = lax.axis_size("tensor")
    dp_size = lax.axis_size("dp")
    me_tensor = lax.axis_index("tensor")
    me_dp = lax.axis_index("dp")
    dp_bits = [1 << b for b in range(dp_size.bit_length() - 1)]

    def swap_tensor(x, bit):
        return lax.ppermute(x, "tensor", [(i, i ^ bit) for i in range(tensor_size)])

    def swap_dp(x, bit):
        return lax.ppermute(x, "dp", [(i, i ^ bit) for i in range(dp_size)])

    def gather(x):
        far = swap_tensor(x, 2)
        return [x, swap_tensor(x, 1), far, swap_tensor(far, 1)]

    def add(a, b):
        return (a.astype(f32) + b.astype(f32)).astype(a.dtype)

    def reduce_blocks(blocks):
        near = add(blocks[0], swap_tensor(blocks[1], 1))
        far = add(blocks[2], swap_tensor(blocks[3], 1))
        x = add(near, swap_tensor(far, 2))
        halved = []
        for bit in dp_bits:
            if x.shape[0] % 2:
                x = add(x, swap_dp(x, bit))
                continue
            halved.append(bit)
            mine = ((me_dp & bit) != 0).astype(jnp.int32)
            half = x.shape[0] // 2
            send = lax.dynamic_slice_in_dim(x, (1 - mine) * half, half, 0)
            keep = lax.dynamic_slice_in_dim(x, mine * half, half, 0)
            x = add(keep, swap_dp(send, bit))
        for bit in reversed(halved):
            other = swap_dp(x, bit)
            mine = (me_dp & bit) != 0
            x = jnp.concatenate([jnp.where(mine, other, x), jnp.where(mine, x, other)])
        return x

    own_shapes = lax.dynamic_slice_in_dim(shapes, me_tensor * packs, packs, 0)
    mask_row = jnp.pad(head_mask.astype(bf16), (0, channels - head_mask.shape[0]))[None, :]
    conv_w = gather(
        jnp.concatenate([w_expand, w_project, w_depth, mask_row, jnp.zeros((6, channels), bf16)])
    )
    attn_w = gather(jnp.concatenate([w_qkv.reshape(width, -1), w_out]))
    mlp_w = gather(jnp.concatenate([w_up, w_down]))
    mask = jnp.concatenate([w[width + channels + 9, : head_mask.shape[0]] for w in conv_w]).astype(jnp.int32)

    gain_conv, gain_attn, gain_mlp = (g[None, :] for g in (gain_conv, gain_attn, gain_mlp))
    mover, side, segment, segment_row = run_geometry(own_shapes)
    exp_a, mix_a, (partial,) = run_conv_forward(tokens, mover, side, conv_w[:2])
    exp_b, mix_b, (projected, residual_one, attn_low) = run_conv_forward(
        tokens, mover, side, conv_w[2:], partial, (gain_conv, gain_attn)
    )
    qkv, (probs, merged, residual_two, mlp_low) = run_attention_forward(
        mask, attn_low, residual_one, segment, segment_row, gain_mlp, attn_w
    )
    (out_tokens, grad_two, gain_m), mlp_g = run_mlp(mlp_low, cotangent, residual_two, gain_mlp, mlp_w)
    mlp_sum = reduce_blocks(mlp_g)
    (grad_one, grad_projected, gain_a, gain_c), attn_g = run_attention_backward(
        mask, grad_two, attn_low, residual_one, projected, merged, probs, gain_attn, gain_conv, attn_w, qkv
    )
    attn_sum = reduce_blocks(attn_g)
    partial, conv_g1 = run_conv_backward(
        grad_projected, tokens, mover, side, grad_one, [conv_w[1], conv_w[3]], [exp_a[1], exp_b[1]],
        [mix_a[1], mix_b[1]], f32,
    )
    grad_tokens, conv_g2 = run_conv_backward(
        grad_projected, tokens, mover, side, partial, [conv_w[0], conv_w[2]], [exp_a[0], exp_b[0]],
        [mix_a[0], mix_b[0]], bf16,
    )
    gains = jnp.sum(jnp.stack([gain_c, gain_a, gain_m]), axis=1)
    for bit in (1, 2):
        gains = gains + swap_tensor(gains, bit)
    for bit in dp_bits:
        gains = gains + swap_dp(gains, bit)
    conv_sum = reduce_blocks([conv_g2[0], conv_g1[0], conv_g2[1], conv_g1[1]])

    mlp_sum, attn_sum, conv_sum = (s.astype(f32) for s in (mlp_sum, attn_sum, conv_sum))
    return (
        out_tokens,
        grad_tokens,
        conv_sum[:width],
        conv_sum[2 * width : 2 * width + 9],
        conv_sum[width : 2 * width].T,
        gains[0],
        gains[1],
        attn_sum[:width].reshape(w_qkv.shape),
        attn_sum[width:],
        gains[2],
        mlp_sum[:width],
        mlp_sum[width:].T,
    )


def solution(mesh):
    rows = P(("dp", "tensor"), None)
    cols = P(None, "tensor")
    down = P("tensor", None)
    return jax.shard_map(
        per_device,
        mesh=mesh,
        in_specs=(
            rows, rows, P("dp", None, None), P("tensor"), cols, cols, down, P(), P(), P(None, None, "tensor"), down,
            P(), cols, down,
        ),
        out_specs=(rows, rows, cols, cols, down, P(), P(), P(None, None, "tensor"), down, P(), cols, down),
        check_vma=False,
    )
```

```python
import functools
import jax
import jax.numpy as jnp
from jax import lax
from jax.experimental import pallas as pl
from jax.experimental.pallas import tpu as pltpu
from jax.sharding import PartitionSpec as P

HSZ = 64
PACK = 512
WINDOWS = (0, 240, 256)
SPAN = 256
UP_ROWS = (0, 256, 496, 512)
DOWN_ROWS = (0, 240, 480, 512)

epsilon = 1e-05
f32 = jnp.float32
bf16 = jnp.bfloat16


def mm(a, b):
    return jnp.dot(a, b, preferred_element_type=f32)


def mm_t(a, b):
    return lax.dot_general(a, b, (((1,), (1,)), ((), ())), preferred_element_type=f32)


def t_mm(a, b):
    return lax.dot_general(a, b, (((0,), (0,)), ((), ())), preferred_element_type=f32)


def standard(values):
    centred = values - jnp.mean(values, axis=-1, keepdims=True)
    inverse = lax.rsqrt(jnp.mean(centred * centred, axis=-1, keepdims=True) + epsilon)
    return centred * inverse, inverse


def standard_back(grad, unit, inverse):
    mean_grad = jnp.mean(grad, axis=-1, keepdims=True)
    mean_both = jnp.mean(grad * unit, axis=-1, keepdims=True)
    return (grad - mean_grad - unit * mean_both) * inverse


def geometry_kernel(shape_ref, mover_ref, side_ref, segment_ref, segment_row_ref, slot_ref):
    own = lax.axis_index("tensor") * pl.num_programs(0) + pl.program_id(0)
    slot_ref[...] = jnp.zeros_like(slot_ref)
    slot_ref[0:2, 0 : shape_ref.shape[2]] = shape_ref[own].astype(f32)
    sides = slot_ref[...]
    height_slots = sides[0:1]
    width_slots = sides[1:2]
    sizes = jnp.broadcast_to(height_slots * width_slots, (8, 128))
    before = lax.broadcasted_iota(jnp.int32, (128, 128), 0)
    after = lax.broadcasted_iota(jnp.int32, (128, 128), 1)
    ends = mm(sizes.astype(bf16), (before <= after).astype(bf16))[0:1]
    starts = ends - height_slots * width_slots
    places = lax.broadcasted_iota(jnp.int32, (PACK, 128), 0).astype(f32)
    here = ((starts <= places) & (places < ends)).astype(f32)
    image_start = jnp.sum(here * starts, axis=1, keepdims=True)
    height = jnp.sum(here * height_slots, axis=1, keepdims=True)
    width = jnp.sum(here * width_slots, axis=1, keepdims=True)
    place = places[:, 0:1]
    offset = place - image_start
    safe = jnp.maximum(width, 1.0)
    grid_row = jnp.floor((offset + 0.5) / safe)
    grid_col = offset - grid_row * safe
    above = jnp.where(grid_row >= 1.0, place - width, -1.0)
    below = jnp.where(grid_row + 1.0 < height, place + width, -1.0)
    lanes = lax.broadcasted_iota(jnp.int32, (1, SPAN), 1).astype(f32)
    for part in range(3):
        base = lanes + WINDOWS[part]
        for which, (target, bounds) in enumerate(((above, UP_ROWS), (below, DOWN_ROWS))):
            low, high = bounds[part], bounds[part + 1]
            hit = (target[low:high] == base).astype(f32).astype(bf16)
            mover_ref[which * PACK + low : which * PACK + high] = hit
    side_ref[:, 0:128] = jnp.broadcast_to((grid_col >= 1.0).astype(f32), (PACK, 128))
    side_ref[:, 128:256] = jnp.broadcast_to((grid_col + 1.0 < width).astype(f32), (PACK, 128))
    segment = jnp.broadcast_to(image_start, (PACK, 128))
    segment_ref[...] = segment
    segment_row_ref[0] = segment.T[0:8]


def move(mover_ref, which, low):
    bounds = DOWN_ROWS if which else UP_ROWS
    parts = []
    for part in range(3):
        hit = mover_ref[which * PACK + bounds[part] : which * PACK + bounds[part + 1]]
        parts.append(mm(hit, low[WINDOWS[part] : WINDOWS[part] + SPAN]))
    return jnp.concatenate(parts, axis=0)


def before_row(values):
    return pltpu.roll(values, 1, 0)


def after_row(values):
    return pltpu.roll(values, values.shape[0] - 1, 0)


def conv_forward_kernel(count, has_partial, final, unused, *refs):
    refs = list(refs)
    token_ref, mover_ref, side_ref = refs[:3]
    weight_refs = refs[3 : 3 + count]
    other_refs = refs[3 + count : 3 + 2 * count]
    rest = refs[3 + 2 * count :]
    if has_partial:
        partial_ref, rest = rest[0], rest[1:]
    if final:
        gain_conv_ref, gain_attn_ref = rest[:2]
        rest = rest[2:]
    rest = rest[unused:]
    expanded_refs = rest[:count]
    mixed_refs = rest[count : 2 * count]
    projected_ref = rest[2 * count]
    tokens = token_ref[...]
    width = tokens.shape[1]
    channels = weight_refs[0].shape[1]
    total = partial_ref[...] if has_partial else None
    for weight_ref, other_ref, expanded_ref, mixed_ref in zip(weight_refs, other_refs, expanded_refs, mixed_refs):
        expanded = mm(tokens, weight_ref[...])
        expanded_ref[...] = expanded.astype(bf16)
        taps = other_ref[channels : channels + 16].astype(f32)
        pieces = []
        for tile in range(channels // 128):
            lanes = slice(tile * 128, tile * 128 + 128)
            mid = expanded[:, lanes]
            left = before_row(mid) * side_ref[:, 0:128]
            right = after_row(mid) * side_ref[:, 128:256]
            lines = [
                left * taps[3 * a : 3 * a + 1, lanes]
                + mid * taps[3 * a + 1 : 3 * a + 2, lanes]
                + right * taps[3 * a + 2 : 3 * a + 3, lanes]
                for a in range(3)
            ]
            pieces.append(lines)
        line_up = jnp.concatenate([p[0].astype(bf16) for p in pieces], axis=1)
        line_mid = jnp.concatenate([p[1] for p in pieces], axis=1)
        line_down = jnp.concatenate([p[2].astype(bf16) for p in pieces], axis=1)
        mixed = move(mover_ref, 0, line_up) + move(mover_ref, 1, line_down) + line_mid
        mixed_ref[...] = mixed.astype(bf16)
        acted = (mixed * jax.nn.sigmoid(mixed)).astype(bf16)
        product = mm(acted, other_ref[0:channels])
        total = product if total is None else total + product
    projected_ref[...] = total
    if final:
        residual_ref, attn_ref = rest[2 * count + 1 :]
        unit, _ = standard(total)
        residual = tokens.astype(f32) + unit * gain_conv_ref[...]
        residual_ref[...] = residual
        unit, _ = standard(residual)
        attn_ref[...] = (unit * gain_attn_ref[...]).astype(bf16)


def flag(flag_ref, side):
    return jnp.max(flag_ref[9:10, side : side + 1].astype(f32)) != 0


def lane_joined(weight_ref):
    rows = weight_ref.shape[0] // 3
    return jnp.concatenate([weight_ref[j * rows : (j + 1) * rows] for j in range(3)], axis=1)


def attention_forward_kernel(attn_ref, residual_ref, segment_ref, segment_row_ref, gain_ref, *refs):
    weight_refs = refs[:4]
    out_weight_refs = refs[4:8]
    flag_refs = refs[8:12]
    qkv_refs = refs[12:16]
    probs_ref, merged_ref, residual_two_ref, mlp_ref = refs[16:]
    attn = attn_ref[...]
    width = attn.shape[1]
    first = lax.broadcasted_iota(jnp.int32, (1, 128), 1) < HSZ
    total = residual_ref[...]
    row_segment = segment_row_ref[0, 0:1]
    for pair in range(4):
        projections = mm(attn, lane_joined(weight_refs[pair])).astype(bf16)
        qkv_refs[pair][...] = projections
        keys = projections[:, 128:256]
        values = projections[:, 256:384]
        merged_ref[:, pair * 128 : pair * 128 + 128] = jnp.zeros((PACK, 128), bf16)
        for side in range(2):
            head = 2 * pair + side
            lanes = first if side == 0 else ~first

            @pl.when(flag(flag_refs[pair], side))
            def _():
                queries = projections[:, 0:128] * jnp.where(lanes, HSZ**-0.5, 0.0).astype(bf16)
                for block in range(PACK // 128):
                    rows = slice(block * 128, block * 128 + 128)
                    scores = mm_t(queries[rows], keys)
                    same = segment_ref[rows, 0:1] == row_segment
                    scores = jnp.where(same, scores, -1e30)
                    weights = jnp.exp(scores - jnp.max(scores, axis=1, keepdims=True))
                    probs = weights * (1.0 / jnp.sum(weights, axis=1, keepdims=True))
                    probs = probs.astype(bf16)
                    probs_ref[0, head, rows] = probs
                    out = mm(probs, values).astype(bf16)
                    merged_ref[rows, pair * 128 : pair * 128 + 128] += jnp.where(lanes, out, 0).astype(bf16)

        total += mm(merged_ref[:, pair * 128 : pair * 128 + 128], out_weight_refs[pair][...])
    residual_two_ref[...] = total
    unit, _ = standard(total)
    mlp_ref[...] = (unit * gain_ref[...]).astype(bf16)


def store_block(keep_ref, mate_ref, block, values):
    rows = values.shape[0]
    start = (block // 2) * rows
    target = mate_ref if block % 2 else keep_ref
    target[start : start + rows] = values.astype(bf16)


def gelu_parts(values):
    size = jnp.abs(values)
    t = 1.0 / (1.0 + size * (0.3275911 * 0.7071067811865476))
    bell = jnp.exp(values * values * -0.5)
    poly = t * (
        0.5 * 0.254829592
        + t * (0.5 * -0.284496736 + t * (0.5 * 1.421413741 + t * (0.5 * -1.453152027 + t * (0.5 * 1.061405429))))
    )
    upper = poly * bell
    cdf = jnp.where(values >= 0, 1.0 - upper, upper)
    return values * cdf, cdf + values * bell * 0.3989422804014327


def mlp_kernel(mlp_ref, cotangent_ref, residual_ref, gain_ref, *refs):
    weight_refs = refs[:4]
    out_ref, grad_two_ref, gain_grad_ref, keep_ref, mate_ref = refs[4:9]
    total_refs = refs[9:13]
    act_ref, pre_ref = refs[13:]
    step = pl.program_id(0)
    mlp = mlp_ref[...]
    cotangent = cotangent_ref[...]
    width = mlp.shape[1]
    mlp_t = mlp.T
    cotangent_t = cotangent.T
    out = residual_ref[...]
    grad_in = None
    for block in range(4):
        up = weight_refs[block][0:width]
        down = weight_refs[block][width:]
        for rows in range(0, PACK, 128):
            rows = slice(rows, rows + 128)
            pre = mm(mlp[rows], up)
            grad_hidden = mm_t(cotangent[rows], down)
            act, slope = gelu_parts(pre)
            act_ref[rows] = act.astype(bf16)
            pre_ref[rows] = (grad_hidden * slope).astype(bf16)
        act = act_ref[...]
        grad_pre = pre_ref[...]
        out = out + mm(act, down)
        product = mm_t(grad_pre, up)
        grad_in = product if grad_in is None else grad_in + product
        grad_up = mm(mlp_t, grad_pre)
        grad_down = mm(cotangent_t, act)

        @pl.when(step == 0)
        def _():
            total_refs[block][0:width] = grad_up
            total_refs[block][width:] = grad_down

        @pl.when(step != 0)
        def _():
            total_refs[block][0:width] += grad_up
            total_refs[block][width:] += grad_down

        @pl.when(step == pl.num_programs(0) - 1)
        def _():
            store_block(keep_ref, mate_ref, block, total_refs[block][...])

    out_ref[...] = out.astype(bf16)
    unit, inverse = standard(residual_ref[...])
    gain_part = jnp.sum((grad_in * unit).reshape(PACK // 8, 8, width), axis=0)

    @pl.when(step == 0)
    def _():
        gain_grad_ref[...] = gain_part

    @pl.when(step != 0)
    def _():
        gain_grad_ref[...] += gain_part

    grad_two_ref[...] = cotangent.astype(f32) + standard_back(grad_in * gain_ref[...], unit, inverse)


def attention_backward_kernel(sides, final, grad_two_ref, attn_ref, merged_ref, probs_ref, *refs):
    count = len(sides)
    refs = list(refs)

    def take(n):
        taken = refs[:n]
        del refs[:n]
        return taken

    weight_refs = take(count)
    out_weight_refs = take(count)
    flag_refs = take(count)
    qkv_refs = take(count)
    if final:
        partial_ref, residual_ref, projected_ref, gain_attn_ref, gain_conv_ref = take(5)
        mixed_refs = take(4)
        del refs[: len(refs) - (6 + count + count + 4 + 3)]
        grad_one_ref, grad_projected_ref, gain_attn_grad_ref, gain_conv_grad_ref, keep_ref, mate_ref = take(6)
    else:
        del refs[: len(refs) - (1 + count + count + 3)]
        (grad_in_ref,) = take(1)
    grad_refs = take(count)
    total_refs = take(count)
    if final:
        project_refs = take(4)
    grad_proj_ref, sum_ref, scores_ref = refs
    step = pl.program_id(0)
    steps = pl.num_programs(0)
    grad_two = grad_two_ref[...]
    low = grad_two.astype(bf16)
    width = low.shape[1]
    attn_t = attn_ref[...].T
    first = lax.broadcasted_iota(jnp.int32, (1, 128), 1) < HSZ
    grad_in = partial_ref[...] if final else None
    for place, pair in enumerate(sides):
        out_weight = out_weight_refs[place][...]
        merged = merged_ref[:, pair * 128 : pair * 128 + 128]
        grad_out = t_mm(merged, low)
        grad_merged = mm_t(low, out_weight).astype(bf16)
        delta_all = grad_merged.astype(f32) * merged.astype(f32)
        sum_ref[...] = jnp.zeros_like(sum_ref)
        for side in range(2):
            head = 2 * pair + side
            lanes = first if side == 0 else ~first

            @pl.when(flag(flag_refs[place], side))
            def _():
                queries = qkv_refs[place][:, 0:128]
                keys = qkv_refs[place][:, 128:256]
                values = qkv_refs[place][:, 256:384]
                keep = lanes.astype(f32).astype(bf16)
                grad_heads = grad_merged * keep
                delta = jnp.sum(jnp.where(lanes, delta_all, 0.0), axis=1, keepdims=True)
                for block in range(PACK // 128):
                    rows = slice(block * 128, block * 128 + 128)
                    grad_probs = mm_t(grad_heads[rows], values)
                    scores_ref[rows] = (probs_ref[0, head, rows].astype(f32) * (grad_probs - delta[rows])).astype(bf16)
                grad_scores = scores_ref[...]
                sum_ref[:, 0:128] += mm(grad_scores, keys * keep)
                sum_ref[:, 128:256] += t_mm(grad_scores, queries * keep)
                sum_ref[:, 256:384] += t_mm(probs_ref[0, head], grad_heads)

        grad_proj_ref[:, 0:256] = (sum_ref[:, 0:256] * HSZ**-0.5).astype(bf16)
        grad_proj_ref[:, 256:384] = sum_ref[:, 256:384].astype(bf16)
        grad_proj = grad_proj_ref[...]
        grad_qkv = mm(attn_t, grad_proj)
        product = mm_t(grad_proj, lane_joined(weight_refs[place]))
        grad_in = product if grad_in is None else grad_in + product

        @pl.when(step == 0)
        def _():
            total_refs[place][0:width] = grad_qkv
            total_refs[place][width:] = grad_out

        @pl.when(step != 0)
        def _():
            total_refs[place][0:width] += grad_qkv
            total_refs[place][width:] += grad_out

        @pl.when(step == steps - 1)
        def _():
            grad_refs[place][...] = total_refs[place][...].astype(bf16)

    if not final:
        grad_in_ref[...] = grad_in
        return
    unit, inverse = standard(residual_ref[...])
    attn_part = jnp.sum((grad_in * unit).reshape(PACK // 8, 8, width), axis=0)
    grad_one = grad_two + standard_back(grad_in * gain_attn_ref[...], unit, inverse)
    grad_one_ref[...] = grad_one
    unit, inverse = standard(projected_ref[...])
    conv_part = jnp.sum((grad_one * unit).reshape(PACK // 8, 8, width), axis=0)
    grad_projected = standard_back(grad_one * gain_conv_ref[...], unit, inverse).astype(bf16)
    grad_projected_ref[...] = grad_projected
    projected_t = grad_projected.T
    for block in range(4):
        mixed = mixed_refs[block][...].astype(f32)
        acted = (mixed * jax.nn.sigmoid(mixed)).astype(bf16)
        grad_project = mm(projected_t, acted)

        @pl.when(step == 0)
        def _():
            project_refs[block][...] = grad_project

        @pl.when(step != 0)
        def _():
            project_refs[block][...] += grad_project

        @pl.when(step == steps - 1)
        def _():
            store_block(keep_ref, mate_ref, block, project_refs[block][...])

    @pl.when(step == 0)
    def _():
        gain_attn_grad_ref[...] = attn_part
        gain_conv_grad_ref[...] = conv_part

    @pl.when(step != 0)
    def _():
        gain_attn_grad_ref[...] += attn_part
        gain_conv_grad_ref[...] += conv_part


def small_rows(gain_refs, width):
    gains = jnp.concatenate([jnp.sum(ref[...], axis=0, keepdims=True) for ref in gain_refs], axis=0)
    high = gains.astype(bf16).astype(f32)
    return high, gains - high


def conv_backward_kernel(
    grad_projected_ref, token_ref, mover_ref, side_ref, gain_c_ref, gain_a_ref, gain_m_ref, other_ref, expanded_ref,
    mixed_ref, *refs
):
    grad_expanded_ref, grad_ref, total_ref = refs[-3:]
    step = pl.program_id(0)
    grad_projected = grad_projected_ref[...]
    tokens = token_ref[...]
    width = tokens.shape[1]
    channels = other_ref.shape[1]
    token_t = tokens.T
    mixed = mixed_ref[...].astype(f32)
    gate = jax.nn.sigmoid(mixed)
    grad_acted = mm_t(grad_projected, other_ref[0:channels])
    grad_mixed = grad_acted * (gate * (1.0 + mixed * (1.0 - gate)))
    grad_low = grad_mixed.astype(bf16)
    grad_up = move(mover_ref, 0, grad_low)
    grad_down = move(mover_ref, 1, grad_low)
    taps = other_ref[channels : channels + 16].astype(f32)
    depth = []
    for tile in range(channels // 128):
        lanes = slice(tile * 128, tile * 128 + 128)
        rows = [grad_up[:, lanes], grad_mixed[:, lanes], grad_down[:, lanes]]
        mid = expanded_ref[:, lanes].astype(f32)
        left_mask = side_ref[:, 0:128]
        right_mask = side_ref[:, 128:256]
        left = before_row(mid) * left_mask
        right = after_row(mid) * right_mask
        sums = [jnp.sum(rows[2 - a] * part, axis=0, keepdims=True) for a in range(3) for part in (left, mid, right)]
        depth.append(jnp.concatenate(sums + [jnp.zeros((7, 128), f32)], axis=0))
        cols = [sum(rows[a] * taps[8 - 3 * a - b : 9 - 3 * a - b, lanes] for a in range(3)) for b in range(3)]
        grad_expanded_ref[:, lanes] = (
            cols[1] + before_row(cols[0]) * left_mask + after_row(cols[2]) * right_mask
        ).astype(bf16)
    grad_depth = jnp.concatenate(depth, axis=1)
    grad_expand = mm(token_t, grad_expanded_ref[...])

    @pl.when(step == 0)
    def _():
        high, rest = small_rows((gain_c_ref, gain_a_ref, gain_m_ref), width)
        total_ref[0:width] = grad_expand
        total_ref[width:] = grad_depth + jnp.concatenate(
            [jnp.zeros((9, width), f32), high, rest, jnp.zeros((1, width), f32)], axis=0
        )

    @pl.when(step != 0)
    def _():
        total_ref[0:width] += grad_expand
        total_ref[width:] += grad_depth

    @pl.when(step == pl.num_programs(0) - 1)
    def _():
        grad_ref[...] = total_ref[...].astype(bf16)


def token_grad_kernel(grad_one_ref, *refs):
    total = grad_one_ref[...]
    for grad_ref, weight_ref in zip(refs[:4], refs[4:8]):
        total = total + mm_t(grad_ref[...], weight_ref[...])
    refs[-1][...] = total.astype(bf16)


def join_kernel(turns, index_ref, mine_ref, other_ref, *refs):
    out_refs = refs[:-1]
    whole_ref = refs[-1]
    first = index_ref[0] == 0
    rows = mine_ref.shape[0]
    mine = mine_ref[...].astype(f32)
    other = other_ref[...].astype(f32)
    whole_ref[0:rows] = jnp.where(first, mine, other)
    whole_ref[rows:] = jnp.where(first, other, mine)
    start = 0
    for out_ref, turn in zip(out_refs, turns):
        if turn == "slabs":
            rows = out_ref.shape[1]
            for j in range(out_ref.shape[0]):
                out_ref[j] = whole_ref[start : start + rows, j * 128 : j * 128 + 128]
        elif turn == "turned":
            rows = out_ref.shape[1]
            out_ref[...] = whole_ref[start : start + rows].T
        else:
            rows = out_ref.shape[0]
            out_ref[...] = whole_ref[start : start + rows]
        start += rows


def whole(shape):
    zeros = (0,) * len(shape)
    return pl.BlockSpec(shape, lambda p: zeros)


def packed(columns):
    return pl.BlockSpec((PACK, columns), lambda p: (p, 0))


def params(megabytes=56):
    return pltpu.CompilerParams(vmem_limit_bytes=megabytes << 20)


def cost(microseconds):
    return pl.CostEstimate(
        flops=int(microseconds * 1.1e9), bytes_accessed=int(microseconds * 3.0e6), transcendentals=0
    )


smem = pl.BlockSpec(memory_space=pltpu.SMEM)


def shaped(shape, dtype):
    return jax.ShapeDtypeStruct(shape, dtype)


def run_geometry(shapes, packs):
    return pl.pallas_call(
        geometry_kernel,
        grid=(packs,),
        in_specs=[whole(shapes.shape)],
        out_specs=[
            pl.BlockSpec((2 * PACK, SPAN), lambda p: (p, 0)),
            packed(256),
            packed(128),
            pl.BlockSpec((1, 8, PACK), lambda p: (p, 0, 0)),
        ],
        out_shape=[
            shaped((packs * 2 * PACK, SPAN), bf16),
            shaped((packs * PACK, 256), f32),
            shaped((packs * PACK, 128), f32),
            shaped((packs, 8, PACK), f32),
        ],
        scratch_shapes=[pltpu.VMEM((8, 128), f32)],
        compiler_params=params(),
        cost_estimate=cost(3),
        name="geometry",
    )(shapes)


def run_conv_forward(tokens, mover, side, weights, others, partial=None, gains=(), after=()):
    rows, width = tokens.shape
    channels = weights[0].shape[1]
    count = len(weights)
    final = len(gains) > 0
    has_partial = partial is not None
    in_specs = [packed(width), pl.BlockSpec((2 * PACK, SPAN), lambda p: (p, 0)), packed(256)]
    in_specs += [whole(w.shape) for w in weights] + [whole(w.shape) for w in others]
    args = [tokens, mover, side, *weights, *others]
    if has_partial:
        in_specs += [packed(width)]
        args += [partial]
    if final:
        in_specs += [whole((width,)), whole((width,))]
        args += [*gains]
    in_specs += [anywhere] * len(after)
    args += [*after]
    outs = [(channels, bf16)] * (2 * count) + [(width, f32)]
    if final:
        outs += [(width, f32), (width, bf16)]
    result = pl.pallas_call(
        functools.partial(conv_forward_kernel, count, has_partial, final, len(after)),
        grid=(rows // PACK,),
        in_specs=in_specs,
        out_specs=[packed(c) for c, _ in outs],
        out_shape=[shaped((rows, c), d) for c, d in outs],
        compiler_params=params(),
        cost_estimate=cost(4 * count),
        name="conv_forward",
    )(*args)
    return result[:count], result[count : 2 * count], result[2 * count :]


def flag_spec(other):
    place = other.shape[0] // 16 - 1
    return pl.BlockSpec((16, other.shape[1]), lambda p: (place, 0))


def run_attention_forward(attn, residual, segment, segment_row, gain, weights, out_weights, others):
    rows, width = attn.shape
    packs = rows // PACK
    heads = 8
    result = pl.pallas_call(
        attention_forward_kernel,
        grid=(packs,),
        in_specs=[packed(width), packed(width), packed(128), pl.BlockSpec((1, 8, PACK), lambda p: (p, 0, 0)),
                  whole((width,))]
        + [whole(w.shape) for w in (*weights, *out_weights)]
        + [flag_spec(w) for w in others],
        out_specs=[packed(384)] * 4
        + [
            pl.BlockSpec((1, heads, PACK, PACK), lambda p: (p, 0, 0, 0)),
            packed(heads * HSZ), packed(width), packed(width),
        ],
        out_shape=[shaped((rows, 384), bf16)] * 4
        + [
            shaped((packs, heads, PACK, PACK), bf16),
            shaped((rows, heads * HSZ), bf16), shaped((rows, width), f32), shaped((rows, width), bf16),
        ],
        compiler_params=params(),
        cost_estimate=cost(28),
        name="attention_forward",
    )(attn, residual, segment, segment_row, gain, *weights, *out_weights, *others)
    return result[:4], result[4:]


def run_mlp(mlp, cotangent, residual, gain, weights):
    rows, width = mlp.shape
    channels = weights[0].shape[1]
    result = pl.pallas_call(
        mlp_kernel,
        grid=(rows // PACK,),
        in_specs=[packed(width)] * 3 + [whole((width,))] + [whole(w.shape) for w in weights],
        out_specs=[packed(width)] * 2 + [whole((8, width))] + [whole((4 * width, channels))] * 2,
        out_shape=[shaped((rows, width), bf16), shaped((rows, width), f32), shaped((8, width), f32)]
        + [shaped((4 * width, channels), bf16)] * 2,
        scratch_shapes=[pltpu.VMEM((2 * width, channels), f32)] * 4 + [pltpu.VMEM((PACK, channels), bf16)] * 2,
        compiler_params=params(),
        cost_estimate=cost(20),
        name="mlp_both",
    )(mlp, cotangent, residual, gain, *weights)
    return result[:3], result[3:]


def run_attention_backward(
    sides, grad_two, attn, merged, probs, weights, out_weights, others, qkv, last=None, after=()
):
    rows, width = attn.shape
    packs = rows // PACK
    heads = probs.shape[1]
    final = last is not None
    count = len(sides)
    in_specs = [packed(width)] * 2
    in_specs += [packed(heads * HSZ), pl.BlockSpec((1, heads, PACK, PACK), lambda p: (p, 0, 0, 0))]
    in_specs += [whole(w.shape) for w in (*weights, *out_weights)] + [flag_spec(w) for w in others]
    in_specs += [packed(384)] * count
    args = [grad_two, attn, merged, probs, *weights, *out_weights, *others, *qkv]
    grads = [whole((width + 128, 384))] * count
    grad_shapes = [shaped((width + 128, 384), bf16)] * count
    scratch = [pltpu.VMEM((width + 128, 384), f32)] * count
    if final:
        partial, residual, projected, gain_attn, gain_conv, mixed = last
        in_specs += [packed(width)] * 3 + [whole((width,))] * 2 + [packed(384)] * 4
        args += [partial, residual, projected, gain_attn, gain_conv, *mixed]
        out_specs = [packed(width)] * 2 + [whole((8, width))] * 2 + [whole((2 * width, 384))] * 2
        out_shape = [shaped((rows, width), f32), shaped((rows, width), bf16)]
        out_shape += [shaped((8, width), f32)] * 2 + [shaped((2 * width, 384), bf16)] * 2
        scratch += [pltpu.VMEM((width, 384), f32)] * 4
    else:
        out_specs = [packed(width)]
        out_shape = [shaped((rows, width), f32)]
    result = pl.pallas_call(
        functools.partial(attention_backward_kernel, sides, final),
        grid=(packs,),
        in_specs=in_specs + [anywhere] * len(after),
        out_specs=out_specs + grads,
        out_shape=out_shape + grad_shapes,
        scratch_shapes=scratch
        + [pltpu.VMEM((PACK, 384), bf16), pltpu.VMEM((PACK, 384), f32), pltpu.VMEM((PACK, PACK), bf16)],
        compiler_params=params(),
        cost_estimate=cost(23 if final else 14),
        name="attention_backward",
    )(*args, *after)
    return result[:-count], result[-count:]


def run_conv_backward(grad_projected, tokens, mover, side, gains, other, expanded, mixed, after=()):
    rows, width = tokens.shape
    channels = other.shape[1]
    grad_shape = (width + 16, channels)
    return pl.pallas_call(
        conv_backward_kernel,
        grid=(rows // PACK,),
        in_specs=[packed(width)] * 2
        + [pl.BlockSpec((2 * PACK, SPAN), lambda p: (p, 0)), packed(256)]
        + [whole((8, width))] * 3
        + [whole(other.shape)]
        + [packed(channels)] * 2
        + [anywhere] * len(after),
        out_specs=[packed(channels), whole(grad_shape)],
        out_shape=[shaped((rows, channels), bf16), shaped(grad_shape, bf16)],
        scratch_shapes=[pltpu.VMEM(grad_shape, f32)],
        compiler_params=params(),
        cost_estimate=cost(7),
        name="conv_backward",
    )(grad_projected, tokens, mover, side, *gains, other, expanded, mixed, *after)


def run_token_grad(grad_one, grads, weights, after=()):
    rows, width = grad_one.shape
    return pl.pallas_call(
        token_grad_kernel,
        grid=(rows // PACK,),
        in_specs=[packed(width)]
        + [packed(g.shape[1]) for g in grads]
        + [whole(w.shape) for w in weights]
        + [anywhere] * len(after),
        out_specs=packed(width),
        out_shape=shaped((rows, width), bf16),
        compiler_params=params(),
        cost_estimate=cost(4),
        name="token_grad",
    )(grad_one, *grads, *weights, *after)


vmem = pl.BlockSpec(memory_space=pltpu.VMEM)
anywhere = pl.BlockSpec(memory_space=pl.ANY)


def run_join(index, mine, other, sizes, turns):
    rows, columns = mine.shape
    forms = {"plain": lambda s: (s, columns), "turned": lambda s: (columns, s), "slabs": lambda s: (columns // 128, s, 128)}
    shapes = [forms[turn](s) for s, turn in zip(sizes, turns)]
    return pl.pallas_call(
        functools.partial(join_kernel, turns),
        in_specs=[smem, vmem, vmem],
        out_specs=[vmem] * len(sizes),
        out_shape=[shaped(s, f32) for s in shapes],
        scratch_shapes=[pltpu.VMEM((2 * rows, columns), f32)],
        compiler_params=params(),
        cost_estimate=cost(2),
        name="join_halves",
    )(index, mine, other)


def per_device(
    tokens, cotangent, shapes, head_mask, w_expand, w_depth, w_project, gain_conv, gain_attn, w_qkv, w_out,
    gain_mlp, w_up, w_down,
):
    rows, width = tokens.shape
    packs = rows // PACK
    channels = w_expand.shape[1]
    tensor_size = lax.axis_size("tensor")
    dp_size = lax.axis_size("dp")
    me_dp = lax.axis_index("dp")
    bits = [1 << b for b in range(dp_size.bit_length() - 1)]
    place = {bit: ((me_dp & bit) != 0).astype(jnp.int32) for bit in bits}

    def hold(x, after):
        return lax.optimization_barrier((x, after))[0]

    def swap_tensor(x, bit):
        return lax.ppermute(x, "tensor", [(i, i ^ bit) for i in range(tensor_size)])

    def swap_dp(x, bit):
        return lax.ppermute(x, "dp", [(i, i ^ bit) for i in range(dp_size)])

    def add(*parts):
        total = parts[0].astype(f32)
        for part in parts[1:]:
            total = total + part.astype(f32)
        return total.astype(bf16)

    def near_far(keep, pair):
        half = keep.shape[0] // 2
        return add(keep[:half], pair[:half]), add(keep[half:], pair[half:])

    def part(x, bit, mine):
        half = x.shape[0] // 2
        chosen = place[bit] if mine else 1 - place[bit]
        return lax.dynamic_slice_in_dim(x, chosen * half, half, 0)

    def halves(x, bit):
        return part(x, bit, True), swap_dp(part(x, bit, False), bit)

    def both(mine, other, bit):
        first = place[bit] == 0
        return jnp.concatenate([jnp.where(first, mine, other), jnp.where(first, other, mine)])

    def rest(x):
        for bit in bits[3:]:
            x = add(x, swap_dp(x, bit))
        return x

    other = jnp.concatenate(
        [
            w_project,
            w_depth,
            jnp.pad(head_mask.astype(bf16)[None, :], ((0, 6), (0, channels - head_mask.shape[0]))),
        ]
    )
    slabs = w_qkv.transpose(1, 0, 2).reshape(-1, w_qkv.shape[2])
    mlp = jnp.concatenate([w_up, w_down])
    near_w = [[x, swap_tensor(x, 1)] for x in (w_expand, other, slabs, w_out, mlp)]
    far_w = [swap_tensor(x, 2) for x in (w_expand, other, slabs, w_out, mlp)]
    expand_w, other_w, slab_w, out_w, mlp_w = near_w

    mover, side, segment, segment_row = run_geometry(shapes, packs)
    exp_a, mix_a, (partial,) = run_conv_forward(tokens, mover, side, expand_w, other_w)
    for which in (0, 1):
        near_w[which] += [far_w[which], swap_tensor(hold(far_w[which], partial), 1)]
    exp_b, mix_b, (partial,) = run_conv_forward(tokens, mover, side, expand_w[2:3], other_w[2:3], partial)
    for which in (2, 3):
        near_w[which] += [far_w[which], swap_tensor(hold(far_w[which], partial), 1)]
    exp_c, mix_c, (projected, residual_one, attn_low) = run_conv_forward(
        tokens, mover, side, expand_w[3:], other_w[3:], partial, (gain_conv, gain_attn)
    )
    expanded, mixed = [*exp_a, *exp_b, *exp_c], [*mix_a, *mix_b, *mix_c]
    qkv, (probs, merged, residual_two, mlp_low) = run_attention_forward(
        attn_low, residual_one, segment, segment_row, gain_mlp, slab_w, out_w, other_w
    )
    mlp_w += [far_w[4], swap_tensor(hold(far_w[4], attn_low), 1)]
    (out_tokens, grad_two, gain_m), (mlp_keep, mlp_mate) = run_mlp(mlp_low, cotangent, residual_two, gain_mlp, mlp_w)
    mlp_pair = swap_tensor(mlp_mate, 1)

    def attention_backward(sides, last=None, after=()):
        return run_attention_backward(
            sides, grad_two, attn_low, merged, probs, *([w[s] for s in sides] for w in (slab_w, out_w, other_w, qkv)),
            last, after,
        )

    def conv_backward(block, after):
        return run_conv_backward(
            grad_projected, tokens, mover, side, gains, other_w[block], expanded[block], mixed[block], after
        )

    (grad_in,), (attn_3, attn_2) = attention_backward((3, 2))
    attn_pair_3 = swap_tensor(attn_3, 1)
    mlp_near, mlp_far = near_far(mlp_keep, hold(mlp_pair, grad_in))
    mlp_cross = swap_tensor(mlp_far, 2)

    last_args = (grad_in, residual_one, projected, gain_attn, gain_conv, mixed)
    (grad_one, grad_projected, gain_a, gain_c, proj_keep, proj_mate), (attn_1, attn_0) = attention_backward(
        (1, 0), last_args, (mlp_near, mlp_far)
    )
    gains = (gain_c, gain_a, gain_m)
    attn_pair_1 = swap_tensor(attn_1, 1)
    proj_pair = swap_tensor(proj_mate, 1)
    attn_far = add(attn_2, hold(attn_pair_3, attn_0))
    attn_cross = swap_tensor(attn_far, 2)
    mlp_half, mlp_other = halves(add(mlp_near, hold(mlp_cross, attn_0)), 1)

    grad_3, conv_3 = conv_backward(3, (attn_far, mlp_half))
    conv_pair_3 = swap_tensor(conv_3, 1)
    proj_near, proj_far = near_far(proj_keep, hold(proj_pair, conv_3))
    proj_cross = swap_tensor(proj_far, 2)
    mlp_half, mlp_other = halves(add(mlp_half, hold(mlp_other, conv_3)), 2)

    grad_2, conv_2 = conv_backward(2, (proj_far, mlp_half))
    conv_far = add(conv_2, hold(conv_pair_3, conv_2))
    conv_cross = swap_tensor(conv_far, 2)
    attn_sum = add(attn_0, attn_pair_1, hold(attn_cross, conv_2))
    proj_sum = add(proj_near, hold(proj_cross, conv_2))
    attn_half, attn_other = halves(jnp.concatenate([attn_sum, proj_sum]), 1)
    mlp_half = add(mlp_half, hold(mlp_other, conv_2))
    mlp_other = swap_dp(mlp_half, 4)

    grad_1, conv_1 = conv_backward(1, (conv_far, mlp_half, attn_half))
    conv_pair_1 = swap_tensor(conv_1, 1)
    attn_half, attn_other = halves(add(attn_half, hold(attn_other, conv_1)), 2)
    mlp_half = rest(add(mlp_half, hold(mlp_other, conv_1)))
    mlp_other = swap_dp(mlp_half, 2)

    grad_0, conv_0 = conv_backward(0, (mlp_half, attn_half))
    conv_near = add(conv_0, hold(conv_pair_1, conv_0), hold(conv_cross, conv_0))
    small = conv_near[width:]
    main = conv_near[:width]
    tail = jnp.concatenate([part(main, 1, True), small])
    tail_other = swap_dp(jnp.concatenate([part(main, 1, False), small]), 1)
    mlp_half = both(mlp_half, hold(mlp_other, conv_0), 2)
    mlp_other = swap_dp(mlp_half, 1)
    attn_half = add(attn_half, hold(attn_other, conv_0))
    attn_other = swap_dp(attn_half, 4)
    grad_tokens = run_token_grad(grad_one, [grad_0, grad_1, grad_2, grad_3], expand_w, (tail, mlp_half, attn_half))
    half = width // 2
    tail = add(tail, hold(tail_other, grad_tokens))
    main, small = tail[:half], tail[half:]
    tail_other = swap_dp(jnp.concatenate([part(main, 2, False), small]), 2)
    tail = jnp.concatenate([part(main, 2, True), small])
    attn_half = rest(add(attn_half, hold(attn_other, grad_tokens)))
    attn_other = swap_dp(attn_half, 2)
    tail = add(tail, tail_other)
    tail = rest(add(tail, swap_dp(tail, 4)))
    half = half // 2
    main, small = tail[:half], tail[half:].astype(f32)
    attn_half = both(attn_half, attn_other, 2)
    attn_other = swap_dp(attn_half, 1)
    main = both(main, swap_dp(main, 2), 2)
    main_other = swap_dp(main, 1)
    index = place[1][None]
    grad_up, grad_down = run_join(index, mlp_half, mlp_other, (width, width), ("plain", "turned"))
    grad_qkv, grad_out, grad_project = run_join(
        index, attn_half, attn_other, (width, w_out.shape[0], width), ("slabs", "plain", "turned")
    )
    (grad_expand,) = run_join(index, main, main_other, (width,), ("plain",))
    gain_sums = small[9:12] + small[12:15]
    return (
        out_tokens, grad_tokens, grad_expand, small[:9], grad_project, gain_sums[0], gain_sums[1],
        grad_qkv.transpose(1, 0, 2), grad_out, gain_sums[2], grad_up, grad_down,
    )


def solution(mesh):
    rows = P(("dp", "tensor"), None)
    cols = P(None, "tensor")
    down = P("tensor", None)
    return jax.shard_map(
        per_device,
        mesh=mesh,
        in_specs=(
            rows, rows, P("dp", None, None), P("tensor"), cols, cols, down, P(), P(), P(None, None, "tensor"), down,
            P(), cols, down,
        ),
        out_specs=(rows, rows, cols, cols, down, P(), P(), P(None, None, "tensor"), down, P(), cols, down),
        check_vma=False,
    )
```

```python
import functools
import jax
import jax.numpy as jnp
from jax import lax
from jax.experimental import pallas as pl
from jax.experimental.pallas import tpu as pltpu
from jax.sharding import PartitionSpec as P

HSZ = 64
PACK = 512
SPAN = 256
SPLIT = (0, 240, 480, 512)
UP_FROM = (0, 224, 256)
DOWN_FROM = (0, 240, 256)

epsilon = 1e-05
f32 = jnp.float32
bf16 = jnp.bfloat16


def mm(a, b):
    return jnp.dot(a, b, preferred_element_type=f32)


def mm_t(a, b):
    return lax.dot_general(a, b, (((1,), (1,)), ((), ())), preferred_element_type=f32)


def t_mm(a, b):
    return lax.dot_general(a, b, (((0,), (0,)), ((), ())), preferred_element_type=f32)


def standard(values):
    centred = values - jnp.mean(values, axis=-1, keepdims=True)
    inverse = lax.rsqrt(jnp.mean(centred * centred, axis=-1, keepdims=True) + epsilon)
    return centred * inverse, inverse


def standard_back(grad, unit, inverse):
    mean_grad = jnp.mean(grad, axis=-1, keepdims=True)
    mean_both = jnp.mean(grad * unit, axis=-1, keepdims=True)
    return (grad - mean_grad - unit * mean_both) * inverse


def geometry_kernel(shape_ref, mover_ref, side_ref, segment_ref, segment_row_ref, slot_ref):
    own = lax.axis_index("tensor") * pl.num_programs(0) + pl.program_id(0)
    slot_ref[...] = jnp.zeros_like(slot_ref)
    slot_ref[0:2, 0 : shape_ref.shape[2]] = shape_ref[own].astype(f32)
    sides = slot_ref[...]
    height_slots = sides[0:1]
    width_slots = sides[1:2]
    sizes = jnp.broadcast_to(height_slots * width_slots, (8, 128))
    before = lax.broadcasted_iota(jnp.int32, (128, 128), 0)
    after = lax.broadcasted_iota(jnp.int32, (128, 128), 1)
    ends = mm(sizes.astype(bf16), (before <= after).astype(bf16))[0:1]
    starts = ends - height_slots * width_slots
    places = lax.broadcasted_iota(jnp.int32, (PACK, 128), 0).astype(f32)
    here = ((starts <= places) & (places < ends)).astype(f32)
    image_start = jnp.sum(here * starts, axis=1, keepdims=True)
    height = jnp.sum(here * height_slots, axis=1, keepdims=True)
    width = jnp.sum(here * width_slots, axis=1, keepdims=True)
    place = places[:, 0:1]
    offset = place - image_start
    safe = jnp.maximum(width, 1.0)
    grid_row = jnp.floor((offset + 0.5) / safe)
    grid_col = offset - grid_row * safe
    above = jnp.where(grid_row >= 1.0, place - width, -1.0)
    below = jnp.where(grid_row + 1.0 < height, place + width, -1.0)
    lanes = lax.broadcasted_iota(jnp.int32, (1, SPAN), 1).astype(f32)
    for part in range(3):
        low, high = SPLIT[part], SPLIT[part + 1]
        for which, (target, origin) in enumerate(((above, UP_FROM[part]), (below, DOWN_FROM[part]))):
            hit = (target[low:high] == lanes + origin).astype(f32).astype(bf16)
            mover_ref[which * PACK + low : which * PACK + high] = hit
    side_ref[:, 0:128] = jnp.broadcast_to((grid_col >= 1.0).astype(f32), (PACK, 128))
    side_ref[:, 128:256] = jnp.broadcast_to((grid_col + 1.0 < width).astype(f32), (PACK, 128))
    segment = jnp.broadcast_to(image_start, (PACK, 128))
    segment_ref[...] = segment
    segment_row_ref[0] = segment.T[0:8]


def gelu_parts(values):
    size = jnp.abs(values)
    t = 1.0 / (1.0 + size * (0.3275911 * 0.7071067811865476))
    bell = jnp.exp(values * values * -0.5)
    poly = t * (
        0.5 * 0.254829592
        + t * (0.5 * -0.284496736 + t * (0.5 * 1.421413741 + t * (0.5 * -1.453152027 + t * (0.5 * 1.061405429))))
    )
    upper = poly * bell
    cdf = jnp.where(values >= 0, 1.0 - upper, upper)
    return values * cdf, cdf + values * bell * 0.3989422804014327


def mlp_kernel(ins, wait, outs, send, act_ref, pre_ref, down_ref, up_ref, turned_ref, *buffers):
    mlp_ref, cotangent_ref, residual_ref, gain_ref = ins[:4]
    weight_refs = ins[4:]
    out_ref, grad_two_ref, gain_grad_ref, keep_ref, mate_ref = outs
    rows, width = mlp_ref.shape
    size = 256
    chunks = rows // size
    wait(0)
    turned_ref[0] = mlp_ref[...].T
    wait(1)
    turned_ref[1] = cotangent_ref[...].T

    def arrange(half, blocks):
        for side, block in enumerate(blocks):
            wait(4 + block)
            lanes = slice(side * width, (side + 1) * width)
            down_ref[half, lanes] = weight_refs[block][width:]
            up_ref[half, :, lanes] = weight_refs[block][0:width]

    arrange(0, (1, 3))
    arrange(1, (0, 2))

    def products(j, buffer):
        half = j // chunks
        r = pl.ds((j % chunks) * size, size)
        buffer[0] = mm(mlp_ref[r], up_ref[half])
        buffer[1] = mm_t(cotangent_ref[r], down_ref[half])

    def gates(j, buffer):
        half = j // chunks
        r = pl.ds((j % chunks) * size, size)
        act, slope = gelu_parts(buffer[0])
        act_ref[half, r] = act.astype(bf16)
        pre_ref[half, r] = (buffer[1] * slope).astype(bf16)

    products(0, buffers[0])

    def one(k, carry):
        products(2 * k + 1, buffers[1])
        gates(2 * k, buffers[0])
        products(jnp.minimum(2 * k + 2, 2 * chunks - 1), buffers[0])
        gates(2 * k + 1, buffers[1])
        return carry

    lax.fori_loop(0, chunks, one, 0)
    for half, target in enumerate((mate_ref, keep_ref)):
        grad_up = mm(turned_ref[0], pre_ref[half]).astype(bf16)
        grad_down = mm(turned_ref[1], act_ref[half]).astype(bf16)
        for place in range(2):
            base = place * 2 * width
            target[base : base + width] = grad_up[:, place * width : place * width + width]
            target[base + width : base + 2 * width] = grad_down[:, place * width : place * width + width]
        send(3 if half else 4)
    wait(2)
    wait(3)
    gain_grad_ref[...] = jnp.zeros_like(gain_grad_ref)

    def finish(c, carry):
        r = pl.ds(c * size, size)
        grad_in = mm_t(pre_ref[0, r], up_ref[0]) + mm_t(pre_ref[1, r], up_ref[1])
        residual = residual_ref[r]
        out = residual + (mm(act_ref[0, r], down_ref[0]) + mm(act_ref[1, r], down_ref[1]))
        out_ref[r] = out.astype(bf16)
        send(0, c)
        unit, inverse = standard(residual)
        gain_grad_ref[...] += jnp.sum((grad_in * unit).reshape(size // 8, 8, width), axis=0)
        grad_two_ref[r] = cotangent_ref[r].astype(f32) + standard_back(grad_in * gain_ref[...], unit, inverse)
        send(1, c)
        return carry

    lax.fori_loop(0, chunks, finish, 0)
    send(2)


def run_mlp(mlp, cotangent, residual, gain, weights):
    rows, width = mlp.shape
    channels = weights[0].shape[1]
    grads = shaped((4 * width, channels), bf16)
    wide = 2 * channels
    result = call_staged(
        mlp_kernel,
        "mlp_both",
        [mlp, cotangent, residual, gain, *weights],
        [shaped((rows, width), bf16), shaped((rows, width), f32), shaped((8, width), f32), grads, grads],
        [
            pltpu.VMEM((2, rows, wide), bf16),
            pltpu.VMEM((2, rows, wide), bf16),
            pltpu.VMEM((2, wide, width), bf16),
            pltpu.VMEM((2, width, wide), bf16),
            pltpu.VMEM((2, width, rows), bf16),
            pltpu.VMEM((2, 256, wide), f32),
            pltpu.VMEM((2, 256, wide), f32),
        ],
        16,
        out_parts={0: rows // 256, 1: rows // 256},
        order=(0, 5, 7, 1, 4, 6, 2, 3),
    )
    return result[:3], result[3:]


HEADS_ON = 6


def list_heads(flag_refs, list_ref):
    count = jnp.int32(0)
    for head in range(2 * len(flag_refs)):
        on = flag(flag_refs[head // 2], head % 2)

        @pl.when(on)
        def _(count=count, head=head):
            list_ref[count] = jnp.int32(head)

        count = count + on.astype(jnp.int32)


def flag(flag_ref, side):
    return jnp.max(flag_ref[9:10, side : side + 1].astype(f32)) != 0


def lane_joined(weight_ref):
    rows = weight_ref.shape[0] // 3
    return jnp.concatenate([weight_ref[j * rows : (j + 1) * rows] for j in range(3)], axis=1)


def attention_forward_kernel(ins, wait, outs, send, list_ref, wide_ref):
    attn_ref, segment_ref, segment_row_ref, residual_ref, gain_ref = ins[:5]
    slab_refs, out_weight_refs, flag_refs = ins[5:9], ins[9:13], ins[13:17]
    qkv_ref, exps_ref, inverse_ref, merged_ref, residual_two_ref, mlp_ref = outs
    rows, width = attn_ref.shape
    for i in range(13, 17):
        wait(i)
    list_heads(flag_refs, list_ref)
    merged_ref[...] = jnp.zeros_like(merged_ref)
    inverse_ref[...] = jnp.zeros_like(inverse_ref)
    wait(5)
    wait(6)
    wait(0)
    for half in range(2):
        if half:
            wait(7)
            wait(8)
        for side in range(2):
            wide_ref[half, :, side * width : (side + 1) * width] = lane_joined(slab_refs[2 * half + side])
        projections = mm(attn_ref[...], wide_ref[half]).astype(bf16)
        for side in range(2):
            qkv_ref[2 * half + side] = projections[:, side * width : (side + 1) * width]
            send(0, 2 * half + side)
    wait(1)
    wait(2)
    lane = lax.broadcasted_iota(jnp.int32, (1, 128), 1)

    def one(i, carry):
        head = list_ref[i]
        pair = head // 2
        mine = (lane // HSZ) == (head % 2)
        scale = jnp.where(mine, HSZ**-0.5, 0.0).astype(bf16)
        for pack in range(rows // PACK):
            part = slice(pack * PACK, (pack + 1) * PACK)
            keys = qkv_ref[pair, part, 128:256]
            values = jnp.concatenate([qkv_ref[pair, part, 256:384], jnp.ones((PACK, 128), bf16)], axis=1)
            segment_row = segment_row_ref[pack, 0:1]
            for block in range(0, PACK, 256):
                r = slice(pack * PACK + block, pack * PACK + block + 256)
                scores = mm_t(qkv_ref[pair, r, 0:128] * scale, keys)
                segment = jnp.concatenate([segment_ref[r]] * (PACK // 128), axis=1)
                scores = jnp.where(segment == segment_row, scores, -1e30)
                exps = jnp.exp(scores - jnp.max(scores, axis=1, keepdims=True)).astype(bf16)
                exps_ref[i, r] = exps
                out = mm(exps, values)
                inverse = 1.0 / out[:, 128:256]
                merged_ref[pair, r] = jnp.where(mine, out[:, 0:128] * inverse, merged_ref[pair, r].astype(f32)).astype(bf16)
                inverse_ref[r] = jnp.where(lane == i, inverse, inverse_ref[r])
        send(1, i)
        return carry

    lax.fori_loop(0, HEADS_ON, one, 0, unroll=2)
    send(2)
    send(3)
    wait(3)
    wait(4)
    for pair in range(4):
        wait(9 + pair)
    out_weight = jnp.concatenate([w[...] for w in out_weight_refs], axis=0)
    for part in range(4):
        r = slice(part * rows // 4, (part + 1) * rows // 4)
        merged = jnp.concatenate([merged_ref[pair, r] for pair in range(4)], axis=1)
        total = residual_ref[r] + mm(merged, out_weight)
        residual_two_ref[r] = total
        send(4, part)
        unit, _ = standard(total)
        mlp_ref[r] = (unit * gain_ref[...]).astype(bf16)
        send(5, part)


def run_attention_forward(attn, residual, segment, segment_row, gain, slabs, out_weights, flags):
    rows, width = attn.shape
    outs = [
        shaped((4, rows, 384), bf16),
        shaped((HEADS_ON, rows, PACK), bf16),
        shaped((rows, 128), f32),
        shaped((4, rows, 128), bf16),
        shaped((rows, width), f32),
        shaped((rows, width), bf16),
    ]
    return call_staged(
        attention_forward_kernel,
        "attention_forward",
        [attn, segment, segment_row, residual, gain, *slabs, *out_weights, *flags],
        outs,
        [pltpu.SMEM((8,), jnp.int32), pltpu.VMEM((2, width, 768), bf16)],
        14,
        out_parts={0: 4, 1: HEADS_ON, 4: 4, 5: 4},
        order=(13, 14, 15, 16, 5, 6, 0, 7, 8, 1, 2, 9, 10, 11, 12, 4, 3),
    )


def attention_core_back_kernel(ins, wait, outs, send, list_ref, merged_grad_ref, score_ref):
    grad_two_ref, qkv_ref, exps_ref, inverse_ref, merged_ref = ins[:5]
    out_weight_refs, flag_refs = ins[5:9], ins[9:13]
    grad_proj_ref, grad_out_ref = outs
    rows, width = grad_two_ref.shape
    for i in range(9, 13):
        wait(i)
    list_heads(flag_refs, list_ref)
    grad_proj_ref[...] = jnp.zeros_like(grad_proj_ref)
    wait(0)
    low = grad_two_ref[...].astype(bf16)
    for i in range(5, 9):
        wait(i)
    out_weight = jnp.concatenate([w[...] for w in out_weight_refs], axis=0)
    grad_merged = mm_t(low, out_weight).astype(bf16)
    for pair in range(4):
        merged_grad_ref[pair] = grad_merged[:, pair * 128 : pair * 128 + 128]
    wait(4)
    for pair in range(4):
        grad_out_ref[pair] = t_mm(merged_ref[pair], low).astype(bf16)
    send(1)
    wait(1)
    wait(3)
    lane = lax.broadcasted_iota(jnp.int32, (1, 128), 1)

    def one(i, carry):
        head = list_ref[i]
        pair = head // 2
        mine = (lane // HSZ) == (head % 2)
        wait(2, i)
        for pack in range(rows // PACK):
            part = slice(pack * PACK, (pack + 1) * PACK)
            inverse = jnp.sum(jnp.where(lane == i, inverse_ref[part], 0.0), axis=1, keepdims=True)
            grad_heads = jnp.where(mine, merged_grad_ref[pair, part].astype(f32) * inverse, 0.0).astype(bf16)
            delta = jnp.sum(grad_heads.astype(f32) * merged_ref[pair, part].astype(f32), axis=1, keepdims=True)
            values = qkv_ref[pair, part, 256:384]
            for block in range(0, PACK, 256):
                r = slice(pack * PACK + block, pack * PACK + block + 256)
                b = slice(block, block + 256)
                grad_probs = mm_t(grad_heads[b], values)
                score_ref[pack, b] = (exps_ref[i, r].astype(f32) * (grad_probs - delta[b])).astype(bf16)
            grad_scores = score_ref[pack]
            grad_q = mm(grad_scores, qkv_ref[pair, part, 128:256]) * HSZ**-0.5
            grad_k = t_mm(grad_scores, qkv_ref[pair, part, 0:128]) * HSZ**-0.5
            grad_v = t_mm(exps_ref[i, part], grad_heads)
            for j, grad in enumerate((grad_q, grad_k, grad_v)):
                lanes = slice(j * 128, j * 128 + 128)
                grad_proj_ref[pair, part, lanes] = jnp.where(
                    mine, grad, grad_proj_ref[pair, part, lanes].astype(f32)
                ).astype(bf16)
        return carry

    lax.fori_loop(0, HEADS_ON, one, 0)
    send(0)


def run_attention_core_back(grad_two, qkv, exps, inverse, merged, out_weights, flags, after=()):
    rows, width = grad_two.shape
    return call_staged(
        attention_core_back_kernel,
        "attention_core_back",
        [grad_two, qkv, exps, inverse, merged, *out_weights, *flags],
        [shaped(qkv.shape, bf16), shaped((4, 128, width), bf16)],
        [pltpu.SMEM((8,), jnp.int32), pltpu.VMEM((4, rows, 128), bf16), pltpu.VMEM((rows // PACK, PACK, PACK), bf16)],
        12,
        after,
        in_parts={2: HEADS_ON},
        order=(9, 10, 11, 12, 5, 6, 7, 8, 0, 4, 3, 1, 2),
    )


def attention_rest_back_kernel(ins, wait, outs, send, wide_ref, pair_ref):
    attn_ref, grad_proj_ref, grad_two_ref, residual_ref, projected_ref, grad_out_ref, gain_attn_ref, gain_conv_ref = ins[:8]
    slab_refs, acted_refs = ins[8:12], ins[12:16]
    grad_one_ref, grad_projected_ref, gain_attn_grad_ref, gain_conv_grad_ref, keep_ref, mate_ref = outs
    rows, width = attn_ref.shape
    stride = 2 * width + 128
    wait(0)
    attn_t = attn_ref[...].T
    for half in range(2):
        for side in range(2):
            wait(8 + 2 * half + side)
            wait(1, 2 * half + side)
            lanes = slice(side * width, (side + 1) * width)
            wide_ref[half, :, lanes] = lane_joined(slab_refs[2 * half + side])
            pair_ref[half, :, lanes] = grad_proj_ref[2 * half + side]
        grad_qkv = mm(attn_t, pair_ref[half]).astype(bf16)
        for side, target in enumerate((keep_ref, mate_ref)):
            target[half * stride : half * stride + width] = grad_qkv[:, side * width : (side + 1) * width]
    for i in (2, 3, 4, 5, 6, 7):
        wait(i)
    for half in range(2):
        for side, target in enumerate((keep_ref, mate_ref)):
            target[half * stride + width : half * stride + width + 128] = grad_out_ref[2 * half + side]
    gain_attn_grad_ref[...] = jnp.zeros_like(gain_attn_grad_ref)
    gain_conv_grad_ref[...] = jnp.zeros_like(gain_conv_grad_ref)
    size = rows // 4
    for part in range(4):
        r = slice(part * size, (part + 1) * size)
        grad_in = mm_t(pair_ref[0, r], wide_ref[0]) + mm_t(pair_ref[1, r], wide_ref[1])
        unit, inverse = standard(residual_ref[r])
        gain_attn_grad_ref[...] += jnp.sum((grad_in * unit).reshape(size // 8, 8, width), axis=0)
        grad_one = grad_two_ref[r] + standard_back(grad_in * gain_attn_ref[...], unit, inverse)
        grad_one_ref[r] = grad_one
        unit, inverse = standard(projected_ref[r])
        gain_conv_grad_ref[...] += jnp.sum((grad_one * unit).reshape(size // 8, 8, width), axis=0)
        grad_projected_ref[r] = standard_back(grad_one * gain_conv_ref[...], unit, inverse).astype(bf16)
    for i in range(4):
        send(i)
    projected_t = grad_projected_ref[...].T
    for half in range(2):
        wait(12 + 2 * half)
        wait(13 + 2 * half)
        acted = jnp.concatenate([acted_refs[2 * half][...], acted_refs[2 * half + 1][...]], axis=1)
        grad_project = mm(projected_t, acted).astype(bf16)
        for side, target in enumerate((keep_ref, mate_ref)):
            start = half * stride + width + 128
            target[start : start + width] = grad_project[:, side * width : (side + 1) * width]
    send(5)
    send(4)


def run_attention_rest_back(
    attn, grad_proj, grad_two, residual, projected, grad_out, gain_attn, gain_conv, slabs, acted, after=()
):
    rows, width = attn.shape
    grads = shaped((2 * (2 * width + 128), 384), bf16)
    return call_staged(
        attention_rest_back_kernel,
        "attention_rest_back",
        [attn, grad_proj, grad_two, residual, projected, grad_out, gain_attn, gain_conv, *slabs, *acted],
        [shaped((rows, width), f32), shaped((rows, width), bf16), *[shaped((8, width), f32)] * 2, grads, grads],
        [pltpu.VMEM((2, width, 2 * width), bf16), pltpu.VMEM((2, rows, 2 * width), bf16)],
        12,
        after,
        in_parts={1: 4},
        order=(0, 8, 9, 1, 10, 11, 3, 2, 6, 4, 7, 5, 12, 13, 14, 15),
    )


def small_rows(gain_refs, width):
    gains = jnp.concatenate([jnp.sum(ref[...], axis=0, keepdims=True) for ref in gain_refs], axis=0)
    high = gains.astype(bf16).astype(f32)
    return high, gains - high


def join_kernel(turns, index_ref, mine_ref, other_ref, *refs):
    out_refs = refs[:-1]
    whole_ref = refs[-1]
    first = index_ref[0] == 0
    rows = mine_ref.shape[0]
    mine = mine_ref[...].astype(f32)
    other = other_ref[...].astype(f32)
    whole_ref[0:rows] = jnp.where(first, mine, other)
    whole_ref[rows:] = jnp.where(first, other, mine)
    start = 0
    for out_ref, turn in zip(out_refs, turns):
        if turn == "slabs":
            rows = out_ref.shape[1]
            for j in range(out_ref.shape[0]):
                out_ref[j] = whole_ref[start : start + rows, j * 128 : j * 128 + 128]
        elif turn == "turned":
            rows = out_ref.shape[1]
            out_ref[...] = whole_ref[start : start + rows].T
        else:
            rows = out_ref.shape[0]
            out_ref[...] = whole_ref[start : start + rows]
        start += rows


def whole(shape):
    zeros = (0,) * len(shape)
    return pl.BlockSpec(shape, lambda p: zeros)


def packed(columns):
    return pl.BlockSpec((PACK, columns), lambda p: (p, 0))


def params(megabytes=56):
    return pltpu.CompilerParams(vmem_limit_bytes=megabytes << 20)


def cost(microseconds):
    return pl.CostEstimate(
        flops=int(microseconds * 1.1e9), bytes_accessed=int(microseconds * 3.0e6), transcendentals=0
    )


smem = pl.BlockSpec(memory_space=pltpu.SMEM)


def shaped(shape, dtype):
    return jax.ShapeDtypeStruct(shape, dtype)


vmem = pl.BlockSpec(memory_space=pltpu.VMEM)
anywhere = pl.BlockSpec(memory_space=pl.ANY)


def call_staged(
    kernel, name, ins, outs, scratch, microseconds, after=(), in_parts=None, out_parts=None, order=None,
    megabytes=56,
):
    in_parts, out_parts = in_parts or {}, out_parts or {}
    n, m, skip = len(ins), len(outs), len(after)
    windows = {i: x[1:] for i, x in enumerate(ins) if isinstance(x, tuple)}
    ins = [x[0] if isinstance(x, tuple) else x for x in ins]
    sizes = [(windows[i][1], *x.shape[1:]) if i in windows else x.shape for i, x in enumerate(ins)]

    def body(*refs):
        in_hbm, refs = refs[:n], refs[n + skip :]
        out_hbm, refs = refs[:m], refs[m:]
        in_vmem, refs = refs[:n], refs[n:]
        out_vmem, refs = refs[:m], refs[m:]
        in_sems, refs = refs[:n], refs[n:]
        out_sems, refs = refs[:m], refs[m:]

        def copy(source, target, sem, parts, which):
            if parts == 1:
                return pltpu.make_async_copy(source, target, sem.at[0])
            size = source.shape[0] // parts
            rows = pl.ds(which * size, size)
            return pltpu.make_async_copy(source.at[rows], target.at[rows], sem.at[which])

        def load(i, which=0):
            source = in_hbm[i].at[pl.ds(*windows[i])] if i in windows else in_hbm[i]
            return copy(source, in_vmem[i], in_sems[i], in_parts.get(i, 1), which)

        def store(i, which=0):
            return copy(out_vmem[i], out_hbm[i], out_sems[i], out_parts.get(i, 1), which)

        for i in order or range(n):
            for which in range(in_parts.get(i, 1)):
                load(i, which).start()
        kernel(
            in_vmem, lambda i, which=0: load(i, which).wait(), out_vmem, lambda i, which=0: store(i, which).start(), *refs
        )
        for i in range(m):
            for which in range(out_parts.get(i, 1)):
                store(i, which).wait()

    return pl.pallas_call(
        body,
        in_specs=[anywhere] * (n + skip),
        out_specs=[anywhere] * m,
        out_shape=list(outs),
        scratch_shapes=[pltpu.VMEM(size, x.dtype) for size, x in zip(sizes, ins)]
        + [pltpu.VMEM(x.shape, x.dtype) for x in outs]
        + [pltpu.SemaphoreType.DMA((in_parts.get(i, 1),)) for i in range(n)]
        + [pltpu.SemaphoreType.DMA((out_parts.get(i, 1),)) for i in range(m)]
        + list(scratch),
        compiler_params=params(megabytes),
        cost_estimate=cost(microseconds),
        name=name,
    )(*ins, *after)


def run_geometry(shapes, packs):
    return pl.pallas_call(
        geometry_kernel,
        grid=(packs,),
        in_specs=[whole(shapes.shape)],
        out_specs=[
            pl.BlockSpec((2 * PACK, SPAN), lambda p: (p, 0)),
            packed(256),
            packed(128),
            pl.BlockSpec((1, 8, PACK), lambda p: (p, 0, 0)),
        ],
        out_shape=[
            shaped((packs * 2 * PACK, SPAN), bf16),
            shaped((packs * PACK, 256), f32),
            shaped((packs * PACK, 128), f32),
            shaped((packs, 8, PACK), f32),
        ],
        scratch_shapes=[pltpu.VMEM((8, 128), f32)],
        compiler_params=params(),
        cost_estimate=cost(3),
        name="geometry",
    )(shapes)


def conv_forward_kernel(count, has_partial, final, ins, wait, outs, send, raw_ref, up_ref, mid_ref, down_ref):
    token_ref, mover_ref, side_ref = ins[:3]
    weight_refs, other_refs = ins[3 : 3 + count], ins[3 + count : 3 + 2 * count]
    extra = ins[3 + 2 * count :]
    expanded_refs, mixed_refs, acted_refs = outs[:count], outs[count : 2 * count], outs[2 * count : 3 * count]
    rows, width = token_ref.shape
    wide = count * width
    wait(0)
    for i in range(3, 3 + count):
        wait(i)
    weight = jnp.concatenate([w[...] for w in weight_refs], axis=1)
    for i in range(3 + count, 3 + 2 * count):
        wait(i)
    taps = jnp.concatenate([w[width : width + 16] for w in other_refs], axis=1).astype(f32)
    project = jnp.concatenate([w[0:width] for w in other_refs], axis=0)
    total_ref = outs[3 * count]
    for pack in range(rows // PACK):
        base = pack * PACK
        expanded = mm(token_ref[base : base + PACK], weight)
        for tile in range(wide // 128):
            values = expanded[:, tile * 128 : tile * 128 + 128]
            raw_ref[tile, 8 : 8 + PACK] = values
            lanes = slice(tile % 3 * 128, tile % 3 * 128 + 128)
            expanded_refs[tile // 3][base : base + PACK, lanes] = values.astype(bf16)
        if pack == 0:
            wait(2)
        for tile in range(wide // 128):
            lanes = slice(tile * 128, tile * 128 + 128)
            kernel = [taps[k : k + 1, lanes] for k in range(9)]
            for start in range(0, PACK, 32):
                left = raw_ref[tile, 7 + start : 39 + start] * side_ref[base + start : base + start + 32, 0:128]
                mid = raw_ref[tile, 8 + start : 40 + start]
                right = raw_ref[tile, 9 + start : 41 + start] * side_ref[base + start : base + start + 32, 128:256]
                line = [left * kernel[3 * a] + mid * kernel[3 * a + 1] + right * kernel[3 * a + 2] for a in range(3)]
                up_ref[start : start + 32, lanes] = line[0].astype(bf16)
                mid_ref[start : start + 32, lanes] = line[1]
                down_ref[start : start + 32, lanes] = line[2].astype(bf16)
        if pack == 0:
            wait(1)
        for part in range(3):
            low, high = SPLIT[part], SPLIT[part + 1]
            hit = jnp.concatenate(
                [mover_ref[(2 * pack + which) * PACK + low : (2 * pack + which) * PACK + high] for which in range(2)], axis=1
            )
            source = jnp.concatenate(
                [
                    up_ref[UP_FROM[part] : UP_FROM[part] + SPAN],
                    down_ref[DOWN_FROM[part] : DOWN_FROM[part] + SPAN],
                ],
                axis=0,
            )
            mixed = mm(hit, source) + mid_ref[low:high]
            r = slice(base + low, base + high)
            acted = (mixed * jax.nn.sigmoid(mixed)).astype(bf16)
            mixed = mixed.astype(bf16)
            for block in range(count):
                lanes = slice(block * width, block * width + width)
                mixed_refs[block][r] = mixed[:, lanes]
                acted_refs[block][r] = acted[:, lanes]
        for i in range(3 * count):
            send(i, pack)
    for i in range(3 + 2 * count, len(ins)):
        wait(i)
    for part in range(4):
        r = slice(part * rows // 4, (part + 1) * rows // 4)
        total = mm(jnp.concatenate([a[r] for a in acted_refs], axis=1), project)
        if has_partial:
            total = total + extra[0][r]
        total_ref[r] = total
        send(3 * count, part)
        if final:
            residual_ref, attn_ref = outs[3 * count + 1 :]
            gain_conv_ref, gain_attn_ref = extra[1:]
            unit, _ = standard(total)
            residual = token_ref[r].astype(f32) + unit * gain_conv_ref[...]
            residual_ref[r] = residual
            send(3 * count + 1, part)
            unit, _ = standard(residual)
            attn_ref[r] = (unit * gain_attn_ref[...]).astype(bf16)
            send(3 * count + 2, part)


def run_conv_forward(tokens, mover, side, weights, others, partial=None, gains=()):
    rows, width = tokens.shape
    count = len(weights)
    final = len(gains) > 0
    has_partial = partial is not None
    wide = count * width
    outs = [shaped((rows, width), bf16)] * (3 * count) + [shaped((rows, width), f32)]
    if final:
        outs += [shaped((rows, width), f32), shaped((rows, width), bf16)]
    result = call_staged(
        functools.partial(conv_forward_kernel, count, has_partial, final),
        "conv_forward",
        [tokens, mover, side, *weights, *others, *([partial] if has_partial else []), *gains],
        outs,
        [
            pltpu.VMEM((wide // 128, PACK + 16, 128), f32),
            pltpu.VMEM((PACK, wide), bf16),
            pltpu.VMEM((PACK, wide), f32),
            pltpu.VMEM((PACK, wide), bf16),
        ],
        4 * count,
        out_parts={i: rows // PACK if i < 3 * count else 4 for i in range(len(outs))},
        order=(0, *range(3, 3 + 2 * count), 2, 1, *range(3 + 2 * count, 3 + 2 * count + has_partial + len(gains))),
    )
    return result[:count], result[count : 2 * count], result[2 * count : 3 * count], result[3 * count :]


def conv_backward_kernel(count, ins, wait, outs, send, acted_ref, low_ref, moved_ref, turned_ref):
    grad_projected_ref, mover_ref, side_ref, token_ref = ins[:4]
    gain_refs, other_refs = ins[4:7], ins[7 : 7 + count]
    mixed_refs, expanded_refs = ins[7 + count : 7 + 2 * count], ins[7 + 2 * count :]
    grad_expanded_refs, grad_refs = outs[:count], outs[count:]
    rows, width = grad_projected_ref.shape
    tiles = width // 128
    wait(0)
    for block in range(count):
        other_ref, mixed_ref, expanded_ref = other_refs[block], mixed_refs[block], expanded_refs[block]
        grad_expanded_ref, grad_ref = grad_expanded_refs[block], grad_refs[block]
        wait(7 + block)
        project = other_ref[0:width]
        taps = other_ref[width : width + 16].astype(f32)
        sums = [[jnp.zeros((8, 128), f32) for _ in range(9)] for _ in range(tiles)]
        for pack in range(rows // PACK):
            base = pack * PACK
            acted_ref[...] = mm_t(grad_projected_ref[base : base + PACK], project)
            if pack == 0:
                wait(7 + count + block)
            for tile in range(tiles):
                lanes = slice(tile * 128, tile * 128 + 128)
                for start in range(0, PACK, 64):
                    mixed = mixed_ref[base + start : base + start + 64, lanes].astype(f32)
                    gate = jax.nn.sigmoid(mixed)
                    grad = acted_ref[start : start + 64, lanes] * (gate * (1.0 + mixed * (1.0 - gate)))
                    moved_ref[1, tile, 8 + start : 72 + start] = grad
                    low_ref[start : start + 64, lanes] = grad.astype(bf16)
            if pack == 0 and block == 0:
                wait(1)
            for part in range(3):
                low, high = SPLIT[part], SPLIT[part + 1]
                for which, place, origin in ((0, 0, UP_FROM[part]), (1, 2, DOWN_FROM[part])):
                    hit = mover_ref[(2 * pack + which) * PACK + low : (2 * pack + which) * PACK + high]
                    moved = mm(hit, low_ref[origin : origin + SPAN])
                    for tile in range(tiles):
                        moved_ref[place, tile, 8 + low : 8 + high] = moved[:, tile * 128 : tile * 128 + 128]
            if pack == 0:
                if block == 0:
                    wait(2)
                wait(7 + 2 * count + block)
            for tile in range(tiles):
                lanes = slice(tile * 128, tile * 128 + 128)
                kernel = [taps[k : k + 1, lanes] for k in range(9)]
                for start in range(0, PACK, 32):
                    r = slice(base + start, base + start + 32)
                    left_mask, right_mask = side_ref[r, 0:128], side_ref[r, 128:256]
                    expanded = expanded_ref[r, lanes].astype(f32)
                    total = None
                    for a in range(3):
                        for b in range(3):
                            near = moved_ref[a, tile, 7 + b + start : 39 + b + start]
                            if b != 1:
                                near = near * (left_mask if b == 0 else right_mask)
                            tap = 8 - 3 * a - b
                            term = near * kernel[tap]
                            total = term if total is None else total + term
                            product = near * expanded
                            sums[tile][tap] = sums[tile][tap] + jnp.sum(product.reshape(4, 8, 128), axis=0)
                    grad_expanded_ref[r, lanes] = total.astype(bf16)
        send(block)
        if block == 0:
            for i in range(3, 7):
                wait(i)
            turned_ref[...] = token_ref[...].T
        grad_ref[0:width] = mm(turned_ref[...], grad_expanded_ref[...]).astype(bf16)
        depth = jnp.concatenate(
            [
                jnp.concatenate([jnp.sum(sums[tile][k], axis=0, keepdims=True) for k in range(9)], axis=0)
                for tile in range(tiles)
            ],
            axis=1,
        )
        high, rest = small_rows(gain_refs, width)
        grad_ref[width:] = jnp.concatenate([depth, high, rest, jnp.zeros((1, width), f32)], axis=0).astype(bf16)
        send(count + block)


def run_conv_backward(grad_projected, tokens, mover, side, gains, others, expanded, mixed, after=()):
    rows, width = grad_projected.shape
    count = len(others)
    loads = [0, 7, 7 + count, 1, 2, 7 + 2 * count, 3, 4, 5, 6]
    for block in range(1, count):
        loads += [7 + block, 7 + count + block, 7 + 2 * count + block]
    result = call_staged(
        functools.partial(conv_backward_kernel, count),
        "conv_backward",
        [grad_projected, mover, side, tokens, *gains, *others, *mixed, *expanded],
        [shaped((rows, width), bf16)] * count + [shaped((width + 16, width), bf16)] * count,
        [
            pltpu.VMEM((PACK, width), f32),
            pltpu.VMEM((PACK, width), bf16),
            pltpu.VMEM((3, width // 128, PACK + 16, 128), f32),
            pltpu.VMEM((width, rows), bf16),
        ],
        6 * count,
        after,
        order=loads,
    )
    return result[:count], result[count:]


def token_grad_kernel(ins, wait, outs, send):
    grad_one_ref, grad_refs, weight_refs = ins[0], ins[1:5], ins[5:9]
    (out_ref,) = outs
    rows = grad_one_ref.shape[0]
    for i in range(9):
        wait(i)
    weight = jnp.concatenate([w[...] for w in weight_refs], axis=1)
    for part in range(4):
        r = slice(part * rows // 4, (part + 1) * rows // 4)
        grad = jnp.concatenate([g[r] for g in grad_refs], axis=1)
        out_ref[r] = (grad_one_ref[r] + mm_t(grad, weight)).astype(bf16)
        send(0, part)


def run_token_grad(grad_one, grads, weights, after=()):
    (result,) = call_staged(
        token_grad_kernel, "token_grad", [grad_one, *grads, *weights], [shaped(grad_one.shape, bf16)], [], 4, after,
        out_parts={0: 4},
        megabytes=20,
    )
    return result


def run_join(index, mine, other, sizes, turns):
    rows, columns = mine.shape
    forms = {"plain": lambda s: (s, columns), "turned": lambda s: (columns, s), "slabs": lambda s: (columns // 128, s, 128)}
    shapes = [forms[turn](s) for s, turn in zip(sizes, turns)]
    return pl.pallas_call(
        functools.partial(join_kernel, turns),
        in_specs=[smem, vmem, vmem],
        out_specs=[vmem] * len(sizes),
        out_shape=[shaped(s, f32) for s in shapes],
        scratch_shapes=[pltpu.VMEM((2 * rows, columns), f32)],
        compiler_params=params(20),
        cost_estimate=cost(2),
        name="join_halves",
    )(index, mine, other)


def per_device(
    tokens, cotangent, shapes, head_mask, w_expand, w_depth, w_project, gain_conv, gain_attn, w_qkv, w_out,
    gain_mlp, w_up, w_down,
):
    rows, width = tokens.shape
    packs = rows // PACK
    channels = w_expand.shape[1]
    tensor_size = lax.axis_size("tensor")
    dp_size = lax.axis_size("dp")
    me_dp = lax.axis_index("dp")
    bits = [1 << b for b in range(dp_size.bit_length() - 1)]
    place = {bit: ((me_dp & bit) != 0).astype(jnp.int32) for bit in bits}

    def hold(x, after):
        return lax.optimization_barrier((x, after))[0]

    def swap_tensor(x, bit):
        return lax.ppermute(x, "tensor", [(i, i ^ bit) for i in range(tensor_size)])

    def swap_dp(x, bit):
        return lax.ppermute(x, "dp", [(i, i ^ bit) for i in range(dp_size)])

    def add(*parts):
        total = parts[0].astype(f32)
        for part in parts[1:]:
            total = total + part.astype(f32)
        return total.astype(bf16)

    def near_far(keep, pair):
        half = keep.shape[0] // 2
        return add(keep[:half], pair[:half]), add(keep[half:], pair[half:])

    def part(x, bit, mine):
        half = x.shape[0] // 2
        chosen = place[bit] if mine else 1 - place[bit]
        return lax.dynamic_slice_in_dim(x, chosen * half, half, 0)

    def halves(x, bit):
        return part(x, bit, True), swap_dp(part(x, bit, False), bit)

    def both(mine, other, bit):
        first = place[bit] == 0
        return jnp.concatenate([jnp.where(first, mine, other), jnp.where(first, other, mine)])

    def rest(x):
        for bit in bits[3:]:
            x = add(x, swap_dp(x, bit))
        return x

    other = jnp.concatenate(
        [
            w_project,
            w_depth,
            jnp.pad(head_mask.astype(bf16)[None, :], ((0, 6), (0, channels - head_mask.shape[0]))),
        ]
    )
    expand_w = [w_expand, swap_tensor(w_expand, 1)]
    other_w = [other, swap_tensor(other, 1)]
    far_expand, far_other = swap_tensor(w_expand, 2), swap_tensor(other, 2)
    mover, side, segment, segment_row = run_geometry(hold(shapes, other), packs)
    slabs, out_weight = hold((w_qkv, w_out), mover)
    slabs = slabs.transpose(1, 0, 2).reshape(-1, w_qkv.shape[2])
    slab_w = [slabs, swap_tensor(slabs, 1), swap_tensor(slabs, 2)]
    out_w = [out_weight, swap_tensor(out_weight, 1), swap_tensor(out_weight, 2)]

    exp_a, mix_a, act_a, (partial,) = run_conv_forward(tokens, mover, side, expand_w, other_w)
    far_expand, far_other = hold((far_expand, far_other), partial)
    expand_w += [far_expand, swap_tensor(far_expand, 1)]
    other_w += [far_other, swap_tensor(far_other, 1)]
    mlp = jnp.concatenate(hold([w_up, w_down], partial))
    mlp_w = [mlp, swap_tensor(mlp, 1), swap_tensor(mlp, 2)]
    exp_b, mix_b, act_b, (projected, residual_one, attn_low) = run_conv_forward(
        tokens, mover, side, expand_w[2:], other_w[2:], partial, (gain_conv, gain_attn)
    )
    slab_w[2], out_w[2] = hold((slab_w[2], out_w[2]), attn_low)
    slab_w.append(swap_tensor(slab_w[2], 1))
    out_w.append(swap_tensor(out_w[2], 1))
    flags = [(w, channels, 16) for w in other_w]
    qkv, exps, inverse, merged, residual_two, mlp_low = run_attention_forward(
        attn_low, residual_one, segment, segment_row, gain_mlp, slab_w, out_w, flags
    )
    mlp_w[2] = hold(mlp_w[2], mlp_low)
    mlp_w.append(swap_tensor(mlp_w[2], 1))
    (out_tokens, grad_two, gain_m), (mlp_keep, mlp_mate) = run_mlp(mlp_low, cotangent, residual_two, gain_mlp, mlp_w)
    mlp_pair = swap_tensor(mlp_mate, 1)

    grad_proj, grad_out = run_attention_core_back(grad_two, qkv, exps, inverse, merged, out_w, flags)
    mlp_near, mlp_far = near_far(mlp_keep, hold(mlp_pair, grad_proj))
    mlp_cross = swap_tensor(mlp_far, 2)
    grad_one, grad_projected, gain_a, gain_c, attn_keep, attn_mate = run_attention_rest_back(
        attn_low, grad_proj, grad_two, residual_one, projected, grad_out, gain_attn, gain_conv, slab_w,
        [*act_a, *act_b], (mlp_near, mlp_far),
    )
    gains = (gain_c, gain_a, gain_m)
    mlp_cross = hold(mlp_cross, grad_one)
    attn_pair = swap_tensor(hold(attn_mate, mlp_cross), 1)
    mlp_half, mlp_other = halves(add(mlp_near, mlp_cross), 1)
    attn_near, attn_far = near_far(attn_keep, hold(attn_pair, mlp_half))
    attn_cross = swap_tensor(attn_far, 2)

    grads_b, (conv_2, conv_3) = run_conv_backward(
        grad_projected, tokens, mover, side, gains, other_w[2:], exp_b, mix_b, (mlp_half, attn_near, attn_far)
    )
    conv_pair_3 = swap_tensor(conv_3, 1)
    mlp_half, mlp_other = halves(add(mlp_half, hold(mlp_other, conv_3)), 2)
    conv_far = add(conv_2, hold(conv_pair_3, mlp_half))
    conv_cross = swap_tensor(conv_far, 2)
    attn_half, attn_other = halves(add(attn_near, hold(attn_cross, conv_far)), 1)

    grads_a, (conv_0, conv_1) = run_conv_backward(
        grad_projected, tokens, mover, side, gains, other_w[:2], exp_a, mix_a, (mlp_half, conv_far, attn_half)
    )
    conv_pair_1 = swap_tensor(conv_1, 1)
    attn_half, attn_other = halves(add(attn_half, hold(attn_other, conv_1)), 2)
    conv_near = add(conv_0, hold(conv_pair_1, attn_half), hold(conv_cross, attn_half))
    small = conv_near[width:]
    main = conv_near[:width]
    tail = jnp.concatenate([part(main, 1, True), small])
    tail_other = swap_dp(jnp.concatenate([part(main, 1, False), small]), 1)
    mlp_half = add(mlp_half, hold(mlp_other, tail))
    mlp_other = swap_dp(mlp_half, 4)
    grad_tokens = run_token_grad(grad_one, [*grads_a, *grads_b], expand_w, (tail, mlp_half, attn_half))
    half = width // 2
    attn_half = add(attn_half, hold(attn_other, grad_tokens))
    attn_other = swap_dp(attn_half, 4)
    tail = add(tail, hold(tail_other, attn_half))
    main, small = tail[:half], tail[half:]
    tail_other = swap_dp(jnp.concatenate([part(main, 2, False), small]), 2)
    tail = jnp.concatenate([part(main, 2, True), small])
    mlp_half = rest(add(mlp_half, hold(mlp_other, tail)))
    mlp_other = swap_dp(mlp_half, 2)
    tail = add(tail, hold(tail_other, mlp_half))
    tail_other = swap_dp(tail, 4)
    attn_half = rest(add(attn_half, hold(attn_other, tail)))
    attn_other = swap_dp(attn_half, 2)
    mlp_half = both(mlp_half, hold(mlp_other, attn_half), 2)
    mlp_other = swap_dp(mlp_half, 1)
    tail = rest(add(tail, hold(tail_other, mlp_half)))
    half = half // 2
    main, small = tail[:half], tail[half:].astype(f32)
    main_other = swap_dp(main, 2)
    attn_half = both(attn_half, hold(attn_other, main), 2)
    attn_other = swap_dp(attn_half, 1)
    main = both(main, hold(main_other, attn_half), 2)
    main_other = swap_dp(main, 1)
    index = place[1][None]
    grad_up, grad_down = run_join(index, mlp_half, mlp_other, (width, width), ("plain", "turned"))
    grad_qkv, grad_out, grad_project = run_join(
        index, attn_half, attn_other, (width, w_out.shape[0], width), ("slabs", "plain", "turned")
    )
    (grad_expand,) = run_join(index, main, main_other, (width,), ("plain",))
    gain_sums = small[9:12] + small[12:15]
    return (
        out_tokens, grad_tokens, grad_expand, small[:9], grad_project, gain_sums[0], gain_sums[1],
        grad_qkv.transpose(1, 0, 2), grad_out, gain_sums[2], grad_up, grad_down,
    )


def solution(mesh):
    rows = P(("dp", "tensor"), None)
    cols = P(None, "tensor")
    down = P("tensor", None)
    return jax.shard_map(
        per_device,
        mesh=mesh,
        in_specs=(
            rows, rows, P("dp", None, None), P("tensor"), cols, cols, down, P(), P(), P(None, None, "tensor"), down,
            P(), cols, down,
        ),
        out_specs=(rows, rows, cols, cols, down, P(), P(), P(None, None, "tensor"), down, P(), cols, down),
        check_vma=False,
    )
```

```python
import functools
import jax
import jax.numpy as jnp
from jax import lax
from jax.experimental import pallas as pl
from jax.experimental.pallas import tpu as pltpu
from jax.sharding import PartitionSpec as P

HSZ = 64
PACK = 512
SPAN = 256
SPLIT = (0, 240, 480, 512)
UP_FROM = (0, 224, 256)
DOWN_FROM = (0, 240, 256)

epsilon = 1e-05
f32 = jnp.float32
bf16 = jnp.bfloat16


def mm(a, b):
    return jnp.dot(a, b, preferred_element_type=f32)


def mm_t(a, b):
    return lax.dot_general(a, b, (((1,), (1,)), ((), ())), preferred_element_type=f32)


def t_mm(a, b):
    return lax.dot_general(a, b, (((0,), (0,)), ((), ())), preferred_element_type=f32)


def standard(values):
    centred = values - jnp.mean(values, axis=-1, keepdims=True)
    inverse = lax.rsqrt(jnp.mean(centred * centred, axis=-1, keepdims=True) + epsilon)
    return centred * inverse, inverse


def standard_back(grad, unit, inverse):
    mean_grad = jnp.mean(grad, axis=-1, keepdims=True)
    mean_both = jnp.mean(grad * unit, axis=-1, keepdims=True)
    return (grad - mean_grad - unit * mean_both) * inverse


def geometry(pack, packs, shape_ref, mover_ref, side_ref, segment_ref, segment_row_ref, slot_ref):
    own = lax.axis_index("tensor") * packs + pack
    rows = slice(pack * PACK, (pack + 1) * PACK)
    slot_ref[...] = jnp.zeros_like(slot_ref)
    slot_ref[0:2, 0 : shape_ref.shape[2]] = shape_ref[own].astype(f32)
    sides = slot_ref[...]
    height_slots = sides[0:1]
    width_slots = sides[1:2]
    sizes = jnp.broadcast_to(height_slots * width_slots, (8, 128))
    before = lax.broadcasted_iota(jnp.int32, (128, 128), 0)
    after = lax.broadcasted_iota(jnp.int32, (128, 128), 1)
    ends = mm(sizes.astype(bf16), (before <= after).astype(bf16))[0:1]
    starts = ends - height_slots * width_slots
    places = lax.broadcasted_iota(jnp.int32, (PACK, 128), 0).astype(f32)
    here = ((starts <= places) & (places < ends)).astype(f32)
    image_start = jnp.sum(here * starts, axis=1, keepdims=True)
    height = jnp.sum(here * height_slots, axis=1, keepdims=True)
    width = jnp.sum(here * width_slots, axis=1, keepdims=True)
    place = places[:, 0:1]
    offset = place - image_start
    safe = jnp.maximum(width, 1.0)
    grid_row = jnp.floor((offset + 0.5) / safe)
    grid_col = offset - grid_row * safe
    above = jnp.where(grid_row >= 1.0, place - width, -1.0)
    below = jnp.where(grid_row + 1.0 < height, place + width, -1.0)
    lanes = lax.broadcasted_iota(jnp.int32, (1, SPAN), 1).astype(f32)
    for part in range(3):
        low, high = SPLIT[part], SPLIT[part + 1]
        for which, (target, origin) in enumerate(((above, UP_FROM[part]), (below, DOWN_FROM[part]))):
            hit = (target[low:high] == lanes + origin).astype(f32).astype(bf16)
            mover_ref[(2 * pack + which) * PACK + low : (2 * pack + which) * PACK + high] = hit
    side_ref[rows, 0:128] = jnp.broadcast_to((grid_col >= 1.0).astype(f32), (PACK, 128))
    side_ref[rows, 128:256] = jnp.broadcast_to((grid_col + 1.0 < width).astype(f32), (PACK, 128))
    segment = jnp.broadcast_to(image_start, (PACK, 128))
    segment_ref[rows] = segment
    segment_row_ref[pack] = segment.T[0:8]


def gelu_parts(values):
    cdf = 0.5 + 0.5 * lax.erf(values * 0.7071067811865476)
    bell = jnp.exp2(values * values * (-0.5 * 1.4426950408889634))
    return values * cdf, cdf + values * bell * 0.3989422804014327


def mlp_kernel(ins, wait, outs, send, act_ref, pre_ref, down_ref, up_ref, turned_ref, *buffers):
    mlp_ref, cotangent_ref, residual_ref, gain_ref = ins[:4]
    weight_refs = ins[4:]
    out_ref, grad_two_ref, gain_grad_ref = outs[:3]
    grad_refs = outs[3:]
    rows, width = mlp_ref.shape
    size = 256
    chunks = rows // size
    wait(0)
    turned_ref[0] = mlp_ref[...].T
    wait(1)
    turned_ref[1] = cotangent_ref[...].T

    def arrange(half, blocks):
        for side, block in enumerate(blocks):
            wait(4 + block)
            lanes = slice(side * width, (side + 1) * width)
            down_ref[half, lanes] = weight_refs[block][width:]
            up_ref[half, :, lanes] = weight_refs[block][0:width]

    arrange(0, (1, 3))
    arrange(1, (0, 2))

    def products(j, buffer):
        half = j // chunks
        r = pl.ds((j % chunks) * size, size)
        buffer[0] = mm(mlp_ref[r], up_ref[half])
        buffer[1] = mm_t(cotangent_ref[r], down_ref[half])

    def gates(j, buffer):
        half = j // chunks
        r = pl.ds((j % chunks) * size, size)
        act, slope = gelu_parts(buffer[0])
        act_ref[half, r] = act.astype(bf16)
        pre_ref[half, r] = (buffer[1] * slope).astype(bf16)

    products(0, buffers[0])

    def one(k, carry):
        products(2 * k + 1, buffers[1])
        gates(2 * k, buffers[0])
        products(jnp.minimum(2 * k + 2, 2 * chunks - 1), buffers[0])
        gates(2 * k + 1, buffers[1])
        return carry

    lax.fori_loop(0, chunks, one, 0)
    for half, blocks in enumerate(((1, 3), (0, 2))):
        grad_up = mm(turned_ref[0], pre_ref[half]).astype(bf16)
        grad_down = mm(turned_ref[1], act_ref[half]).astype(bf16)
        for place, block in enumerate(blocks):
            lanes = slice(place * width, (place + 1) * width)
            grad_refs[block][0:width] = grad_up[:, lanes]
            grad_refs[block][width:] = grad_down[:, lanes]
            send(3 + block)
    wait(2)
    wait(3)
    gain_grad_ref[...] = jnp.zeros_like(gain_grad_ref)

    def finish(c, carry):
        r = pl.ds(c * size, size)
        grad_in = mm_t(pre_ref[0, r], up_ref[0]) + mm_t(pre_ref[1, r], up_ref[1])
        residual = residual_ref[r]
        out = residual + (mm(act_ref[0, r], down_ref[0]) + mm(act_ref[1, r], down_ref[1]))
        out_ref[r] = out.astype(bf16)
        send(0, c)
        unit, inverse = standard(residual)
        gain_grad_ref[...] += jnp.sum((grad_in * unit).reshape(size // 8, 8, width), axis=0)
        grad_two_ref[r] = cotangent_ref[r].astype(f32) + standard_back(grad_in * gain_ref[...], unit, inverse)
        send(1, c)
        return carry

    lax.fori_loop(0, chunks, finish, 0)
    send(2)


def run_mlp(mlp, cotangent, residual, gain, weights):
    rows, width = mlp.shape
    channels = weights[0].shape[1]
    grads = shaped((2 * width, channels), bf16)
    wide = 2 * channels
    result = call_staged(
        mlp_kernel,
        "mlp_both",
        [mlp, cotangent, residual, gain, *weights],
        [shaped((rows, width), bf16), shaped((rows, width), f32), shaped((8, width), f32), *[grads] * 4],
        [
            pltpu.VMEM((2, rows, wide), bf16),
            pltpu.VMEM((2, rows, wide), bf16),
            pltpu.VMEM((2, wide, width), bf16),
            pltpu.VMEM((2, width, wide), bf16),
            pltpu.VMEM((2, width, rows), bf16),
            pltpu.VMEM((2, 256, wide), f32),
            pltpu.VMEM((2, 256, wide), f32),
        ],
        16,
        out_parts={0: rows // 256, 1: rows // 256},
        order=(0, 5, 7, 1, 4, 6, 2, 3),
    )
    return result[:3], result[3:]


HEADS_ON = 6


def list_heads(flag_refs, list_ref):
    count = jnp.int32(0)
    for head in range(2 * len(flag_refs)):
        on = flag(flag_refs[head // 2], head % 2)

        @pl.when(on)
        def _(count=count, head=head):
            list_ref[count] = jnp.int32(head)

        count = count + on.astype(jnp.int32)


def flag(flag_ref, side):
    return jnp.max(flag_ref[9:10, side : side + 1].astype(f32)) != 0


def lane_joined(weight_ref):
    rows = weight_ref.shape[0] // 3
    return jnp.concatenate([weight_ref[j * rows : (j + 1) * rows] for j in range(3)], axis=1)


def attention_forward_kernel(ins, wait, outs, send, list_ref, wide_ref):
    attn_ref, segment_ref, segment_row_ref, residual_ref, gain_ref = ins[:5]
    slab_refs, out_weight_refs, flag_refs = ins[5:9], ins[9:13], ins[13:17]
    qkv_ref, exps_ref, inverse_ref, merged_ref, residual_two_ref, mlp_ref = outs
    rows, width = attn_ref.shape
    for i in range(13, 17):
        wait(i)
    list_heads(flag_refs, list_ref)
    merged_ref[...] = jnp.zeros_like(merged_ref)
    inverse_ref[...] = jnp.zeros_like(inverse_ref)
    wait(5)
    wait(6)
    wait(0)
    for half in range(2):
        if half:
            wait(7)
            wait(8)
        for side in range(2):
            wide_ref[half, :, side * width : (side + 1) * width] = lane_joined(slab_refs[2 * half + side])
        projections = mm(attn_ref[...], wide_ref[half]).astype(bf16)
        for side in range(2):
            qkv_ref[2 * half + side] = projections[:, side * width : (side + 1) * width]
            send(0, 2 * half + side)
    wait(1)
    wait(2)
    lane = lax.broadcasted_iota(jnp.int32, (1, 128), 1)

    def one(i, carry):
        head = list_ref[i]
        pair = head // 2
        mine = (lane // HSZ) == (head % 2)
        scale = jnp.where(mine, HSZ**-0.5, 0.0).astype(bf16)
        for pack in range(rows // PACK):
            part = slice(pack * PACK, (pack + 1) * PACK)
            keys = qkv_ref[pair, part, 128:256]
            values = jnp.concatenate([qkv_ref[pair, part, 256:384], jnp.ones((PACK, 128), bf16)], axis=1)
            segment_row = segment_row_ref[pack, 0:1]
            for block in range(0, PACK, 256):
                r = slice(pack * PACK + block, pack * PACK + block + 256)
                scores = mm_t(qkv_ref[pair, r, 0:128] * scale, keys)
                segment = jnp.concatenate([segment_ref[r]] * (PACK // 128), axis=1)
                scores = jnp.where(segment == segment_row, scores, -1e30)
                exps = jnp.exp(scores - jnp.max(scores, axis=1, keepdims=True)).astype(bf16)
                exps_ref[i, r] = exps
                out = mm(exps, values)
                inverse = 1.0 / out[:, 128:256]
                merged_ref[pair, r] = jnp.where(mine, out[:, 0:128] * inverse, merged_ref[pair, r].astype(f32)).astype(bf16)
                inverse_ref[r] = jnp.where(lane == i, inverse, inverse_ref[r])
        send(1, i)
        return carry

    lax.fori_loop(0, HEADS_ON, one, 0, unroll=2)
    send(2)
    send(3)
    wait(3)
    wait(4)
    for pair in range(4):
        wait(9 + pair)
    out_weight = jnp.concatenate([w[...] for w in out_weight_refs], axis=0)
    for part in range(4):
        r = slice(part * rows // 4, (part + 1) * rows // 4)
        merged = jnp.concatenate([merged_ref[pair, r] for pair in range(4)], axis=1)
        total = residual_ref[r] + mm(merged, out_weight)
        residual_two_ref[r] = total
        send(4, part)
        unit, _ = standard(total)
        mlp_ref[r] = (unit * gain_ref[...]).astype(bf16)
        send(5, part)


def run_attention_forward(attn, residual, segment, segment_row, gain, slabs, out_weights, flags):
    rows, width = attn.shape
    outs = [
        shaped((4, rows, 384), bf16),
        shaped((HEADS_ON, rows, PACK), bf16),
        shaped((rows, 128), f32),
        shaped((4, rows, 128), bf16),
        shaped((rows, width), f32),
        shaped((rows, width), bf16),
    ]
    return call_staged(
        attention_forward_kernel,
        "attention_forward",
        [attn, segment, segment_row, residual, gain, *slabs, *out_weights, *flags],
        outs,
        [pltpu.SMEM((8,), jnp.int32), pltpu.VMEM((2, width, 768), bf16)],
        14,
        out_parts={0: 4, 1: HEADS_ON, 4: 4, 5: 4},
        order=(13, 14, 15, 16, 5, 6, 0, 7, 8, 1, 2, 9, 10, 11, 12, 4, 3),
    )


def attention_back_kernel(
    ins, wait, outs, send, list_ref, merged_grad_ref, score_ref, wide_ref, pair_ref, merged_wide_ref
):
    grad_two_ref, qkv_ref, exps_ref, inverse_ref, merged_ref = ins[:5]
    out_weight_refs, flag_refs = ins[5:9], ins[9:13]
    attn_ref, residual_ref, projected_ref, gain_attn_ref, gain_conv_ref = ins[13:18]
    slab_refs, acted_refs = ins[18:22], ins[22:26]
    grad_one_ref, grad_projected_ref, gain_attn_grad_ref, gain_conv_grad_ref = outs[:4]
    grad_refs = outs[4:]
    rows, width = grad_two_ref.shape
    for i in range(9, 13):
        wait(i)
    list_heads(flag_refs, list_ref)
    pair_ref[...] = jnp.zeros_like(pair_ref)
    gain_attn_grad_ref[...] = jnp.zeros_like(gain_attn_grad_ref)
    gain_conv_grad_ref[...] = jnp.zeros_like(gain_conv_grad_ref)
    wait(0)
    low = grad_two_ref[...].astype(bf16)
    for i in range(5, 9):
        wait(i)
    out_weight = jnp.concatenate([w[...] for w in out_weight_refs], axis=0)
    grad_merged = mm_t(low, out_weight).astype(bf16)
    for pair in range(4):
        merged_grad_ref[pair] = grad_merged[:, pair * 128 : pair * 128 + 128]
    wait(4)
    for pair in range(4):
        merged_wide_ref[:, pair * 128 : pair * 128 + 128] = merged_ref[pair]
    grad_out = t_mm(merged_wide_ref[...], low).astype(bf16)
    for pair in range(4):
        grad_refs[pair][width : width + 128] = grad_out[pair * 128 : pair * 128 + 128]
    wait(1)
    wait(3)
    lane = lax.broadcasted_iota(jnp.int32, (1, 128), 1)

    def one(i, carry):
        head = list_ref[i]
        pair = head // 2
        half = head // 4
        mine = (lane // HSZ) == (head % 2)
        wait(2, i)
        for pack in range(rows // PACK):
            part = slice(pack * PACK, (pack + 1) * PACK)
            inverse = jnp.sum(jnp.where(lane == i, inverse_ref[part], 0.0), axis=1, keepdims=True)
            grad_heads = jnp.where(mine, merged_grad_ref[pair, part].astype(f32) * inverse, 0.0).astype(bf16)
            delta = jnp.sum(grad_heads.astype(f32) * merged_ref[pair, part].astype(f32), axis=1, keepdims=True)
            values = qkv_ref[pair, part, 256:384]
            for block in range(0, PACK, 256):
                r = slice(pack * PACK + block, pack * PACK + block + 256)
                b = slice(block, block + 256)
                grad_probs = mm_t(grad_heads[b], values)
                score_ref[pack, b] = (exps_ref[i, r].astype(f32) * (grad_probs - delta[b])).astype(bf16)
            grad_scores = score_ref[pack]
            grad_q = mm(grad_scores, qkv_ref[pair, part, 128:256]) * HSZ**-0.5
            grad_k = t_mm(grad_scores, qkv_ref[pair, part, 0:128]) * HSZ**-0.5
            grad_v = t_mm(exps_ref[i, part], grad_heads)
            for j, grad in enumerate((grad_q, grad_k, grad_v)):
                lanes = pl.ds(pl.multiple_of((pair % 2) * width + j * 128, 128), 128)
                pair_ref[half, part, lanes] = jnp.where(
                    mine, grad, pair_ref[half, part, lanes].astype(f32)
                ).astype(bf16)
        return carry

    lax.fori_loop(0, HEADS_ON, one, 0)
    for i in range(18, 22):
        wait(i)
    for half in range(2):
        for side in range(2):
            wide_ref[half, :, side * width : (side + 1) * width] = lane_joined(slab_refs[2 * half + side])
    for i in range(13, 18):
        wait(i)
    attn_t = attn_ref[...].T
    size = rows // 4
    for part in range(4):
        if part % 2:
            half = part // 2
            grad_qkv = mm(attn_t, pair_ref[half]).astype(bf16)
            for side in range(2):
                grad_refs[2 * half + side][0:width] = grad_qkv[:, side * width : (side + 1) * width]
        r = slice(part * size, (part + 1) * size)
        grad_in = mm_t(pair_ref[0, r], wide_ref[0]) + mm_t(pair_ref[1, r], wide_ref[1])
        unit, inverse = standard(residual_ref[r])
        gain_attn_grad_ref[...] += jnp.sum((grad_in * unit).reshape(size // 8, 8, width), axis=0)
        grad_one = grad_two_ref[r] + standard_back(grad_in * gain_attn_ref[...], unit, inverse)
        grad_one_ref[r] = grad_one
        unit, inverse = standard(projected_ref[r])
        gain_conv_grad_ref[...] += jnp.sum((grad_one * unit).reshape(size // 8, 8, width), axis=0)
        grad_projected_ref[r] = standard_back(grad_one * gain_conv_ref[...], unit, inverse).astype(bf16)
    for i in range(4):
        send(i)
    for i in range(22, 26):
        wait(i)
    projected_t = grad_projected_ref[...].T
    for half in (1, 0):
        acted = jnp.concatenate([acted_refs[2 * half][...], acted_refs[2 * half + 1][...]], axis=1)
        grad_project = mm(projected_t, acted).astype(bf16)
        for side in range(2):
            grad_refs[2 * half + side][width + 128 :] = grad_project[:, side * width : (side + 1) * width]
            send(4 + 2 * half + side)


def run_attention_back(
    grad_two, qkv, exps, inverse, merged, out_weights, flags, attn, residual, projected, gain_attn, gain_conv, slabs,
    acted, after=(),
):
    rows, width = grad_two.shape
    grads = shaped((2 * width + 128, 384), bf16)
    return call_staged(
        attention_back_kernel,
        "attention_back",
        [
            grad_two, qkv, exps, inverse, merged, *out_weights, *flags, attn, residual, projected, gain_attn, gain_conv,
            *slabs, *acted,
        ],
        [shaped((rows, width), f32), shaped((rows, width), bf16), *[shaped((8, width), f32)] * 2, *[grads] * 4],
        [
            pltpu.SMEM((8,), jnp.int32),
            pltpu.VMEM((4, rows, 128), bf16),
            pltpu.VMEM((rows // PACK, PACK, PACK), bf16),
            pltpu.VMEM((2, width, 2 * width), bf16),
            pltpu.VMEM((2, rows, 2 * width), bf16),
            pltpu.VMEM((rows, 512), bf16),
        ],
        24,
        after,
        in_parts={2: HEADS_ON},
        order=(9, 10, 11, 12, 5, 6, 7, 8, 0, 4, 3, 1, 2, *range(18, 22), *range(13, 18), *range(22, 26)),
    )


def small_rows(gain_refs, width):
    gains = jnp.concatenate([jnp.sum(ref[...], axis=0, keepdims=True) for ref in gain_refs], axis=0)
    high = gains.astype(bf16).astype(f32)
    return high, gains - high


def join_kernel(turns, index_ref, mine_ref, other_ref, *refs):
    out_refs = refs[:-1]
    whole_ref = refs[-1]
    first = index_ref[0] == 0
    rows = mine_ref.shape[0]
    mine = mine_ref[...].astype(f32)
    other = other_ref[...].astype(f32)
    whole_ref[0:rows] = jnp.where(first, mine, other)
    whole_ref[rows:] = jnp.where(first, other, mine)
    start = 0
    for out_ref, turn in zip(out_refs, turns):
        if turn == "slabs":
            rows = out_ref.shape[1]
            for j in range(out_ref.shape[0]):
                out_ref[j] = whole_ref[start : start + rows, j * 128 : j * 128 + 128]
        elif turn == "turned":
            rows = out_ref.shape[1]
            out_ref[...] = whole_ref[start : start + rows].T
        else:
            rows = out_ref.shape[0]
            out_ref[...] = whole_ref[start : start + rows]
        start += rows


def whole(shape):
    zeros = (0,) * len(shape)
    return pl.BlockSpec(shape, lambda p: zeros)


def params(megabytes=56):
    return pltpu.CompilerParams(vmem_limit_bytes=megabytes << 20)


def cost(microseconds):
    return pl.CostEstimate(
        flops=int(microseconds * 1.1e9), bytes_accessed=int(microseconds * 3.0e6), transcendentals=0
    )


smem = pl.BlockSpec(memory_space=pltpu.SMEM)


def shaped(shape, dtype):
    return jax.ShapeDtypeStruct(shape, dtype)


vmem = pl.BlockSpec(memory_space=pltpu.VMEM)
anywhere = pl.BlockSpec(memory_space=pl.ANY)


def call_staged(
    kernel, name, ins, outs, scratch, microseconds, after=(), in_parts=None, out_parts=None, order=None,
    megabytes=56,
):
    in_parts, out_parts = in_parts or {}, out_parts or {}
    n, m, skip = len(ins), len(outs), len(after)
    windows = {i: x[1:] for i, x in enumerate(ins) if isinstance(x, tuple)}
    ins = [x[0] if isinstance(x, tuple) else x for x in ins]
    sizes = [(windows[i][1], *x.shape[1:]) if i in windows else x.shape for i, x in enumerate(ins)]

    def body(*refs):
        in_hbm, refs = refs[:n], refs[n + skip :]
        out_hbm, refs = refs[:m], refs[m:]
        in_vmem, refs = refs[:n], refs[n:]
        out_vmem, refs = refs[:m], refs[m:]
        in_sems, refs = refs[:n], refs[n:]
        out_sems, refs = refs[:m], refs[m:]

        def copy(source, target, sem, parts, which):
            if parts == 1:
                return pltpu.make_async_copy(source, target, sem.at[0])
            size = source.shape[0] // parts
            rows = pl.ds(which * size, size)
            return pltpu.make_async_copy(source.at[rows], target.at[rows], sem.at[which])

        def load(i, which=0):
            source = in_hbm[i].at[pl.ds(*windows[i])] if i in windows else in_hbm[i]
            return copy(source, in_vmem[i], in_sems[i], in_parts.get(i, 1), which)

        def store(i, which=0):
            return copy(out_vmem[i], out_hbm[i], out_sems[i], out_parts.get(i, 1), which)

        for i in order or range(n):
            for which in range(in_parts.get(i, 1)):
                load(i, which).start()
        kernel(
            in_vmem, lambda i, which=0: load(i, which).wait(), out_vmem, lambda i, which=0: store(i, which).start(), *refs
        )
        for i in range(m):
            for which in range(out_parts.get(i, 1)):
                store(i, which).wait()

    return pl.pallas_call(
        body,
        in_specs=[anywhere] * (n + skip),
        out_specs=[anywhere] * m,
        out_shape=list(outs),
        scratch_shapes=[pltpu.VMEM(size, x.dtype) for size, x in zip(sizes, ins)]
        + [pltpu.VMEM(x.shape, x.dtype) for x in outs]
        + [pltpu.SemaphoreType.DMA((in_parts.get(i, 1),)) for i in range(n)]
        + [pltpu.SemaphoreType.DMA((out_parts.get(i, 1),)) for i in range(m)]
        + list(scratch),
        compiler_params=params(megabytes),
        cost_estimate=cost(microseconds),
        name=name,
    )(*ins, *after)


def conv_forward_kernel(
    count, first, has_partial, final, ins, wait, outs, send, raw_ref, up_ref, mid_ref, down_ref, slot_ref
):
    token_ref, mover_ref, side_ref = ins[:3]
    weight_refs, project_refs, small_refs = (ins[3 + j * count : 3 + (j + 1) * count] for j in range(3))
    extra = ins[3 + 3 * count :]
    expanded_refs, mixed_refs, acted_refs = outs[:count], outs[count : 2 * count], outs[2 * count : 3 * count]
    rows, width = token_ref.shape
    wide = count * width
    wait(0)
    for i in range(3, 3 + count):
        wait(i)
    weight = jnp.concatenate([w[...] for w in weight_refs], axis=1)
    for i in range(3 + count, 3 + 3 * count):
        wait(i)
    raw_ref[:, 0:8] = jnp.zeros((wide // 128, 8, 128), f32)
    raw_ref[:, 8 + PACK :] = jnp.zeros((wide // 128, 8, 128), f32)
    taps = jnp.concatenate([w[...] for w in small_refs], axis=1).astype(f32)
    project = jnp.concatenate([w[...] for w in project_refs], axis=0)
    total_ref = outs[3 * count]
    if first:
        shape_ref = mover_ref
        mover_ref, side_ref, segment_ref, segment_row_ref = outs[3 * count + 1 :]
        wait(1)
        wait(2)
        for pack in range(rows // PACK):
            geometry(pack, rows // PACK, shape_ref, mover_ref, side_ref, segment_ref, segment_row_ref, slot_ref)
        for i in range(3 * count + 1, 3 * count + 5):
            send(i)
    for pack in range(rows // PACK):
        base = pack * PACK
        expanded = mm(token_ref[base : base + PACK], weight)
        for tile in range(wide // 128):
            values = expanded[:, tile * 128 : tile * 128 + 128]
            raw_ref[tile, 8 : 8 + PACK] = values
            lanes = slice(tile % 3 * 128, tile % 3 * 128 + 128)
            expanded_refs[tile // 3][base : base + PACK, lanes] = values.astype(bf16)
        if pack == 0 and not first:
            wait(2)
        for tile in range(wide // 128):
            lanes = slice(tile * 128, tile * 128 + 128)
            kernel = [taps[k : k + 1, lanes] for k in range(9)]
            for start in range(0, PACK, 32):
                left = raw_ref[tile, 7 + start : 39 + start] * side_ref[base + start : base + start + 32, 0:128]
                mid = raw_ref[tile, 8 + start : 40 + start]
                right = raw_ref[tile, 9 + start : 41 + start] * side_ref[base + start : base + start + 32, 128:256]
                line = [left * kernel[3 * a] + mid * kernel[3 * a + 1] + right * kernel[3 * a + 2] for a in range(3)]
                up_ref[start : start + 32, lanes] = line[0].astype(bf16)
                mid_ref[start : start + 32, lanes] = line[1]
                down_ref[start : start + 32, lanes] = line[2].astype(bf16)
        if pack == 0 and not first:
            wait(1)
        for part in range(3):
            low, high = SPLIT[part], SPLIT[part + 1]
            hit = jnp.concatenate(
                [mover_ref[(2 * pack + which) * PACK + low : (2 * pack + which) * PACK + high] for which in range(2)], axis=1
            )
            source = jnp.concatenate(
                [
                    up_ref[UP_FROM[part] : UP_FROM[part] + SPAN],
                    down_ref[DOWN_FROM[part] : DOWN_FROM[part] + SPAN],
                ],
                axis=0,
            )
            mixed = mm(hit, source) + mid_ref[low:high]
            r = slice(base + low, base + high)
            acted = (mixed * jax.nn.sigmoid(mixed)).astype(bf16)
            mixed = mixed.astype(bf16)
            for block in range(count):
                lanes = slice(block * width, block * width + width)
                mixed_refs[block][r] = mixed[:, lanes]
                acted_refs[block][r] = acted[:, lanes]
        for i in range(3 * count):
            send(i, pack)
    for i in range(3 + 3 * count, len(ins)):
        wait(i)
    for part in range(4):
        r = slice(part * rows // 4, (part + 1) * rows // 4)
        total = mm(jnp.concatenate([a[r] for a in acted_refs], axis=1), project)
        if has_partial:
            total = total + extra[0][r]
        total_ref[r] = total
        send(3 * count, part)
        if final:
            residual_ref, attn_ref = outs[3 * count + 1 :]
            gain_conv_ref, gain_attn_ref = extra[1:]
            unit, _ = standard(total)
            residual = token_ref[r].astype(f32) + unit * gain_conv_ref[...]
            residual_ref[r] = residual
            send(3 * count + 1, part)
            unit, _ = standard(residual)
            attn_ref[r] = (unit * gain_attn_ref[...]).astype(bf16)
            send(3 * count + 2, part)


def run_conv_forward(tokens, mover, side, weights, projects, smalls, partial=None, gains=(), first=False):
    rows, width = tokens.shape
    count = len(weights)
    final = len(gains) > 0
    has_partial = partial is not None
    wide = count * width
    outs = [shaped((rows, width), bf16)] * (3 * count) + [shaped((rows, width), f32)]
    if final:
        outs += [shaped((rows, width), f32), shaped((rows, width), bf16)]
    out_parts = {i: rows // PACK if i < 3 * count else 4 for i in range(len(outs))}
    if first:
        packs = rows // PACK
        outs += [shaped((2 * rows, SPAN), bf16), shaped((rows, 256), f32), shaped((rows, 128), f32)]
        outs += [shaped((packs, 8, PACK), f32)]
    result = call_staged(
        functools.partial(conv_forward_kernel, count, first, has_partial, final),
        "conv_forward",
        [tokens, mover, side, *weights, *projects, *smalls, *([partial] if has_partial else []), *gains],
        outs,
        [
            pltpu.VMEM((wide // 128, PACK + 16, 128), f32),
            pltpu.VMEM((PACK, wide), bf16),
            pltpu.VMEM((PACK, wide), f32),
            pltpu.VMEM((PACK, wide), bf16),
            pltpu.VMEM((8, 128), f32),
        ],
        4 * count,
        out_parts=out_parts,
        order=(*((1,) if first else ()), 0, *range(3, 3 + 3 * count), 2, *(() if first else (1,)), *range(3 + 3 * count, 3 + 3 * count + has_partial + len(gains))),
    )
    return result[:count], result[count : 2 * count], result[2 * count : 3 * count], result[3 * count :]


def conv_backward_kernel(count, ins, wait, outs, send, acted_ref, low_ref, moved_ref, turned_ref):
    grad_projected_ref, mover_ref, side_ref, token_ref = ins[:4]
    gain_refs = ins[4:7]
    project_refs, mixed_refs, expanded_refs, small_refs = (ins[7 + j * count : 7 + (j + 1) * count] for j in range(4))
    grad_expanded_refs, grad_refs = outs[:count], outs[count:]
    rows, width = grad_projected_ref.shape
    tiles = width // 128
    moved_ref[:, :, 0:8] = jnp.zeros((3, tiles, 8, 128), f32)
    moved_ref[:, :, 8 + PACK :] = jnp.zeros((3, tiles, 8, 128), f32)
    wait(0)
    for block in range(count):
        mixed_ref, expanded_ref = mixed_refs[block], expanded_refs[block]
        grad_expanded_ref, grad_ref = grad_expanded_refs[block], grad_refs[block]
        wait(7 + block)
        wait(7 + 3 * count + block)
        project = project_refs[block][...]
        taps = small_refs[block][...].astype(f32)
        sums = [[jnp.zeros((8, 128), f32) for _ in range(9)] for _ in range(tiles)]
        for pack in range(rows // PACK):
            base = pack * PACK
            acted_ref[...] = mm_t(grad_projected_ref[base : base + PACK], project)
            if pack == 0:
                wait(7 + count + block)
            for tile in range(tiles):
                lanes = slice(tile * 128, tile * 128 + 128)
                for start in range(0, PACK, 64):
                    mixed = mixed_ref[base + start : base + start + 64, lanes].astype(f32)
                    gate = jax.nn.sigmoid(mixed)
                    grad = acted_ref[start : start + 64, lanes] * (gate * (1.0 + mixed * (1.0 - gate)))
                    moved_ref[1, tile, 8 + start : 72 + start] = grad
                    low_ref[start : start + 64, lanes] = grad.astype(bf16)
            if pack == 0 and block == 0:
                wait(1)
            for part in range(3):
                low, high = SPLIT[part], SPLIT[part + 1]
                for which, place, origin in ((0, 0, UP_FROM[part]), (1, 2, DOWN_FROM[part])):
                    hit = mover_ref[(2 * pack + which) * PACK + low : (2 * pack + which) * PACK + high]
                    moved = mm(hit, low_ref[origin : origin + SPAN])
                    for tile in range(tiles):
                        moved_ref[place, tile, 8 + low : 8 + high] = moved[:, tile * 128 : tile * 128 + 128]
            if pack == 0:
                if block == 0:
                    wait(2)
                wait(7 + 2 * count + block)
            for tile in range(tiles):
                lanes = slice(tile * 128, tile * 128 + 128)
                kernel = [taps[k : k + 1, lanes] for k in range(9)]
                for start in range(0, PACK, 32):
                    r = slice(base + start, base + start + 32)
                    left_mask, right_mask = side_ref[r, 0:128], side_ref[r, 128:256]
                    expanded = expanded_ref[r, lanes].astype(f32)
                    total = None
                    for a in range(3):
                        for b in range(3):
                            near = moved_ref[a, tile, 7 + b + start : 39 + b + start]
                            if b != 1:
                                near = near * (left_mask if b == 0 else right_mask)
                            tap = 8 - 3 * a - b
                            term = near * kernel[tap]
                            total = term if total is None else total + term
                            product = near * expanded
                            sums[tile][tap] = sums[tile][tap] + jnp.sum(product.reshape(4, 8, 128), axis=0)
                    grad_expanded_ref[r, lanes] = total.astype(bf16)
        send(block)
        if block == 0:
            for i in range(3, 7):
                wait(i)
            turned_ref[...] = token_ref[...].T
        grad_ref[0:width] = mm(turned_ref[...], grad_expanded_ref[...]).astype(bf16)
        depth = jnp.concatenate(
            [
                jnp.concatenate([jnp.sum(sums[tile][k], axis=0, keepdims=True) for k in range(9)], axis=0)
                for tile in range(tiles)
            ],
            axis=1,
        )
        high, rest = small_rows(gain_refs, width)
        grad_ref[width:] = jnp.concatenate([depth, high, rest, jnp.zeros((1, width), f32)], axis=0).astype(bf16)
        send(count + block)


def run_conv_backward(grad_projected, tokens, mover, side, gains, projects, smalls, expanded, mixed, after=()):
    rows, width = grad_projected.shape
    count = len(projects)
    loads = [0, 7, 7 + 3 * count, 7 + count, 1, 2, 7 + 2 * count, 3, 4, 5, 6]
    for block in range(1, count):
        loads += [7 + block, 7 + 3 * count + block, 7 + count + block, 7 + 2 * count + block]
    result = call_staged(
        functools.partial(conv_backward_kernel, count),
        "conv_backward",
        [grad_projected, mover, side, tokens, *gains, *projects, *mixed, *expanded, *smalls],
        [shaped((rows, width), bf16)] * count + [shaped((width + 16, width), bf16)] * count,
        [
            pltpu.VMEM((PACK, width), f32),
            pltpu.VMEM((PACK, width), bf16),
            pltpu.VMEM((3, width // 128, PACK + 16, 128), f32),
            pltpu.VMEM((width, rows), bf16),
        ],
        6 * count,
        after,
        order=loads,
    )
    return result[:count], result[count:]


def token_grad_kernel(ins, wait, outs, send):
    grad_one_ref, grad_refs, weight_refs = ins[0], ins[1:5], ins[5:9]
    (out_ref,) = outs
    rows = grad_one_ref.shape[0]
    for i in range(9):
        wait(i)
    weight = jnp.concatenate([w[...] for w in weight_refs], axis=1)
    for part in range(4):
        r = slice(part * rows // 4, (part + 1) * rows // 4)
        grad = jnp.concatenate([g[r] for g in grad_refs], axis=1)
        out_ref[r] = (grad_one_ref[r] + mm_t(grad, weight)).astype(bf16)
        send(0, part)


def run_token_grad(grad_one, grads, weights, after=()):
    (result,) = call_staged(
        token_grad_kernel, "token_grad", [grad_one, *grads, *weights], [shaped(grad_one.shape, bf16)], [], 4, after,
        out_parts={0: 4},
        megabytes=20,
    )
    return result


def run_join(index, mine, other, sizes, turns):
    rows, columns = mine.shape
    forms = {"plain": lambda s: (s, columns), "turned": lambda s: (columns, s), "slabs": lambda s: (columns // 128, s, 128)}
    shapes = [forms[turn](s) for s, turn in zip(sizes, turns)]
    return pl.pallas_call(
        functools.partial(join_kernel, turns),
        in_specs=[smem, vmem, vmem],
        out_specs=[vmem] * len(sizes),
        out_shape=[shaped(s, f32) for s in shapes],
        scratch_shapes=[pltpu.VMEM((2 * rows, columns), f32)],
        compiler_params=params(20),
        cost_estimate=cost(2),
        name="join_halves",
    )(index, mine, other)


def per_device(
    tokens, cotangent, shapes, head_mask, w_expand, w_depth, w_project, gain_conv, gain_attn, w_qkv, w_out,
    gain_mlp, w_up, w_down,
):
    rows, width = tokens.shape
    packs = rows // PACK
    channels = w_expand.shape[1]
    tensor_size = lax.axis_size("tensor")
    dp_size = lax.axis_size("dp")
    me_dp = lax.axis_index("dp")
    bits = [1 << b for b in range(dp_size.bit_length() - 1)]
    place = {bit: ((me_dp & bit) != 0).astype(jnp.int32) for bit in bits}

    def hold(x, after):
        return lax.optimization_barrier((x, after))[0]

    def swap_tensor(x, bit):
        return lax.ppermute(x, "tensor", [(i, i ^ bit) for i in range(tensor_size)])

    def swap_dp(x, bit):
        return lax.ppermute(x, "dp", [(i, i ^ bit) for i in range(dp_size)])

    def add(*parts):
        total = parts[0].astype(f32)
        for part in parts[1:]:
            total = total + part.astype(f32)
        return total.astype(bf16)

    def near_far(keep, pair):
        half = keep.shape[0] // 2
        return add(keep[:half], pair[:half]), add(keep[half:], pair[half:])

    def part(x, bit, mine):
        half = x.shape[0] // 2
        chosen = place[bit] if mine else 1 - place[bit]
        return lax.dynamic_slice_in_dim(x, chosen * half, half, 0)

    def halves(x, bit):
        send = part(x, bit, False)
        return part(x, bit, True), send, swap_dp(send, bit)

    def both(mine, other, bit):
        first = place[bit] == 0
        return jnp.concatenate([jnp.where(first, mine, other), jnp.where(first, other, mine)])

    def rest(x):
        for bit in bits[3:]:
            x = add(x, swap_dp(x, bit))
        return x

    other = jnp.concatenate(
        [
            w_project,
            w_depth,
            jnp.pad(head_mask.astype(bf16)[None, :], ((0, 6), (0, channels - head_mask.shape[0]))),
        ]
    )
    expand_w = [w_expand, swap_tensor(w_expand, 1)]
    other_w = [other, swap_tensor(other, 1)]
    far_expand, far_other = swap_tensor(w_expand, 2), swap_tensor(other, 2)
    project_w = [(w, 0, channels) for w in other_w]
    small_w = [(w, channels, 16) for w in other_w]
    exp_a, mix_a, act_a, (partial, mover, side, segment, segment_row) = run_conv_forward(
        tokens, shapes, shapes, expand_w, project_w, small_w, first=True
    )
    slabs, out_weight = hold((w_qkv, w_out), partial)
    slabs = slabs.transpose(1, 0, 2).reshape(-1, w_qkv.shape[2])
    slab_w = [slabs, swap_tensor(slabs, 1), swap_tensor(slabs, 2)]
    out_w = [out_weight, swap_tensor(out_weight, 1), swap_tensor(out_weight, 2)]
    far_expand, far_other = hold((far_expand, far_other), partial)
    expand_w += [far_expand, swap_tensor(far_expand, 1)]
    other_w += [far_other, swap_tensor(far_other, 1)]
    project_w = [(w, 0, channels) for w in other_w]
    small_w = [(w, channels, 16) for w in other_w]
    mlp = jnp.concatenate(hold([w_up, w_down], partial))
    mlp_w = [mlp, swap_tensor(mlp, 1), swap_tensor(mlp, 2)]
    exp_b, mix_b, act_b, (projected, residual_one, attn_low) = run_conv_forward(
        tokens, mover, side, expand_w[2:], project_w[2:], small_w[2:], partial, (gain_conv, gain_attn)
    )
    slab_w[2], out_w[2] = hold((slab_w[2], out_w[2]), attn_low)
    slab_w.append(swap_tensor(slab_w[2], 1))
    out_w.append(swap_tensor(out_w[2], 1))
    qkv, exps, inverse, merged, residual_two, mlp_low = run_attention_forward(
        attn_low, residual_one, segment, segment_row, gain_mlp, slab_w, out_w, small_w
    )
    mlp_w[2] = hold(mlp_w[2], mlp_low)
    mlp_w.append(swap_tensor(mlp_w[2], 1))
    (out_tokens, grad_two, gain_m), (mlp_0, mlp_1, mlp_2, mlp_3) = run_mlp(
        mlp_low, cotangent, residual_two, gain_mlp, mlp_w
    )
    mlp_far = add(mlp_2, swap_tensor(mlp_3, 1))
    mlp_cross = swap_tensor(mlp_far, 2)
    mlp_pair = swap_tensor(mlp_1, 1)
    grad_one, grad_projected, gain_a, gain_c, attn_0, attn_1, attn_2, attn_3 = run_attention_back(
        grad_two, qkv, exps, inverse, merged, out_w, small_w, attn_low, residual_one, projected, gain_attn, gain_conv,
        slab_w, [*act_a, *act_b], (mlp_far,),
    )
    gains = (gain_c, gain_a, gain_m)
    mlp_cross = hold(mlp_cross, grad_one)
    attn_pair_3 = swap_tensor(hold(attn_3, mlp_cross), 1)
    mlp_half, mlp_send, mlp_other = halves(add(mlp_0, mlp_pair, mlp_cross), 1)
    attn_far = add(attn_2, hold(attn_pair_3, mlp_half))
    attn_cross = swap_tensor(attn_far, 2)
    attn_pair_1 = swap_tensor(attn_1, 1)

    grads_b, (conv_2, conv_3) = run_conv_backward(
        grad_projected, tokens, mover, side, gains, project_w[2:], small_w[2:], exp_b, mix_b,
        (mlp_half, mlp_send, attn_far),
    )
    mlp_other = hold(mlp_other, conv_3)
    conv_pair_3 = swap_tensor(hold(conv_3, mlp_other), 1)
    mlp_half, mlp_send, mlp_other = halves(add(mlp_half, mlp_other), 2)
    conv_far = add(conv_2, hold(conv_pair_3, mlp_half))
    conv_cross = swap_tensor(conv_far, 2)
    attn_half, attn_send, attn_other = halves(add(attn_0, attn_pair_1, hold(attn_cross, conv_far)), 1)

    grads_a, (conv_0, conv_1) = run_conv_backward(
        grad_projected, tokens, mover, side, gains, project_w[:2], small_w[:2], exp_a, mix_a,
        (mlp_half, mlp_send, conv_far, attn_half, attn_send),
    )
    attn_other = hold(attn_other, conv_1)
    conv_pair_1 = swap_tensor(hold(conv_1, attn_other), 1)
    attn_half, attn_send, attn_other = halves(add(attn_half, attn_other), 2)
    conv_near = add(conv_0, hold(conv_pair_1, attn_half), hold(conv_cross, attn_half))
    small = conv_near[width:]
    main = conv_near[:width]
    tail = jnp.concatenate([part(main, 1, True), small])
    tail_other = swap_dp(jnp.concatenate([part(main, 1, False), small]), 1)
    mlp_half = add(mlp_half, hold(mlp_other, tail))
    mlp_other = swap_dp(mlp_half, 4)
    grad_tokens = run_token_grad(grad_one, [*grads_a, *grads_b], expand_w, (tail, mlp_half, attn_half, attn_send))
    half = width // 2
    attn_half = add(attn_half, hold(attn_other, grad_tokens))
    attn_other = swap_dp(attn_half, 4)
    tail = add(tail, hold(tail_other, attn_half))
    main, small = tail[:half], tail[half:]
    tail_other = swap_dp(jnp.concatenate([part(main, 2, False), small]), 2)
    tail = jnp.concatenate([part(main, 2, True), small])
    mlp_half = rest(add(mlp_half, hold(mlp_other, tail)))
    mlp_other = swap_dp(mlp_half, 2)
    tail = add(tail, hold(tail_other, mlp_half))
    tail_other = swap_dp(tail, 4)
    attn_half = rest(add(attn_half, hold(attn_other, tail)))
    attn_other = swap_dp(attn_half, 2)
    mlp_half = both(mlp_half, hold(mlp_other, attn_half), 2)
    mlp_other = swap_dp(mlp_half, 1)
    tail = rest(add(tail, hold(tail_other, mlp_half)))
    half = half // 2
    main, small = tail[:half], tail[half:].astype(f32)
    main_other = swap_dp(main, 2)
    attn_half = both(attn_half, hold(attn_other, main), 2)
    attn_other = swap_dp(attn_half, 1)
    main = both(main, hold(main_other, attn_half), 2)
    main_other = swap_dp(main, 1)
    index = place[1][None]
    grad_up, grad_down = run_join(index, mlp_half, mlp_other, (width, width), ("plain", "turned"))
    grad_qkv, grad_out, grad_project = run_join(
        index, attn_half, attn_other, (width, w_out.shape[0], width), ("slabs", "plain", "turned")
    )
    (grad_expand,) = run_join(index, main, main_other, (width,), ("plain",))
    gain_sums = small[9:12] + small[12:15]
    return (
        out_tokens, grad_tokens, grad_expand, small[:9], grad_project, gain_sums[0], gain_sums[1],
        grad_qkv.transpose(1, 0, 2), grad_out, gain_sums[2], grad_up, grad_down,
    )


def solution(mesh):
    rows = P(("dp", "tensor"), None)
    cols = P(None, "tensor")
    down = P("tensor", None)
    return jax.shard_map(
        per_device,
        mesh=mesh,
        in_specs=(
            rows, rows, P("dp", None, None), P("tensor"), cols, cols, down, P(), P(), P(None, None, "tensor"), down,
            P(), cols, down,
        ),
        out_specs=(rows, rows, cols, cols, down, P(), P(), P(None, None, "tensor"), down, P(), cols, down),
        check_vma=False,
    )
```

```python
import functools
import jax
import jax.numpy as jnp
from jax import lax
from jax.experimental import pallas as pl
from jax.experimental.pallas import tpu as pltpu
from jax.sharding import PartitionSpec as P

HSZ = 64
PACK = 512
SPAN = 256
SPLIT = (0, 240, 480, 512)
UP_FROM = (0, 224, 256)
DOWN_FROM = (0, 240, 256)

epsilon = 1e-05
f32 = jnp.float32
bf16 = jnp.bfloat16


def mm(a, b):
    return jnp.dot(a, b, preferred_element_type=f32)


def mm_t(a, b):
    return lax.dot_general(a, b, (((1,), (1,)), ((), ())), preferred_element_type=f32)


def t_mm(a, b):
    return lax.dot_general(a, b, (((0,), (0,)), ((), ())), preferred_element_type=f32)


def standard(values):
    centred = values - jnp.mean(values, axis=-1, keepdims=True)
    inverse = lax.rsqrt(jnp.mean(centred * centred, axis=-1, keepdims=True) + epsilon)
    return centred * inverse, inverse


def standard_back(grad, unit, inverse):
    mean_grad = jnp.mean(grad, axis=-1, keepdims=True)
    mean_both = jnp.mean(grad * unit, axis=-1, keepdims=True)
    return (grad - mean_grad - unit * mean_both) * inverse


def geometry(pack, packs, shape_ref, mover_ref, side_ref, segment_ref, segment_row_ref, slot_ref):
    own = lax.axis_index("tensor") * packs + pack
    rows = slice(pack * PACK, (pack + 1) * PACK)
    slot_ref[...] = jnp.zeros_like(slot_ref)
    slot_ref[0:2, 0 : shape_ref.shape[2]] = shape_ref[own].astype(f32)
    sides = slot_ref[...]
    height_slots = sides[0:1]
    width_slots = sides[1:2]
    sizes = jnp.broadcast_to(height_slots * width_slots, (8, 128))
    before = lax.broadcasted_iota(jnp.int32, (128, 128), 0)
    after = lax.broadcasted_iota(jnp.int32, (128, 128), 1)
    ends = mm(sizes.astype(bf16), (before <= after).astype(bf16))[0:1]
    starts = ends - height_slots * width_slots
    places = lax.broadcasted_iota(jnp.int32, (PACK, 128), 0).astype(f32)
    here = ((starts <= places) & (places < ends)).astype(f32)
    image_start = jnp.sum(here * starts, axis=1, keepdims=True)
    height = jnp.sum(here * height_slots, axis=1, keepdims=True)
    width = jnp.sum(here * width_slots, axis=1, keepdims=True)
    place = places[:, 0:1]
    offset = place - image_start
    safe = jnp.maximum(width, 1.0)
    grid_row = jnp.floor((offset + 0.5) / safe)
    grid_col = offset - grid_row * safe
    above = jnp.where(grid_row >= 1.0, place - width, -1.0)
    below = jnp.where(grid_row + 1.0 < height, place + width, -1.0)
    lanes = lax.broadcasted_iota(jnp.int32, (1, SPAN), 1).astype(f32)
    for part in range(3):
        low, high = SPLIT[part], SPLIT[part + 1]
        for which, (target, origin) in enumerate(((above, UP_FROM[part]), (below, DOWN_FROM[part]))):
            hit = (target[low:high] == lanes + origin).astype(f32).astype(bf16)
            mover_ref[(2 * pack + which) * PACK + low : (2 * pack + which) * PACK + high] = hit
    side_ref[rows, 0:128] = jnp.broadcast_to((grid_col >= 1.0).astype(f32), (PACK, 128))
    side_ref[rows, 128:256] = jnp.broadcast_to((grid_col + 1.0 < width).astype(f32), (PACK, 128))
    segment = jnp.broadcast_to(image_start, (PACK, 128))
    segment_ref[rows] = segment
    segment_row_ref[pack] = segment.T[0:8]


def gelu_parts(values):
    cdf = 0.5 + 0.5 * lax.erf(values * 0.7071067811865476)
    bell = jnp.exp2(values * values * (-0.5 * 1.4426950408889634))
    return values * cdf, cdf + values * bell * 0.3989422804014327


def mlp_kernel(ins, wait, outs, send, act_ref, pre_ref, down_ref, up_ref, turned_ref, *buffers):
    mlp_ref, cotangent_ref, residual_ref, gain_ref = ins[:4]
    weight_refs = ins[4:]
    out_ref, grad_two_ref, gain_grad_ref = outs[:3]
    grad_refs = outs[3:]
    rows, width = mlp_ref.shape
    size = 256
    chunks = rows // size
    wait(0)
    turned_ref[0] = mlp_ref[...].T
    wait(1)
    turned_ref[1] = cotangent_ref[...].T

    def arrange(half, blocks):
        for side, block in enumerate(blocks):
            wait(4 + block)
            lanes = slice(side * width, (side + 1) * width)
            down_ref[half, lanes] = weight_refs[block][width:]
            up_ref[half, :, lanes] = weight_refs[block][0:width]

    arrange(0, (1, 3))
    arrange(1, (0, 2))

    def products(j, buffer):
        half = j // chunks
        r = pl.ds((j % chunks) * size, size)
        buffer[0] = mm(mlp_ref[r], up_ref[half])
        buffer[1] = mm_t(cotangent_ref[r], down_ref[half])

    def gates(j, buffer):
        half = j // chunks
        r = pl.ds((j % chunks) * size, size)
        act, slope = gelu_parts(buffer[0])
        act_ref[half, r] = act.astype(bf16)
        pre_ref[half, r] = (buffer[1] * slope).astype(bf16)

    products(0, buffers[0])

    def one(k, carry):
        products(2 * k + 1, buffers[1])
        gates(2 * k, buffers[0])
        products(jnp.minimum(2 * k + 2, 2 * chunks - 1), buffers[0])
        gates(2 * k + 1, buffers[1])
        return carry

    lax.fori_loop(0, chunks, one, 0, unroll=4)
    for half, blocks in enumerate(((1, 3), (0, 2))):
        grad_up = mm(turned_ref[0], pre_ref[half]).astype(bf16)
        grad_down = mm(turned_ref[1], act_ref[half]).astype(bf16)
        for place, block in enumerate(blocks):
            lanes = slice(place * width, (place + 1) * width)
            grad_refs[block][0:width] = grad_up[:, lanes]
            grad_refs[block][width:] = grad_down[:, lanes]
            send(3 + block)
    wait(2)
    wait(3)
    gain_grad_ref[...] = jnp.zeros_like(gain_grad_ref)

    def finish(c, carry):
        r = pl.ds(c * size, size)
        grad_in = mm_t(pre_ref[0, r], up_ref[0]) + mm_t(pre_ref[1, r], up_ref[1])
        residual = residual_ref[r]
        out = residual + (mm(act_ref[0, r], down_ref[0]) + mm(act_ref[1, r], down_ref[1]))
        out_ref[r] = out.astype(bf16)
        send(0, c)
        unit, inverse = standard(residual)
        gain_grad_ref[...] += jnp.sum((grad_in * unit).reshape(size // 8, 8, width), axis=0)
        grad_two_ref[r] = cotangent_ref[r].astype(f32) + standard_back(grad_in * gain_ref[...], unit, inverse)
        send(1, c)
        return carry

    lax.fori_loop(0, chunks, finish, 0, unroll=4)
    send(2)


def run_mlp(mlp, cotangent, residual, gain, weights):
    rows, width = mlp.shape
    channels = weights[0].shape[1]
    grads = shaped((2 * width, channels), bf16)
    wide = 2 * channels
    result = call_staged(
        mlp_kernel,
        "mlp_both",
        [mlp, cotangent, residual, gain, *weights],
        [shaped((rows, width), bf16), shaped((rows, width), f32), shaped((8, width), f32), *[grads] * 4],
        [
            pltpu.VMEM((2, rows, wide), bf16),
            pltpu.VMEM((2, rows, wide), bf16),
            pltpu.VMEM((2, wide, width), bf16),
            pltpu.VMEM((2, width, wide), bf16),
            pltpu.VMEM((2, width, rows), bf16),
            pltpu.VMEM((2, 256, wide), f32),
            pltpu.VMEM((2, 256, wide), f32),
        ],
        16,
        out_parts={0: rows // 256, 1: rows // 256},
        order=(0, 5, 7, 1, 4, 6, 2, 3),
    )
    return result[:3], result[3:]


HEADS_ON = 6


def list_heads(flag_refs, list_ref):
    count = jnp.int32(0)
    for head in range(2 * len(flag_refs)):
        on = flag(flag_refs[head // 2], head % 2)

        @pl.when(on)
        def _(count=count, head=head):
            list_ref[count] = jnp.int32(head)

        count = count + on.astype(jnp.int32)


def flag(flag_ref, side):
    return jnp.max(flag_ref[9:10, side : side + 1].astype(f32)) != 0


def lane_joined(weight_ref):
    rows = weight_ref.shape[0] // 3
    return jnp.concatenate([weight_ref[j * rows : (j + 1) * rows] for j in range(3)], axis=1)


def attention_forward_kernel(ins, wait, outs, send, list_ref, wide_ref):
    attn_ref, segment_ref, segment_row_ref, residual_ref, gain_ref = ins[:5]
    slab_refs, out_weight_refs, flag_refs = ins[5:9], ins[9:13], ins[13:17]
    qkv_ref, exps_ref, inverse_ref, merged_ref, residual_two_ref, mlp_ref = outs
    rows, width = attn_ref.shape
    for i in range(13, 17):
        wait(i)
    list_heads(flag_refs, list_ref)
    merged_ref[...] = jnp.zeros_like(merged_ref)
    inverse_ref[...] = jnp.zeros_like(inverse_ref)
    wait(5)
    wait(6)
    wait(0)
    for half in range(2):
        if half:
            wait(7)
            wait(8)
        for side in range(2):
            wide_ref[half, :, side * width : (side + 1) * width] = lane_joined(slab_refs[2 * half + side])
        projections = mm(attn_ref[...], wide_ref[half]).astype(bf16)
        for side in range(2):
            qkv_ref[2 * half + side] = projections[:, side * width : (side + 1) * width]
            send(0, 2 * half + side)
    wait(1)
    wait(2)
    lane = lax.broadcasted_iota(jnp.int32, (1, 128), 1)

    def one(i, carry):
        head = list_ref[i]
        pair = head // 2
        mine = (lane // HSZ) == (head % 2)
        scale = jnp.where(mine, HSZ**-0.5, 0.0).astype(bf16)
        for pack in range(rows // PACK):
            part = slice(pack * PACK, (pack + 1) * PACK)
            keys = qkv_ref[pair, part, 128:256]
            values = jnp.concatenate([qkv_ref[pair, part, 256:384], jnp.ones((PACK, 128), bf16)], axis=1)
            segment_row = segment_row_ref[pack, 0:1]
            for block in range(0, PACK, 256):
                r = slice(pack * PACK + block, pack * PACK + block + 256)
                scores = mm_t(qkv_ref[pair, r, 0:128] * scale, keys)
                segment = jnp.concatenate([segment_ref[r]] * (PACK // 128), axis=1)
                scores = jnp.where(segment == segment_row, scores, -1e30)
                exps = jnp.exp(scores - jnp.max(scores, axis=1, keepdims=True)).astype(bf16)
                exps_ref[i, r] = exps
                out = mm(exps, values)
                inverse = 1.0 / out[:, 128:256]
                merged_ref[pair, r] = jnp.where(mine, out[:, 0:128] * inverse, merged_ref[pair, r].astype(f32)).astype(bf16)
                inverse_ref[r] = jnp.where(lane == i, inverse, inverse_ref[r])
        send(1, i)
        return carry

    lax.fori_loop(0, HEADS_ON, one, 0, unroll=HEADS_ON)
    send(2)
    send(3)
    wait(3)
    wait(4)
    for pair in range(4):
        wait(9 + pair)
    out_weight = jnp.concatenate([w[...] for w in out_weight_refs], axis=0)
    for part in range(4):
        r = slice(part * rows // 4, (part + 1) * rows // 4)
        merged = jnp.concatenate([merged_ref[pair, r] for pair in range(4)], axis=1)
        total = residual_ref[r] + mm(merged, out_weight)
        residual_two_ref[r] = total
        send(4, part)
        unit, _ = standard(total)
        mlp_ref[r] = (unit * gain_ref[...]).astype(bf16)
        send(5, part)


def run_attention_forward(attn, residual, segment, segment_row, gain, slabs, out_weights, flags):
    rows, width = attn.shape
    outs = [
        shaped((4, rows, 384), bf16),
        shaped((HEADS_ON, rows, PACK), bf16),
        shaped((rows, 128), f32),
        shaped((4, rows, 128), bf16),
        shaped((rows, width), f32),
        shaped((rows, width), bf16),
    ]
    return call_staged(
        attention_forward_kernel,
        "attention_forward",
        [attn, segment, segment_row, residual, gain, *slabs, *out_weights, *flags],
        outs,
        [pltpu.SMEM((8,), jnp.int32), pltpu.VMEM((2, width, 768), bf16)],
        2,
        out_parts={0: 4, 1: HEADS_ON, 4: 4, 5: 4},
        order=(13, 14, 15, 16, 5, 6, 0, 7, 8, 1, 2, 9, 10, 11, 12, 4, 3),
    )


def attention_back_kernel(
    ins, wait, outs, send, list_ref, merged_grad_ref, score_ref, wide_ref, pair_ref, merged_wide_ref
):
    grad_two_ref, qkv_ref, exps_ref, inverse_ref, merged_ref = ins[:5]
    out_weight_refs, flag_refs = ins[5:9], ins[9:13]
    attn_ref, residual_ref, projected_ref, gain_attn_ref, gain_conv_ref = ins[13:18]
    slab_refs, acted_refs = ins[18:22], ins[22:26]
    grad_one_ref, grad_projected_ref, gain_attn_grad_ref, gain_conv_grad_ref = outs[:4]
    grad_refs = outs[4:]
    rows, width = grad_two_ref.shape
    for i in range(9, 13):
        wait(i)
    list_heads(flag_refs, list_ref)
    pair_ref[...] = jnp.zeros_like(pair_ref)
    gain_attn_grad_ref[...] = jnp.zeros_like(gain_attn_grad_ref)
    gain_conv_grad_ref[...] = jnp.zeros_like(gain_conv_grad_ref)
    wait(0)
    low = grad_two_ref[...].astype(bf16)
    for i in range(5, 9):
        wait(i)
    out_weight = jnp.concatenate([w[...] for w in out_weight_refs], axis=0)
    grad_merged = mm_t(low, out_weight).astype(bf16)
    for pair in range(4):
        merged_grad_ref[pair] = grad_merged[:, pair * 128 : pair * 128 + 128]
    wait(4)
    wait.more()
    for pair in range(4):
        merged_wide_ref[:, pair * 128 : pair * 128 + 128] = merged_ref[pair]
    grad_out = t_mm(merged_wide_ref[...], low).astype(bf16)
    for pair in range(4):
        grad_refs[pair][width : width + 128] = grad_out[pair * 128 : pair * 128 + 128]
    wait(1)
    wait(3)
    lane = lax.broadcasted_iota(jnp.int32, (1, 128), 1)

    def one(i, carry):
        head = list_ref[i]
        pair = head // 2
        half = head // 4
        mine = (lane // HSZ) == (head % 2)
        wait(2, i)
        for pack in range(rows // PACK):
            part = slice(pack * PACK, (pack + 1) * PACK)
            inverse = jnp.sum(jnp.where(lane == i, inverse_ref[part], 0.0), axis=1, keepdims=True)
            grad_heads = jnp.where(mine, merged_grad_ref[pair, part].astype(f32) * inverse, 0.0).astype(bf16)
            delta = jnp.sum(grad_heads.astype(f32) * merged_ref[pair, part].astype(f32), axis=1, keepdims=True)
            values = qkv_ref[pair, part, 256:384]
            for block in range(0, PACK, 256):
                r = slice(pack * PACK + block, pack * PACK + block + 256)
                b = slice(block, block + 256)
                grad_probs = mm_t(grad_heads[b], values)
                score_ref[pack, b] = (exps_ref[i, r].astype(f32) * (grad_probs - delta[b])).astype(bf16)
            grad_scores = score_ref[pack]
            grad_q = mm(grad_scores, qkv_ref[pair, part, 128:256]) * HSZ**-0.5
            grad_k = t_mm(grad_scores, qkv_ref[pair, part, 0:128]) * HSZ**-0.5
            grad_v = t_mm(exps_ref[i, part], grad_heads)
            for j, grad in enumerate((grad_q, grad_k, grad_v)):
                lanes = pl.ds(pl.multiple_of((pair % 2) * width + j * 128, 128), 128)
                pair_ref[half, part, lanes] = jnp.where(
                    mine, grad, pair_ref[half, part, lanes].astype(f32)
                ).astype(bf16)
        return carry

    lax.fori_loop(0, HEADS_ON, one, 0)
    for i in range(18, 22):
        wait(i)
    for half in range(2):
        for side in range(2):
            wide_ref[half, :, side * width : (side + 1) * width] = lane_joined(slab_refs[2 * half + side])
    for i in range(13, 18):
        wait(i)
    attn_t = attn_ref[...].T
    size = rows // 4
    for part in range(4):
        if part % 2:
            half = part // 2
            grad_qkv = mm(attn_t, pair_ref[half]).astype(bf16)
            for side in range(2):
                grad_refs[2 * half + side][0:width] = grad_qkv[:, side * width : (side + 1) * width]
        r = slice(part * size, (part + 1) * size)
        grad_in = mm_t(pair_ref[0, r], wide_ref[0]) + mm_t(pair_ref[1, r], wide_ref[1])
        unit, inverse = standard(residual_ref[r])
        gain_attn_grad_ref[...] += jnp.sum((grad_in * unit).reshape(size // 8, 8, width), axis=0)
        grad_one = grad_two_ref[r] + standard_back(grad_in * gain_attn_ref[...], unit, inverse)
        grad_one_ref[r] = grad_one
        unit, inverse = standard(projected_ref[r])
        gain_conv_grad_ref[...] += jnp.sum((grad_one * unit).reshape(size // 8, 8, width), axis=0)
        grad_projected_ref[r] = standard_back(grad_one * gain_conv_ref[...], unit, inverse).astype(bf16)
    for i in range(4):
        send(i)
    for i in range(22, 26):
        wait(i)
    projected_t = grad_projected_ref[...].T
    for half in (1, 0):
        acted = jnp.concatenate([acted_refs[2 * half][...], acted_refs[2 * half + 1][...]], axis=1)
        grad_project = mm(projected_t, acted).astype(bf16)
        for side in range(2):
            grad_refs[2 * half + side][width + 128 :] = grad_project[:, side * width : (side + 1) * width]
            send(4 + 2 * half + side)


def run_attention_back(
    grad_two, qkv, exps, inverse, merged, out_weights, flags, attn, residual, projected, gain_attn, gain_conv, slabs,
    acted, after=(),
):
    rows, width = grad_two.shape
    grads = shaped((2 * width + 128, 384), bf16)
    return call_staged(
        attention_back_kernel,
        "attention_back",
        [
            grad_two, qkv, exps, inverse, merged, *out_weights, *flags, attn, residual, projected, gain_attn, gain_conv,
            *slabs, *acted,
        ],
        [shaped((rows, width), f32), shaped((rows, width), bf16), *[shaped((8, width), f32)] * 2, *[grads] * 4],
        [
            pltpu.SMEM((8,), jnp.int32),
            pltpu.VMEM((4, rows, 128), bf16),
            pltpu.VMEM((rows // PACK, PACK, PACK), bf16),
            pltpu.VMEM((2, width, 2 * width), bf16),
            pltpu.VMEM((2, rows, 2 * width), bf16),
            pltpu.VMEM((rows, 512), bf16),
        ],
        24,
        after,
        in_parts={2: HEADS_ON},
        order=(9, 10, 11, 12, 5, 6, 7, 8, 0, 4, 1, 3, None, 2, *range(18, 22), *range(13, 18), *range(22, 26)),
    )


def small_rows(gain_refs, width):
    gains = jnp.concatenate([jnp.sum(ref[...], axis=0, keepdims=True) for ref in gain_refs], axis=0)
    high = gains.astype(bf16).astype(f32)
    return high, gains - high


def join_kernel(turns, index_ref, mine_ref, other_ref, *refs):
    out_refs = refs[:-1]
    whole_ref = refs[-1]
    first = index_ref[0] == 0
    rows = mine_ref.shape[0]
    mine = mine_ref[...].astype(f32)
    other = other_ref[...].astype(f32)
    whole_ref[0:rows] = jnp.where(first, mine, other)
    whole_ref[rows:] = jnp.where(first, other, mine)
    start = 0
    for out_ref, turn in zip(out_refs, turns):
        if turn == "slabs":
            rows = out_ref.shape[1]
            for j in range(out_ref.shape[0]):
                out_ref[j] = whole_ref[start : start + rows, j * 128 : j * 128 + 128]
        elif turn == "turned":
            rows = out_ref.shape[1]
            out_ref[...] = whole_ref[start : start + rows].T
        else:
            rows = out_ref.shape[0]
            out_ref[...] = whole_ref[start : start + rows]
        start += rows


def whole(shape):
    zeros = (0,) * len(shape)
    return pl.BlockSpec(shape, lambda p: zeros)


def params(megabytes=56):
    return pltpu.CompilerParams(vmem_limit_bytes=megabytes << 20)


def cost(microseconds):
    return pl.CostEstimate(
        flops=int(microseconds * 1.1e9), bytes_accessed=int(microseconds * 3.0e6), transcendentals=0
    )


smem = pl.BlockSpec(memory_space=pltpu.SMEM)


def shaped(shape, dtype):
    return jax.ShapeDtypeStruct(shape, dtype)


vmem = pl.BlockSpec(memory_space=pltpu.VMEM)
anywhere = pl.BlockSpec(memory_space=pl.ANY)


def call_staged(
    kernel, name, ins, outs, scratch, microseconds, after=(), in_parts=None, out_parts=None, order=None,
    megabytes=56,
):
    in_parts, out_parts = in_parts or {}, out_parts or {}
    n, m, skip = len(ins), len(outs), len(after)
    windows = {i: x[1:] for i, x in enumerate(ins) if isinstance(x, tuple)}
    ins = [x[0] if isinstance(x, tuple) else x for x in ins]
    sizes = [(windows[i][1], *x.shape[1:]) if i in windows else x.shape for i, x in enumerate(ins)]

    def body(*refs):
        in_hbm, refs = refs[:n], refs[n + skip :]
        out_hbm, refs = refs[:m], refs[m:]
        in_vmem, refs = refs[:n], refs[n:]
        out_vmem, refs = refs[:m], refs[m:]
        in_sems, refs = refs[:n], refs[n:]
        out_sems, refs = refs[:m], refs[m:]

        def copy(source, target, sem, parts, which):
            if parts == 1:
                return pltpu.make_async_copy(source, target, sem.at[0])
            size = source.shape[0] // parts
            rows = pl.ds(which * size, size)
            return pltpu.make_async_copy(source.at[rows], target.at[rows], sem.at[which])

        def load(i, which=0):
            source = in_hbm[i].at[pl.ds(*windows[i])] if i in windows else in_hbm[i]
            return copy(source, in_vmem[i], in_sems[i], in_parts.get(i, 1), which)

        def store(i, which=0):
            return copy(out_vmem[i], out_hbm[i], out_sems[i], out_parts.get(i, 1), which)

        queue = list(order or range(n))

        def more():
            while queue:
                i = queue.pop(0)
                if i is None:
                    return
                for which in range(in_parts.get(i, 1)):
                    load(i, which).start()

        def wait(i, which=0):
            load(i, which).wait()

        wait.more = more
        more()
        kernel(in_vmem, wait, out_vmem, lambda i, which=0: store(i, which).start(), *refs)
        for i in range(m):
            for which in range(out_parts.get(i, 1)):
                store(i, which).wait()

    return pl.pallas_call(
        body,
        in_specs=[anywhere] * (n + skip),
        out_specs=[anywhere] * m,
        out_shape=list(outs),
        scratch_shapes=[pltpu.VMEM(size, x.dtype) for size, x in zip(sizes, ins)]
        + [pltpu.VMEM(x.shape, x.dtype) for x in outs]
        + [pltpu.SemaphoreType.DMA((in_parts.get(i, 1),)) for i in range(n)]
        + [pltpu.SemaphoreType.DMA((out_parts.get(i, 1),)) for i in range(m)]
        + list(scratch),
        compiler_params=params(megabytes),
        cost_estimate=cost(microseconds),
        name=name,
    )(*ins, *after)


def conv_forward_kernel(
    count, first, has_partial, final, ins, wait, outs, send, raw_ref, up_ref, mid_ref, down_ref, slot_ref
):
    token_ref, mover_ref, side_ref = ins[:3]
    weight_refs, project_refs, small_refs = (ins[3 + j * count : 3 + (j + 1) * count] for j in range(3))
    extra = ins[3 + 3 * count :]
    expanded_refs, mixed_refs, acted_refs = outs[:count], outs[count : 2 * count], outs[2 * count : 3 * count]
    rows, width = token_ref.shape
    wide = count * width
    wait(0)
    for i in range(3, 3 + count):
        wait(i)
    weight = jnp.concatenate([w[...] for w in weight_refs], axis=1)
    for i in range(3 + count, 3 + 3 * count):
        wait(i)
    raw_ref[:, 0:8] = jnp.zeros((wide // 128, 8, 128), f32)
    raw_ref[:, 8 + PACK :] = jnp.zeros((wide // 128, 8, 128), f32)
    taps = jnp.concatenate([w[...] for w in small_refs], axis=1).astype(f32)
    project = jnp.concatenate([w[...] for w in project_refs], axis=0)
    total_ref = outs[3 * count]
    if first:
        shape_ref = mover_ref
        mover_ref, side_ref, segment_ref, segment_row_ref = outs[3 * count + 1 :]
        wait(1)
        wait(2)
        for pack in range(rows // PACK):
            geometry(pack, rows // PACK, shape_ref, mover_ref, side_ref, segment_ref, segment_row_ref, slot_ref)
        for i in range(3 * count + 1, 3 * count + 5):
            send(i)
    for pack in range(rows // PACK):
        base = pack * PACK
        expanded = mm(token_ref[base : base + PACK], weight)
        for tile in range(wide // 128):
            values = expanded[:, tile * 128 : tile * 128 + 128]
            raw_ref[tile, 8 : 8 + PACK] = values
            lanes = slice(tile % 3 * 128, tile % 3 * 128 + 128)
            expanded_refs[tile // 3][base : base + PACK, lanes] = values.astype(bf16)
        if pack == 0 and not first:
            wait(2)
        for tile in range(wide // 128):
            lanes = slice(tile * 128, tile * 128 + 128)
            kernel = [taps[k : k + 1, lanes] for k in range(9)]
            for start in range(0, PACK, 32):
                left = raw_ref[tile, 7 + start : 39 + start] * side_ref[base + start : base + start + 32, 0:128]
                mid = raw_ref[tile, 8 + start : 40 + start]
                right = raw_ref[tile, 9 + start : 41 + start] * side_ref[base + start : base + start + 32, 128:256]
                line = [left * kernel[3 * a] + mid * kernel[3 * a + 1] + right * kernel[3 * a + 2] for a in range(3)]
                up_ref[start : start + 32, lanes] = line[0].astype(bf16)
                mid_ref[start : start + 32, lanes] = line[1]
                down_ref[start : start + 32, lanes] = line[2].astype(bf16)
        if pack == 0 and not first:
            wait(1)
        for part in range(3):
            low, high = SPLIT[part], SPLIT[part + 1]
            hit = jnp.concatenate(
                [mover_ref[(2 * pack + which) * PACK + low : (2 * pack + which) * PACK + high] for which in range(2)], axis=1
            )
            source = jnp.concatenate(
                [
                    up_ref[UP_FROM[part] : UP_FROM[part] + SPAN],
                    down_ref[DOWN_FROM[part] : DOWN_FROM[part] + SPAN],
                ],
                axis=0,
            )
            mixed = mm(hit, source) + mid_ref[low:high]
            r = slice(base + low, base + high)
            acted = (mixed * jax.nn.sigmoid(mixed)).astype(bf16)
            mixed = mixed.astype(bf16)
            for block in range(count):
                lanes = slice(block * width, block * width + width)
                mixed_refs[block][r] = mixed[:, lanes]
                acted_refs[block][r] = acted[:, lanes]
        for i in range(3 * count):
            send(i, pack)
    for i in range(3 + 3 * count, len(ins)):
        wait(i)
    for part in range(4):
        r = slice(part * rows // 4, (part + 1) * rows // 4)
        total = mm(jnp.concatenate([a[r] for a in acted_refs], axis=1), project)
        if has_partial:
            total = total + extra[0][r]
        total_ref[r] = total
        send(3 * count, part)
        if final:
            residual_ref, attn_ref = outs[3 * count + 1 :]
            gain_conv_ref, gain_attn_ref = extra[1:]
            unit, _ = standard(total)
            residual = token_ref[r].astype(f32) + unit * gain_conv_ref[...]
            residual_ref[r] = residual
            send(3 * count + 1, part)
            unit, _ = standard(residual)
            attn_ref[r] = (unit * gain_attn_ref[...]).astype(bf16)
            send(3 * count + 2, part)


def run_conv_forward(tokens, mover, side, weights, projects, smalls, partial=None, gains=(), first=False):
    rows, width = tokens.shape
    count = len(weights)
    final = len(gains) > 0
    has_partial = partial is not None
    wide = count * width
    outs = [shaped((rows, width), bf16)] * (3 * count) + [shaped((rows, width), f32)]
    if final:
        outs += [shaped((rows, width), f32), shaped((rows, width), bf16)]
    out_parts = {i: rows // PACK if i < 3 * count else 4 for i in range(len(outs))}
    if first:
        packs = rows // PACK
        outs += [shaped((2 * rows, SPAN), bf16), shaped((rows, 256), f32), shaped((rows, 128), f32)]
        outs += [shaped((packs, 8, PACK), f32)]
    result = call_staged(
        functools.partial(conv_forward_kernel, count, first, has_partial, final),
        "conv_forward",
        [tokens, mover, side, *weights, *projects, *smalls, *([partial] if has_partial else []), *gains],
        outs,
        [
            pltpu.VMEM((wide // 128, PACK + 16, 128), f32),
            pltpu.VMEM((PACK, wide), bf16),
            pltpu.VMEM((PACK, wide), f32),
            pltpu.VMEM((PACK, wide), bf16),
            pltpu.VMEM((8, 128), f32),
        ],
        4 * count,
        out_parts=out_parts,
        order=(*((1,) if first else ()), 0, *range(3, 3 + 3 * count), 2, *(() if first else (1,)), *range(3 + 3 * count, 3 + 3 * count + has_partial + len(gains))),
    )
    return result[:count], result[count : 2 * count], result[2 * count : 3 * count], result[3 * count :]


def conv_backward_kernel(count, ins, wait, outs, send, acted_ref, low_ref, moved_ref, turned_ref):
    grad_projected_ref, mover_ref, side_ref, token_ref = ins[:4]
    gain_refs = ins[4:7]
    project_refs, mixed_refs, expanded_refs, small_refs = (ins[7 + j * count : 7 + (j + 1) * count] for j in range(4))
    grad_expanded_refs, grad_refs = outs[:count], outs[count:]
    rows, width = grad_projected_ref.shape
    tiles = width // 128
    moved_ref[:, :, 0:8] = jnp.zeros((3, tiles, 8, 128), f32)
    moved_ref[:, :, 8 + PACK :] = jnp.zeros((3, tiles, 8, 128), f32)
    wait(0)
    for block in range(count):
        mixed_ref, expanded_ref = mixed_refs[block], expanded_refs[block]
        grad_expanded_ref, grad_ref = grad_expanded_refs[block], grad_refs[block]
        wait(7 + block)
        wait(7 + 3 * count + block)
        project = project_refs[block][...]
        taps = small_refs[block][...].astype(f32)
        sums = [[jnp.zeros((8, 128), f32) for _ in range(9)] for _ in range(tiles)]
        for pack in range(rows // PACK):
            base = pack * PACK
            acted_ref[...] = mm_t(grad_projected_ref[base : base + PACK], project)
            if pack == 0:
                wait(7 + count + block)
            for tile in range(tiles):
                lanes = slice(tile * 128, tile * 128 + 128)
                for start in range(0, PACK, 64):
                    mixed = mixed_ref[base + start : base + start + 64, lanes].astype(f32)
                    gate = jax.nn.sigmoid(mixed)
                    grad = acted_ref[start : start + 64, lanes] * (gate * (1.0 + mixed * (1.0 - gate)))
                    moved_ref[1, tile, 8 + start : 72 + start] = grad
                    low_ref[start : start + 64, lanes] = grad.astype(bf16)
            if pack == 0 and block == 0:
                wait(1)
            for part in range(3):
                low, high = SPLIT[part], SPLIT[part + 1]
                for which, place, origin in ((0, 0, UP_FROM[part]), (1, 2, DOWN_FROM[part])):
                    hit = mover_ref[(2 * pack + which) * PACK + low : (2 * pack + which) * PACK + high]
                    moved = mm(hit, low_ref[origin : origin + SPAN])
                    for tile in range(tiles):
                        moved_ref[place, tile, 8 + low : 8 + high] = moved[:, tile * 128 : tile * 128 + 128]
            if pack == 0:
                if block == 0:
                    wait(2)
                wait(7 + 2 * count + block)
            for tile in range(tiles):
                lanes = slice(tile * 128, tile * 128 + 128)
                kernel = [taps[k : k + 1, lanes] for k in range(9)]
                for start in range(0, PACK, 32):
                    r = slice(base + start, base + start + 32)
                    left_mask, right_mask = side_ref[r, 0:128], side_ref[r, 128:256]
                    expanded = expanded_ref[r, lanes].astype(f32)
                    total = None
                    for a in range(3):
                        for b in range(3):
                            near = moved_ref[a, tile, 7 + b + start : 39 + b + start]
                            if b != 1:
                                near = near * (left_mask if b == 0 else right_mask)
                            tap = 8 - 3 * a - b
                            term = near * kernel[tap]
                            total = term if total is None else total + term
                            product = near * expanded
                            sums[tile][tap] = sums[tile][tap] + jnp.sum(product.reshape(4, 8, 128), axis=0)
                    grad_expanded_ref[r, lanes] = total.astype(bf16)
        send(block)
        if block == 0:
            for i in range(3, 7):
                wait(i)
            turned_ref[...] = token_ref[...].T
        grad_ref[0:width] = mm(turned_ref[...], grad_expanded_ref[...]).astype(bf16)
        depth = jnp.concatenate(
            [
                jnp.concatenate([jnp.sum(sums[tile][k], axis=0, keepdims=True) for k in range(9)], axis=0)
                for tile in range(tiles)
            ],
            axis=1,
        )
        high, rest = small_rows(gain_refs, width)
        grad_ref[width:] = jnp.concatenate([depth, high, rest, jnp.zeros((1, width), f32)], axis=0).astype(bf16)
        send(count + block)


def run_conv_backward(grad_projected, tokens, mover, side, gains, projects, smalls, expanded, mixed, after=()):
    rows, width = grad_projected.shape
    count = len(projects)
    loads = [0, 7, 7 + 3 * count, 7 + count, 1, 2, 7 + 2 * count, 3, 4, 5, 6]
    for block in range(1, count):
        loads += [7 + block, 7 + 3 * count + block, 7 + count + block, 7 + 2 * count + block]
    result = call_staged(
        functools.partial(conv_backward_kernel, count),
        "conv_backward",
        [grad_projected, mover, side, tokens, *gains, *projects, *mixed, *expanded, *smalls],
        [shaped((rows, width), bf16)] * count + [shaped((width + 16, width), bf16)] * count,
        [
            pltpu.VMEM((PACK, width), f32),
            pltpu.VMEM((PACK, width), bf16),
            pltpu.VMEM((3, width // 128, PACK + 16, 128), f32),
            pltpu.VMEM((width, rows), bf16),
        ],
        6 * count,
        after,
        order=loads,
    )
    return result[:count], result[count:]


def token_grad_kernel(ins, wait, outs, send):
    grad_one_ref, grad_refs, weight_refs = ins[0], ins[1:5], ins[5:9]
    (out_ref,) = outs
    rows = grad_one_ref.shape[0]
    for i in range(9):
        wait(i)
    weight = jnp.concatenate([w[...] for w in weight_refs], axis=1)
    for part in range(4):
        r = slice(part * rows // 4, (part + 1) * rows // 4)
        grad = jnp.concatenate([g[r] for g in grad_refs], axis=1)
        out_ref[r] = (grad_one_ref[r] + mm_t(grad, weight)).astype(bf16)
        send(0, part)


def run_token_grad(grad_one, grads, weights, after=()):
    (result,) = call_staged(
        token_grad_kernel, "token_grad", [grad_one, *grads, *weights], [shaped(grad_one.shape, bf16)], [], 4, after,
        out_parts={0: 4},
        megabytes=20,
    )
    return result


def merge_kernel(splits, unused, place_ref, *refs):
    count = len(splits)
    parts, refs = refs[: 2 * count], refs[2 * count + unused :]
    for item, split in enumerate(splits):
        total = (parts[2 * item][...].astype(f32) + parts[2 * item + 1][...].astype(f32)).astype(bf16)
        if split is None:
            refs[0][...] = total
            refs = refs[1:]
            continue
        keep_ref, send_ref = refs[:2]
        refs = refs[2:]
        half = total.shape[0] // 2
        second = place_ref[split] != 0
        keep_ref[...] = jnp.where(second, total[half:], total[:half])
        send_ref[...] = jnp.where(second, total[:half], total[half:])


def run_merge(place, items, splits, after=()):
    outs = []
    for (mine, _), split in zip(items, splits):
        rows, columns = mine.shape
        outs += [shaped((rows, columns), bf16)] if split is None else [shaped((rows // 2, columns), bf16)] * 2
    return pl.pallas_call(
        functools.partial(merge_kernel, splits, len(after)),
        in_specs=[smem] + [vmem] * (2 * len(items)) + [anywhere] * len(after),
        out_specs=[vmem] * len(outs),
        out_shape=outs,
        compiler_params=params(20),
        cost_estimate=cost(1),
        name="merge_parts",
    )(place, *[x for pair in items for x in pair], *after)


def run_join(index, mine, other, sizes, turns):
    rows, columns = mine.shape
    forms = {"plain": lambda s: (s, columns), "turned": lambda s: (columns, s), "slabs": lambda s: (columns // 128, s, 128)}
    shapes = [forms[turn](s) for s, turn in zip(sizes, turns)]
    return pl.pallas_call(
        functools.partial(join_kernel, turns),
        in_specs=[smem, vmem, vmem],
        out_specs=[vmem] * len(sizes),
        out_shape=[shaped(s, f32) for s in shapes],
        scratch_shapes=[pltpu.VMEM((2 * rows, columns), f32)],
        compiler_params=params(20),
        cost_estimate=cost(2),
        name="join_halves",
    )(index, mine, other)


def per_device(
    tokens, cotangent, shapes, head_mask, w_expand, w_depth, w_project, gain_conv, gain_attn, w_qkv, w_out,
    gain_mlp, w_up, w_down,
):
    rows, width = tokens.shape
    packs = rows // PACK
    channels = w_expand.shape[1]
    tensor_size = lax.axis_size("tensor")
    dp_size = lax.axis_size("dp")
    me_dp = lax.axis_index("dp")
    bits = [1 << b for b in range(dp_size.bit_length() - 1)]
    place = {bit: ((me_dp & bit) != 0).astype(jnp.int32) for bit in bits}

    def hold(x, after):
        return lax.optimization_barrier((x, after))[0]

    def swap_tensor(x, bit):
        return lax.ppermute(x, "tensor", [(i, i ^ bit) for i in range(tensor_size)])

    def swap_dp(x, bit):
        return lax.ppermute(x, "dp", [(i, i ^ bit) for i in range(dp_size)])

    def add(*parts):
        total = parts[0].astype(f32)
        for part in parts[1:]:
            total = total + part.astype(f32)
        return total.astype(bf16)

    def near_far(keep, pair):
        half = keep.shape[0] // 2
        return add(keep[:half], pair[:half]), add(keep[half:], pair[half:])

    def part(x, bit, mine):
        half = x.shape[0] // 2
        chosen = place[bit] if mine else 1 - place[bit]
        return lax.dynamic_slice_in_dim(x, chosen * half, half, 0)

    def halves(x, bit):
        send = part(x, bit, False)
        return part(x, bit, True), send, swap_dp(send, bit)

    def both(mine, other, bit):
        first = place[bit] == 0
        return jnp.concatenate([jnp.where(first, mine, other), jnp.where(first, other, mine)])

    def rest(x):
        for bit in bits[3:]:
            x = add(x, swap_dp(x, bit))
        return x

    other = jnp.concatenate(
        [
            w_project,
            w_depth,
            jnp.pad(head_mask.astype(bf16)[None, :], ((0, 6), (0, channels - head_mask.shape[0]))),
        ]
    )
    expand_w = [w_expand, swap_tensor(w_expand, 1)]
    other_w = [other, swap_tensor(other, 1)]
    far_expand, far_other = swap_tensor(w_expand, 2), swap_tensor(other, 2)
    project_w = [(w, 0, channels) for w in other_w]
    small_w = [(w, channels, 16) for w in other_w]
    exp_a, mix_a, act_a, (partial, mover, side, segment, segment_row) = run_conv_forward(
        tokens, shapes, shapes, expand_w, project_w, small_w, first=True
    )
    slabs, out_weight = hold((w_qkv, w_out), partial)
    slabs = slabs.transpose(1, 0, 2).reshape(-1, w_qkv.shape[2])
    slab_w = [slabs, swap_tensor(slabs, 1), swap_tensor(slabs, 2)]
    out_w = [out_weight, swap_tensor(out_weight, 1), swap_tensor(out_weight, 2)]
    far_expand, far_other = hold((far_expand, far_other), partial)
    expand_w += [far_expand, swap_tensor(far_expand, 1)]
    other_w += [far_other, swap_tensor(far_other, 1)]
    project_w = [(w, 0, channels) for w in other_w]
    small_w = [(w, channels, 16) for w in other_w]
    mlp = jnp.concatenate(hold([w_up, w_down], partial))
    mlp_w = [mlp, swap_tensor(mlp, 1), swap_tensor(mlp, 2)]
    exp_b, mix_b, act_b, (projected, residual_one, attn_low) = run_conv_forward(
        tokens, mover, side, expand_w[2:], project_w[2:], small_w[2:], partial, (gain_conv, gain_attn)
    )
    slab_w[2], out_w[2] = hold((slab_w[2], out_w[2]), attn_low)
    slab_w.append(swap_tensor(slab_w[2], 1))
    out_w.append(swap_tensor(out_w[2], 1))
    qkv, exps, inverse, merged, residual_two, mlp_low = run_attention_forward(
        attn_low, residual_one, segment, segment_row, gain_mlp, slab_w, out_w, small_w
    )
    mlp_w[2] = hold(mlp_w[2], mlp_low)
    mlp_w.append(swap_tensor(mlp_w[2], 1))
    (out_tokens, grad_two, gain_m), (mlp_0, mlp_1, mlp_2, mlp_3) = run_mlp(
        mlp_low, cotangent, residual_two, gain_mlp, mlp_w
    )
    mlp_far = add(mlp_2, swap_tensor(mlp_3, 1))
    mlp_cross = swap_tensor(mlp_far, 2)
    mlp_pair = swap_tensor(mlp_1, 1)
    grad_one, grad_projected, gain_a, gain_c, attn_0, attn_1, attn_2, attn_3 = run_attention_back(
        grad_two, qkv, exps, inverse, merged, out_w, small_w, attn_low, residual_one, projected, gain_attn, gain_conv,
        slab_w, [*act_a, *act_b], (mlp_far,),
    )
    gains = (gain_c, gain_a, gain_m)
    mlp_cross = hold(mlp_cross, grad_one)
    attn_pair_3 = swap_tensor(hold(attn_3, mlp_cross), 1)
    mlp_half, mlp_send, mlp_other = halves(add(mlp_0, mlp_pair, mlp_cross), 1)
    attn_far = add(attn_2, hold(attn_pair_3, mlp_half))
    attn_cross = swap_tensor(attn_far, 2)
    attn_pair_1 = swap_tensor(attn_1, 1)

    grads_b, (conv_2, conv_3) = run_conv_backward(
        grad_projected, tokens, mover, side, gains, project_w[2:], small_w[2:], exp_b, mix_b,
        (mlp_half, mlp_send, attn_far),
    )
    mlp_other = hold(mlp_other, conv_3)
    conv_pair_3 = swap_tensor(hold(conv_3, mlp_other), 1)
    mlp_half, mlp_send, mlp_other = halves(add(mlp_half, mlp_other), 2)
    conv_far = add(conv_2, hold(conv_pair_3, mlp_half))
    conv_cross = swap_tensor(conv_far, 2)
    attn_half, attn_send, attn_other = halves(add(attn_0, attn_pair_1, hold(attn_cross, conv_far)), 1)

    grads_a, (conv_0, conv_1) = run_conv_backward(
        grad_projected, tokens, mover, side, gains, project_w[:2], small_w[:2], exp_a, mix_a,
        (mlp_half, mlp_send, conv_far, attn_half, attn_send),
    )
    places = jnp.stack([place[bit] for bit in bits[:2]])
    attn_half, attn_send, mlp_half = run_merge(
        places, ((attn_half, attn_other), (mlp_half, mlp_other)), (1, None), (conv_1, conv_cross)
    )
    attn_other = swap_dp(attn_send, 2)
    mlp_other = swap_dp(mlp_half, 4)
    conv_pair_1 = swap_tensor(hold(conv_1, attn_half), 1)
    conv_near = add(conv_0, conv_pair_1, conv_cross)
    small = conv_near[width:]
    main = conv_near[:width]
    tail = jnp.concatenate([part(main, 1, True), small])
    tail_other = swap_dp(jnp.concatenate([part(main, 1, False), small]), 1)
    grad_tokens = run_token_grad(grad_one, [*grads_a, *grads_b], expand_w, (tail,))
    half = width // 2
    attn_half = add(attn_half, attn_other)
    attn_other = swap_dp(attn_half, 4)
    tail = add(tail, hold(tail_other, attn_half))
    main, small = tail[:half], tail[half:]
    tail_other = swap_dp(jnp.concatenate([part(main, 2, False), small]), 2)
    tail = jnp.concatenate([part(main, 2, True), small])
    mlp_half = rest(add(mlp_half, hold(mlp_other, tail)))
    mlp_other = swap_dp(mlp_half, 2)
    tail = add(tail, hold(tail_other, mlp_half))
    tail_other = swap_dp(tail, 4)
    attn_half = rest(add(attn_half, hold(attn_other, tail)))
    attn_other = swap_dp(attn_half, 2)
    mlp_half = both(mlp_half, hold(mlp_other, attn_half), 2)
    mlp_other = swap_dp(mlp_half, 1)
    tail = rest(add(tail, hold(tail_other, mlp_half)))
    half = half // 2
    main, small = tail[:half], tail[half:].astype(f32)
    main_other = swap_dp(main, 2)
    attn_half = both(attn_half, hold(attn_other, main), 2)
    attn_other = swap_dp(attn_half, 1)
    main = both(main, hold(main_other, attn_half), 2)
    main_other = swap_dp(main, 1)
    index = place[1][None]
    grad_up, grad_down = run_join(index, mlp_half, mlp_other, (width, width), ("plain", "turned"))
    grad_qkv, grad_out, grad_project = run_join(
        index, attn_half, attn_other, (width, w_out.shape[0], width), ("slabs", "plain", "turned")
    )
    (grad_expand,) = run_join(index, main, main_other, (width,), ("plain",))
    gain_sums = small[9:12] + small[12:15]
    return (
        out_tokens, grad_tokens, grad_expand, small[:9], grad_project, gain_sums[0], gain_sums[1],
        grad_qkv.transpose(1, 0, 2), grad_out, gain_sums[2], grad_up, grad_down,
    )


def solution(mesh):
    rows = P(("dp", "tensor"), None)
    cols = P(None, "tensor")
    down = P("tensor", None)
    return jax.shard_map(
        per_device,
        mesh=mesh,
        in_specs=(
            rows, rows, P("dp", None, None), P("tensor"), cols, cols, down, P(), P(), P(None, None, "tensor"), down,
            P(), cols, down,
        ),
        out_specs=(rows, rows, cols, cols, down, P(), P(), P(None, None, "tensor"), down, P(), cols, down),
        check_vma=False,
    )
```

```python
import functools
import jax
import jax.numpy as jnp
from jax import lax
from jax.experimental import pallas as pl
from jax.experimental.pallas import tpu as pltpu
from jax.sharding import PartitionSpec as P

HSZ = 64
PACK = 512
SPAN = 256
SPLIT = (0, 240, 480, 512)
UP_FROM = (0, 224, 256)
DOWN_FROM = (0, 240, 256)

epsilon = 1e-05
f32 = jnp.float32
bf16 = jnp.bfloat16


def mm(a, b):
    return jnp.dot(a, b, preferred_element_type=f32)


def mm_t(a, b):
    return lax.dot_general(a, b, (((1,), (1,)), ((), ())), preferred_element_type=f32)


def t_mm(a, b):
    return lax.dot_general(a, b, (((0,), (0,)), ((), ())), preferred_element_type=f32)


def standard(values):
    centred = values - jnp.mean(values, axis=-1, keepdims=True)
    inverse = lax.rsqrt(jnp.mean(centred * centred, axis=-1, keepdims=True) + epsilon)
    return centred * inverse, inverse


def standard_back(grad, unit, inverse):
    mean_grad = jnp.mean(grad, axis=-1, keepdims=True)
    mean_both = jnp.mean(grad * unit, axis=-1, keepdims=True)
    return (grad - mean_grad - unit * mean_both) * inverse


def geometry(pack, packs, shape_ref, mover_ref, side_ref, segment_ref, segment_row_ref, slot_ref):
    own = lax.axis_index("tensor") * packs + pack
    rows = slice(pack * PACK, (pack + 1) * PACK)
    slot_ref[...] = jnp.zeros_like(slot_ref)
    slot_ref[0:2, 0 : shape_ref.shape[2]] = shape_ref[own].astype(f32)
    sides = slot_ref[...]
    height_slots = sides[0:1]
    width_slots = sides[1:2]
    sizes = jnp.broadcast_to(height_slots * width_slots, (8, 128))
    before = lax.broadcasted_iota(jnp.int32, (128, 128), 0)
    after = lax.broadcasted_iota(jnp.int32, (128, 128), 1)
    ends = mm(sizes.astype(bf16), (before <= after).astype(bf16))[0:1]
    starts = ends - height_slots * width_slots
    places = lax.broadcasted_iota(jnp.int32, (PACK, 128), 0).astype(f32)
    here = ((starts <= places) & (places < ends)).astype(f32)
    image_start = jnp.sum(here * starts, axis=1, keepdims=True)
    height = jnp.sum(here * height_slots, axis=1, keepdims=True)
    width = jnp.sum(here * width_slots, axis=1, keepdims=True)
    place = places[:, 0:1]
    offset = place - image_start
    safe = jnp.maximum(width, 1.0)
    grid_row = jnp.floor((offset + 0.5) / safe)
    grid_col = offset - grid_row * safe
    above = jnp.where(grid_row >= 1.0, place - width, -1.0)
    below = jnp.where(grid_row + 1.0 < height, place + width, -1.0)
    lanes = lax.broadcasted_iota(jnp.int32, (1, SPAN), 1).astype(f32)
    for part in range(3):
        low, high = SPLIT[part], SPLIT[part + 1]
        for which, (target, origin) in enumerate(((above, UP_FROM[part]), (below, DOWN_FROM[part]))):
            hit = (target[low:high] == lanes + origin).astype(f32).astype(bf16)
            mover_ref[(2 * pack + which) * PACK + low : (2 * pack + which) * PACK + high] = hit
    side_ref[rows, 0:128] = jnp.broadcast_to((grid_col >= 1.0).astype(f32), (PACK, 128))
    side_ref[rows, 128:256] = jnp.broadcast_to((grid_col + 1.0 < width).astype(f32), (PACK, 128))
    segment = jnp.broadcast_to(image_start, (PACK, 128))
    segment_ref[rows] = segment
    segment_row_ref[pack] = segment.T[0:8]


def gelu_parts(values):
    cdf = 0.5 + 0.5 * lax.erf(values * 0.7071067811865476)
    bell = jnp.exp2(values * values * (-0.5 * 1.4426950408889634))
    return values * cdf, cdf + values * bell * 0.3989422804014327


def mlp_kernel(ins, wait, outs, send, act_ref, pre_ref, down_ref, up_ref, turned_ref, *buffers):
    mlp_ref, cotangent_ref, residual_ref, gain_ref = ins[:4]
    weight_refs = ins[4:]
    out_ref, grad_two_ref, gain_grad_ref = outs[:3]
    grad_refs = outs[3:]
    rows, width = mlp_ref.shape
    size = 256
    chunks = rows // size
    wait(0)
    turned_ref[0] = mlp_ref[...].T
    wait(1)
    turned_ref[1] = cotangent_ref[...].T

    def arrange(half, blocks):
        for side, block in enumerate(blocks):
            wait(4 + block)
            lanes = slice(side * width, (side + 1) * width)
            down_ref[half, lanes] = weight_refs[block][width:]
            up_ref[half, :, lanes] = weight_refs[block][0:width]

    arrange(0, (1, 3))
    arrange(1, (0, 2))

    def products(j, buffer):
        half = j // chunks
        r = pl.ds((j % chunks) * size, size)
        buffer[0] = mm(mlp_ref[r], up_ref[half])
        buffer[1] = mm_t(cotangent_ref[r], down_ref[half])

    def gates(j, buffer):
        half = j // chunks
        r = pl.ds((j % chunks) * size, size)
        act, slope = gelu_parts(buffer[0])
        act_ref[half, r] = act.astype(bf16)
        pre_ref[half, r] = (buffer[1] * slope).astype(bf16)

    products(0, buffers[0])

    def one(k, carry):
        products(2 * k + 1, buffers[1])
        gates(2 * k, buffers[0])
        products(jnp.minimum(2 * k + 2, 2 * chunks - 1), buffers[0])
        gates(2 * k + 1, buffers[1])
        return carry

    lax.fori_loop(0, chunks, one, 0, unroll=4)
    for half, blocks in enumerate(((1, 3), (0, 2))):
        grad_up = mm(turned_ref[0], pre_ref[half]).astype(bf16)
        grad_down = mm(turned_ref[1], act_ref[half]).astype(bf16)
        for place, block in enumerate(blocks):
            lanes = slice(place * width, (place + 1) * width)
            grad_refs[block][0:width] = grad_up[:, lanes]
            grad_refs[block][width:] = grad_down[:, lanes]
            send(3 + block)
    wait(2)
    wait(3)
    gain_grad_ref[...] = jnp.zeros_like(gain_grad_ref)

    def finish(c, carry):
        r = pl.ds(c * size, size)
        grad_in = mm_t(pre_ref[0, r], up_ref[0]) + mm_t(pre_ref[1, r], up_ref[1])
        residual = residual_ref[r]
        out = residual + (mm(act_ref[0, r], down_ref[0]) + mm(act_ref[1, r], down_ref[1]))
        out_ref[r] = out.astype(bf16)
        send(0, c)
        unit, inverse = standard(residual)
        gain_grad_ref[...] += jnp.sum((grad_in * unit).reshape(size // 8, 8, width), axis=0)
        grad_two_ref[r] = cotangent_ref[r].astype(f32) + standard_back(grad_in * gain_ref[...], unit, inverse)
        send(1, c)
        return carry

    lax.fori_loop(0, chunks, finish, 0, unroll=4)
    send(2)


def run_mlp(mlp, cotangent, residual, gain, weights):
    rows, width = mlp.shape
    channels = weights[0].shape[1]
    grads = shaped((2 * width, channels), bf16)
    wide = 2 * channels
    result = call_staged(
        mlp_kernel,
        "mlp_both",
        [mlp, cotangent, residual, gain, *weights],
        [shaped((rows, width), bf16), shaped((rows, width), f32), shaped((8, width), f32), *[grads] * 4],
        [
            pltpu.VMEM((2, rows, wide), bf16),
            pltpu.VMEM((2, rows, wide), bf16),
            pltpu.VMEM((2, wide, width), bf16),
            pltpu.VMEM((2, width, wide), bf16),
            pltpu.VMEM((2, width, rows), bf16),
            pltpu.VMEM((2, 256, wide), f32),
            pltpu.VMEM((2, 256, wide), f32),
        ],
        16,
        out_parts={0: rows // 256, 1: rows // 256},
        order=(0, 5, 7, 1, 4, 6, 2, 3),
    )
    return result[:3], result[3:]


HEADS_ON = 6


def list_heads(flag_refs, list_ref):
    count = jnp.int32(0)
    for head in range(2 * len(flag_refs)):
        on = flag(flag_refs[head // 2], head % 2)

        @pl.when(on)
        def _(count=count, head=head):
            list_ref[count] = jnp.int32(head)

        count = count + on.astype(jnp.int32)


def flag(flag_ref, side):
    return jnp.max(flag_ref[9:10, side : side + 1].astype(f32)) != 0


def lane_joined(weight_ref):
    rows = weight_ref.shape[0] // 3
    return jnp.concatenate([weight_ref[j * rows : (j + 1) * rows] for j in range(3)], axis=1)


def attention_forward_kernel(ins, wait, outs, send, list_ref, wide_ref):
    attn_ref, segment_ref, segment_row_ref, residual_ref, gain_ref = ins[:5]
    slab_refs, out_weight_refs, flag_refs = ins[5:9], ins[9:13], ins[13:17]
    qkv_ref, exps_ref, inverse_ref, merged_ref, residual_two_ref, mlp_ref = outs
    rows, width = attn_ref.shape
    for i in range(13, 17):
        wait(i)
    list_heads(flag_refs, list_ref)
    merged_ref[...] = jnp.zeros_like(merged_ref)
    inverse_ref[...] = jnp.zeros_like(inverse_ref)
    wait(5)
    wait(6)
    wait(0)
    for half in range(2):
        if half:
            wait(7)
            wait(8)
        for side in range(2):
            wide_ref[half, :, side * width : (side + 1) * width] = lane_joined(slab_refs[2 * half + side])
        projections = mm(attn_ref[...], wide_ref[half]).astype(bf16)
        for side in range(2):
            qkv_ref[2 * half + side] = projections[:, side * width : (side + 1) * width]
            send(0, 2 * half + side)
    wait(1)
    wait(2)
    lane = lax.broadcasted_iota(jnp.int32, (1, 128), 1)

    def one(i, carry):
        head = list_ref[i]
        pair = head // 2
        mine = (lane // HSZ) == (head % 2)
        scale = jnp.where(mine, HSZ**-0.5, 0.0).astype(bf16)
        for pack in range(rows // PACK):
            part = slice(pack * PACK, (pack + 1) * PACK)
            keys = qkv_ref[pair, part, 128:256]
            values = jnp.concatenate([qkv_ref[pair, part, 256:384], jnp.ones((PACK, 128), bf16)], axis=1)
            segment_row = segment_row_ref[pack, 0:1]
            for block in range(0, PACK, 256):
                r = slice(pack * PACK + block, pack * PACK + block + 256)
                scores = mm_t(qkv_ref[pair, r, 0:128] * scale, keys)
                segment = jnp.concatenate([segment_ref[r]] * (PACK // 128), axis=1)
                scores = jnp.where(segment == segment_row, scores, -1e30)
                exps = jnp.exp(scores - jnp.max(scores, axis=1, keepdims=True)).astype(bf16)
                exps_ref[i, r] = exps
                out = mm(exps, values)
                inverse = 1.0 / out[:, 128:256]
                merged_ref[pair, r] = jnp.where(mine, out[:, 0:128] * inverse, merged_ref[pair, r].astype(f32)).astype(bf16)
                inverse_ref[r] = jnp.where(lane == i, inverse, inverse_ref[r])
        send(1, i)
        return carry

    lax.fori_loop(0, HEADS_ON, one, 0, unroll=HEADS_ON)
    send(2)
    send(3)
    wait(3)
    wait(4)
    for pair in range(4):
        wait(9 + pair)
    out_weight = jnp.concatenate([w[...] for w in out_weight_refs], axis=0)
    for part in range(4):
        r = slice(part * rows // 4, (part + 1) * rows // 4)
        merged = jnp.concatenate([merged_ref[pair, r] for pair in range(4)], axis=1)
        total = residual_ref[r] + mm(merged, out_weight)
        residual_two_ref[r] = total
        send(4, part)
        unit, _ = standard(total)
        mlp_ref[r] = (unit * gain_ref[...]).astype(bf16)
        send(5, part)


def run_attention_forward(attn, residual, segment, segment_row, gain, slabs, out_weights, flags):
    rows, width = attn.shape
    outs = [
        shaped((4, rows, 384), bf16),
        shaped((HEADS_ON, rows, PACK), bf16),
        shaped((rows, 128), f32),
        shaped((4, rows, 128), bf16),
        shaped((rows, width), f32),
        shaped((rows, width), bf16),
    ]
    return call_staged(
        attention_forward_kernel,
        "attention_forward",
        [attn, segment, segment_row, residual, gain, *slabs, *out_weights, *flags],
        outs,
        [pltpu.SMEM((8,), jnp.int32), pltpu.VMEM((2, width, 768), bf16)],
        2,
        out_parts={0: 4, 1: HEADS_ON, 4: 4, 5: 4},
        order=(13, 14, 15, 16, 5, 6, 0, 7, 8, 1, 2, 9, 10, 11, 12, 4, 3),
    )


def attention_back_kernel(
    ins, wait, outs, send, list_ref, merged_grad_ref, score_ref, wide_ref, pair_ref, merged_wide_ref
):
    grad_two_ref, qkv_ref, exps_ref, inverse_ref, merged_ref = ins[:5]
    out_weight_refs, flag_refs = ins[5:9], ins[9:13]
    attn_ref, residual_ref, projected_ref, gain_attn_ref, gain_conv_ref = ins[13:18]
    slab_refs, acted_refs = ins[18:22], ins[22:26]
    grad_one_ref, grad_projected_ref, gain_attn_grad_ref, gain_conv_grad_ref = outs[:4]
    grad_refs = outs[4:]
    rows, width = grad_two_ref.shape
    for i in range(9, 13):
        wait(i)
    list_heads(flag_refs, list_ref)
    pair_ref[...] = jnp.zeros_like(pair_ref)
    gain_attn_grad_ref[...] = jnp.zeros_like(gain_attn_grad_ref)
    gain_conv_grad_ref[...] = jnp.zeros_like(gain_conv_grad_ref)
    wait(0)
    low = grad_two_ref[...].astype(bf16)
    for i in range(5, 9):
        wait(i)
    out_weight = jnp.concatenate([w[...] for w in out_weight_refs], axis=0)
    grad_merged = mm_t(low, out_weight).astype(bf16)
    for pair in range(4):
        merged_grad_ref[pair] = grad_merged[:, pair * 128 : pair * 128 + 128]
    wait(4)
    wait.more()
    for pair in range(4):
        merged_wide_ref[:, pair * 128 : pair * 128 + 128] = merged_ref[pair]
    grad_out = t_mm(merged_wide_ref[...], low).astype(bf16)
    for pair in range(4):
        grad_refs[pair][width : width + 128] = grad_out[pair * 128 : pair * 128 + 128]
    wait(1)
    wait(3)
    lane = lax.broadcasted_iota(jnp.int32, (1, 128), 1)

    def one(i, carry):
        head = list_ref[i]
        pair = head // 2
        half = head // 4
        mine = (lane // HSZ) == (head % 2)
        wait(2, i)
        for pack in range(rows // PACK):
            part = slice(pack * PACK, (pack + 1) * PACK)
            inverse = jnp.sum(jnp.where(lane == i, inverse_ref[part], 0.0), axis=1, keepdims=True)
            grad_heads = jnp.where(mine, merged_grad_ref[pair, part].astype(f32) * inverse, 0.0).astype(bf16)
            delta = jnp.sum(grad_heads.astype(f32) * merged_ref[pair, part].astype(f32), axis=1, keepdims=True)
            values = qkv_ref[pair, part, 256:384]
            for block in range(0, PACK, 256):
                r = slice(pack * PACK + block, pack * PACK + block + 256)
                b = slice(block, block + 256)
                grad_probs = mm_t(grad_heads[b], values)
                score_ref[pack, b] = (exps_ref[i, r].astype(f32) * (grad_probs - delta[b])).astype(bf16)
            grad_scores = score_ref[pack]
            grad_q = mm(grad_scores, qkv_ref[pair, part, 128:256]) * HSZ**-0.5
            grad_k = t_mm(grad_scores, qkv_ref[pair, part, 0:128]) * HSZ**-0.5
            grad_v = t_mm(exps_ref[i, part], grad_heads)
            for j, grad in enumerate((grad_q, grad_k, grad_v)):
                lanes = pl.ds(pl.multiple_of((pair % 2) * width + j * 128, 128), 128)
                pair_ref[half, part, lanes] = jnp.where(
                    mine, grad, pair_ref[half, part, lanes].astype(f32)
                ).astype(bf16)
        return carry

    lax.fori_loop(0, HEADS_ON, one, 0)
    for i in range(18, 22):
        wait(i)
    for half in range(2):
        for side in range(2):
            wide_ref[half, :, side * width : (side + 1) * width] = lane_joined(slab_refs[2 * half + side])
    for i in range(13, 18):
        wait(i)
    attn_t = attn_ref[...].T
    size = rows // 4
    for part in range(4):
        if part % 2:
            half = part // 2
            grad_qkv = mm(attn_t, pair_ref[half]).astype(bf16)
            for side in range(2):
                grad_refs[2 * half + side][0:width] = grad_qkv[:, side * width : (side + 1) * width]
        r = slice(part * size, (part + 1) * size)
        grad_in = mm_t(pair_ref[0, r], wide_ref[0]) + mm_t(pair_ref[1, r], wide_ref[1])
        unit, inverse = standard(residual_ref[r])
        gain_attn_grad_ref[...] += jnp.sum((grad_in * unit).reshape(size // 8, 8, width), axis=0)
        grad_one = grad_two_ref[r] + standard_back(grad_in * gain_attn_ref[...], unit, inverse)
        grad_one_ref[r] = grad_one
        unit, inverse = standard(projected_ref[r])
        gain_conv_grad_ref[...] += jnp.sum((grad_one * unit).reshape(size // 8, 8, width), axis=0)
        grad_projected_ref[r] = standard_back(grad_one * gain_conv_ref[...], unit, inverse).astype(bf16)
    for i in range(4):
        send(i)
    for i in range(22, 26):
        wait(i)
    projected_t = grad_projected_ref[...].T
    for half in (1, 0):
        acted = jnp.concatenate([acted_refs[2 * half][...], acted_refs[2 * half + 1][...]], axis=1)
        grad_project = mm(projected_t, acted).astype(bf16)
        for side in range(2):
            grad_refs[2 * half + side][width + 128 :] = grad_project[:, side * width : (side + 1) * width]
            send(4 + 2 * half + side)


def run_attention_back(
    grad_two, qkv, exps, inverse, merged, out_weights, flags, attn, residual, projected, gain_attn, gain_conv, slabs,
    acted, after=(),
):
    rows, width = grad_two.shape
    grads = shaped((2 * width + 128, 384), bf16)
    return call_staged(
        attention_back_kernel,
        "attention_back",
        [
            grad_two, qkv, exps, inverse, merged, *out_weights, *flags, attn, residual, projected, gain_attn, gain_conv,
            *slabs, *acted,
        ],
        [shaped((rows, width), f32), shaped((rows, width), bf16), *[shaped((8, width), f32)] * 2, *[grads] * 4],
        [
            pltpu.SMEM((8,), jnp.int32),
            pltpu.VMEM((4, rows, 128), bf16),
            pltpu.VMEM((rows // PACK, PACK, PACK), bf16),
            pltpu.VMEM((2, width, 2 * width), bf16),
            pltpu.VMEM((2, rows, 2 * width), bf16),
            pltpu.VMEM((rows, 512), bf16),
        ],
        24,
        after,
        in_parts={2: HEADS_ON},
        order=(9, 10, 11, 12, 5, 6, 7, 8, 0, 4, 1, 3, None, 2, *range(18, 22), *range(13, 18), *range(22, 26)),
    )


def small_rows(gain_refs, width):
    gains = jnp.concatenate([jnp.sum(ref[...], axis=0, keepdims=True) for ref in gain_refs], axis=0)
    high = gains.astype(bf16).astype(f32)
    return high, gains - high


def join_kernel(turns, index_ref, mine_ref, other_ref, *refs):
    out_refs = refs[:-1]
    whole_ref = refs[-1]
    first = index_ref[0] == 0
    rows = mine_ref.shape[0]
    mine = mine_ref[...].astype(f32)
    other = other_ref[...].astype(f32)
    whole_ref[0:rows] = jnp.where(first, mine, other)
    whole_ref[rows:] = jnp.where(first, other, mine)
    start = 0
    for out_ref, turn in zip(out_refs, turns):
        if turn == "slabs":
            rows = out_ref.shape[1]
            for j in range(out_ref.shape[0]):
                out_ref[j] = whole_ref[start : start + rows, j * 128 : j * 128 + 128]
        elif turn == "turned":
            rows = out_ref.shape[1]
            out_ref[...] = whole_ref[start : start + rows].T
        else:
            rows = out_ref.shape[0]
            out_ref[...] = whole_ref[start : start + rows]
        start += rows


def whole(shape):
    zeros = (0,) * len(shape)
    return pl.BlockSpec(shape, lambda p: zeros)


def params(megabytes=56):
    return pltpu.CompilerParams(vmem_limit_bytes=megabytes << 20)


def cost(microseconds):
    return pl.CostEstimate(
        flops=int(microseconds * 1.1e9), bytes_accessed=int(microseconds * 3.0e6), transcendentals=0
    )


smem = pl.BlockSpec(memory_space=pltpu.SMEM)


def shaped(shape, dtype):
    return jax.ShapeDtypeStruct(shape, dtype)


vmem = pl.BlockSpec(memory_space=pltpu.VMEM)
anywhere = pl.BlockSpec(memory_space=pl.ANY)


def call_staged(
    kernel, name, ins, outs, scratch, microseconds, after=(), in_parts=None, out_parts=None, order=None,
    megabytes=56,
):
    in_parts, out_parts = in_parts or {}, out_parts or {}
    n, m, skip = len(ins), len(outs), len(after)
    windows = {i: x[1:] for i, x in enumerate(ins) if isinstance(x, tuple)}
    ins = [x[0] if isinstance(x, tuple) else x for x in ins]
    sizes = [(windows[i][1], *x.shape[1:]) if i in windows else x.shape for i, x in enumerate(ins)]

    def body(*refs):
        in_hbm, refs = refs[:n], refs[n + skip :]
        out_hbm, refs = refs[:m], refs[m:]
        in_vmem, refs = refs[:n], refs[n:]
        out_vmem, refs = refs[:m], refs[m:]
        in_sems, refs = refs[:n], refs[n:]
        out_sems, refs = refs[:m], refs[m:]

        def copy(source, target, sem, parts, which):
            if parts == 1:
                return pltpu.make_async_copy(source, target, sem.at[0])
            size = source.shape[0] // parts
            rows = pl.ds(which * size, size)
            return pltpu.make_async_copy(source.at[rows], target.at[rows], sem.at[which])

        def load(i, which=0):
            source = in_hbm[i].at[pl.ds(*windows[i])] if i in windows else in_hbm[i]
            return copy(source, in_vmem[i], in_sems[i], in_parts.get(i, 1), which)

        def store(i, which=0):
            return copy(out_vmem[i], out_hbm[i], out_sems[i], out_parts.get(i, 1), which)

        queue = list(order or range(n))

        def more():
            while queue:
                i = queue.pop(0)
                if i is None:
                    return
                for which in range(in_parts.get(i, 1)):
                    load(i, which).start()

        def wait(i, which=0):
            load(i, which).wait()

        wait.more = more
        more()
        kernel(in_vmem, wait, out_vmem, lambda i, which=0: store(i, which).start(), *refs)
        for i in range(m):
            for which in range(out_parts.get(i, 1)):
                store(i, which).wait()

    return pl.pallas_call(
        body,
        in_specs=[anywhere] * (n + skip),
        out_specs=[anywhere] * m,
        out_shape=list(outs),
        scratch_shapes=[pltpu.VMEM(size, x.dtype) for size, x in zip(sizes, ins)]
        + [pltpu.VMEM(x.shape, x.dtype) for x in outs]
        + [pltpu.SemaphoreType.DMA((in_parts.get(i, 1),)) for i in range(n)]
        + [pltpu.SemaphoreType.DMA((out_parts.get(i, 1),)) for i in range(m)]
        + list(scratch),
        compiler_params=params(megabytes),
        cost_estimate=cost(microseconds),
        name=name,
    )(*ins, *after)


def conv_forward_kernel(
    count, first, has_partial, final, ins, wait, outs, send, raw_ref, up_ref, mid_ref, down_ref, slot_ref
):
    token_ref, mover_ref, side_ref = ins[:3]
    weight_refs, project_refs, small_refs = (ins[3 + j * count : 3 + (j + 1) * count] for j in range(3))
    extra = ins[3 + 3 * count :]
    expanded_refs, mixed_refs, acted_refs = outs[:count], outs[count : 2 * count], outs[2 * count : 3 * count]
    rows, width = token_ref.shape
    wide = count * width
    wait(0)
    for i in range(3, 3 + count):
        wait(i)
    weight = jnp.concatenate([w[...] for w in weight_refs], axis=1)
    for i in range(3 + count, 3 + 3 * count):
        wait(i)
    raw_ref[:, 0:8] = jnp.zeros((wide // 128, 8, 128), f32)
    raw_ref[:, 8 + PACK :] = jnp.zeros((wide // 128, 8, 128), f32)
    taps = jnp.concatenate([w[...] for w in small_refs], axis=1).astype(f32)
    project = jnp.concatenate([w[...] for w in project_refs], axis=0)
    total_ref = outs[3 * count]
    if first:
        shape_ref = mover_ref
        mover_ref, side_ref, segment_ref, segment_row_ref = outs[3 * count + 1 :]
        wait(1)
        wait(2)
        for pack in range(rows // PACK):
            geometry(pack, rows // PACK, shape_ref, mover_ref, side_ref, segment_ref, segment_row_ref, slot_ref)
        for i in range(3 * count + 1, 3 * count + 5):
            send(i)
    for pack in range(rows // PACK):
        base = pack * PACK
        expanded = mm(token_ref[base : base + PACK], weight)
        for tile in range(wide // 128):
            values = expanded[:, tile * 128 : tile * 128 + 128]
            raw_ref[tile, 8 : 8 + PACK] = values
            lanes = slice(tile % 3 * 128, tile % 3 * 128 + 128)
            expanded_refs[tile // 3][base : base + PACK, lanes] = values.astype(bf16)
        if pack == 0 and not first:
            wait(2)
        for tile in range(wide // 128):
            lanes = slice(tile * 128, tile * 128 + 128)
            kernel = [taps[k : k + 1, lanes] for k in range(9)]
            for start in range(0, PACK, 32):
                left = raw_ref[tile, 7 + start : 39 + start] * side_ref[base + start : base + start + 32, 0:128]
                mid = raw_ref[tile, 8 + start : 40 + start]
                right = raw_ref[tile, 9 + start : 41 + start] * side_ref[base + start : base + start + 32, 128:256]
                line = [left * kernel[3 * a] + mid * kernel[3 * a + 1] + right * kernel[3 * a + 2] for a in range(3)]
                up_ref[start : start + 32, lanes] = line[0].astype(bf16)
                mid_ref[start : start + 32, lanes] = line[1]
                down_ref[start : start + 32, lanes] = line[2].astype(bf16)
        if pack == 0 and not first:
            wait(1)
        for part in range(3):
            low, high = SPLIT[part], SPLIT[part + 1]
            hit = jnp.concatenate(
                [mover_ref[(2 * pack + which) * PACK + low : (2 * pack + which) * PACK + high] for which in range(2)], axis=1
            )
            source = jnp.concatenate(
                [
                    up_ref[UP_FROM[part] : UP_FROM[part] + SPAN],
                    down_ref[DOWN_FROM[part] : DOWN_FROM[part] + SPAN],
                ],
                axis=0,
            )
            mixed = mm(hit, source) + mid_ref[low:high]
            r = slice(base + low, base + high)
            acted = (mixed * jax.nn.sigmoid(mixed)).astype(bf16)
            mixed = mixed.astype(bf16)
            for block in range(count):
                lanes = slice(block * width, block * width + width)
                mixed_refs[block][r] = mixed[:, lanes]
                acted_refs[block][r] = acted[:, lanes]
        for i in range(3 * count):
            send(i, pack)
    for i in range(3 + 3 * count, len(ins)):
        wait(i)
    for part in range(4):
        r = slice(part * rows // 4, (part + 1) * rows // 4)
        total = mm(jnp.concatenate([a[r] for a in acted_refs], axis=1), project)
        if has_partial:
            total = total + extra[0][r]
        total_ref[r] = total
        send(3 * count, part)
        if final:
            residual_ref, attn_ref = outs[3 * count + 1 :]
            gain_conv_ref, gain_attn_ref = extra[1:]
            unit, _ = standard(total)
            residual = token_ref[r].astype(f32) + unit * gain_conv_ref[...]
            residual_ref[r] = residual
            send(3 * count + 1, part)
            unit, _ = standard(residual)
            attn_ref[r] = (unit * gain_attn_ref[...]).astype(bf16)
            send(3 * count + 2, part)


def run_conv_forward(tokens, mover, side, weights, projects, smalls, partial=None, gains=(), first=False):
    rows, width = tokens.shape
    count = len(weights)
    final = len(gains) > 0
    has_partial = partial is not None
    wide = count * width
    outs = [shaped((rows, width), bf16)] * (3 * count) + [shaped((rows, width), f32)]
    if final:
        outs += [shaped((rows, width), f32), shaped((rows, width), bf16)]
    out_parts = {i: rows // PACK if i < 3 * count else 4 for i in range(len(outs))}
    if first:
        packs = rows // PACK
        outs += [shaped((2 * rows, SPAN), bf16), shaped((rows, 256), f32), shaped((rows, 128), f32)]
        outs += [shaped((packs, 8, PACK), f32)]
    result = call_staged(
        functools.partial(conv_forward_kernel, count, first, has_partial, final),
        "conv_forward",
        [tokens, mover, side, *weights, *projects, *smalls, *([partial] if has_partial else []), *gains],
        outs,
        [
            pltpu.VMEM((wide // 128, PACK + 16, 128), f32),
            pltpu.VMEM((PACK, wide), bf16),
            pltpu.VMEM((PACK, wide), f32),
            pltpu.VMEM((PACK, wide), bf16),
            pltpu.VMEM((8, 128), f32),
        ],
        4 * count,
        out_parts=out_parts,
        order=(*((1,) if first else ()), 0, *range(3, 3 + 3 * count), 2, *(() if first else (1,)), *range(3 + 3 * count, 3 + 3 * count + has_partial + len(gains))),
    )
    return result[:count], result[count : 2 * count], result[2 * count : 3 * count], result[3 * count :]


def conv_backward_kernel(count, ins, wait, outs, send, acted_ref, low_ref, moved_ref, turned_ref):
    grad_projected_ref, mover_ref, side_ref, token_ref = ins[:4]
    gain_refs = ins[4:7]
    project_refs, mixed_refs, expanded_refs, small_refs = (ins[7 + j * count : 7 + (j + 1) * count] for j in range(4))
    grad_expanded_refs, grad_refs = outs[:count], outs[count:]
    rows, width = grad_projected_ref.shape
    tiles = width // 128
    moved_ref[:, :, 0:8] = jnp.zeros((3, tiles, 8, 128), f32)
    moved_ref[:, :, 8 + PACK :] = jnp.zeros((3, tiles, 8, 128), f32)
    wait(0)
    for block in range(count):
        mixed_ref, expanded_ref = mixed_refs[block], expanded_refs[block]
        grad_expanded_ref, grad_ref = grad_expanded_refs[block], grad_refs[block]
        wait(7 + block)
        wait(7 + 3 * count + block)
        project = project_refs[block][...]
        taps = small_refs[block][...].astype(f32)
        sums = [[jnp.zeros((8, 128), f32) for _ in range(9)] for _ in range(tiles)]
        for pack in range(rows // PACK):
            base = pack * PACK
            acted_ref[...] = mm_t(grad_projected_ref[base : base + PACK], project)
            if pack == 0:
                wait(7 + count + block)
            for tile in range(tiles):
                lanes = slice(tile * 128, tile * 128 + 128)
                for start in range(0, PACK, 64):
                    mixed = mixed_ref[base + start : base + start + 64, lanes].astype(f32)
                    gate = jax.nn.sigmoid(mixed)
                    grad = acted_ref[start : start + 64, lanes] * (gate * (1.0 + mixed * (1.0 - gate)))
                    moved_ref[1, tile, 8 + start : 72 + start] = grad
                    low_ref[start : start + 64, lanes] = grad.astype(bf16)
            if pack == 0 and block == 0:
                wait(1)
            for part in range(3):
                low, high = SPLIT[part], SPLIT[part + 1]
                for which, place, origin in ((0, 0, UP_FROM[part]), (1, 2, DOWN_FROM[part])):
                    hit = mover_ref[(2 * pack + which) * PACK + low : (2 * pack + which) * PACK + high]
                    moved = mm(hit, low_ref[origin : origin + SPAN])
                    for tile in range(tiles):
                        moved_ref[place, tile, 8 + low : 8 + high] = moved[:, tile * 128 : tile * 128 + 128]
            if pack == 0:
                if block == 0:
                    wait(2)
                wait(7 + 2 * count + block)
            for tile in range(tiles):
                lanes = slice(tile * 128, tile * 128 + 128)
                kernel = [taps[k : k + 1, lanes] for k in range(9)]
                for start in range(0, PACK, 32):
                    r = slice(base + start, base + start + 32)
                    left_mask, right_mask = side_ref[r, 0:128], side_ref[r, 128:256]
                    expanded = expanded_ref[r, lanes].astype(f32)
                    total = None
                    for a in range(3):
                        for b in range(3):
                            near = moved_ref[a, tile, 7 + b + start : 39 + b + start]
                            if b != 1:
                                near = near * (left_mask if b == 0 else right_mask)
                            tap = 8 - 3 * a - b
                            term = near * kernel[tap]
                            total = term if total is None else total + term
                            product = near * expanded
                            sums[tile][tap] = sums[tile][tap] + jnp.sum(product.reshape(4, 8, 128), axis=0)
                    grad_expanded_ref[r, lanes] = total.astype(bf16)
        send(block)
        if block == 0:
            for i in range(3, 7):
                wait(i)
            turned_ref[...] = token_ref[...].T
        grad_ref[0:width] = mm(turned_ref[...], grad_expanded_ref[...]).astype(bf16)
        depth = jnp.concatenate(
            [
                jnp.concatenate([jnp.sum(sums[tile][k], axis=0, keepdims=True) for k in range(9)], axis=0)
                for tile in range(tiles)
            ],
            axis=1,
        )
        high, rest = small_rows(gain_refs, width)
        grad_ref[width:] = jnp.concatenate([depth, high, rest, jnp.zeros((1, width), f32)], axis=0).astype(bf16)
        send(count + block)


def run_conv_backward(grad_projected, tokens, mover, side, gains, projects, smalls, expanded, mixed, after=()):
    rows, width = grad_projected.shape
    count = len(projects)
    loads = [0, 7, 7 + 3 * count, 7 + count, 1, 2, 7 + 2 * count, 3, 4, 5, 6]
    for block in range(1, count):
        loads += [7 + block, 7 + 3 * count + block, 7 + count + block, 7 + 2 * count + block]
    result = call_staged(
        functools.partial(conv_backward_kernel, count),
        "conv_backward",
        [grad_projected, mover, side, tokens, *gains, *projects, *mixed, *expanded, *smalls],
        [shaped((rows, width), bf16)] * count + [shaped((width + 16, width), bf16)] * count,
        [
            pltpu.VMEM((PACK, width), f32),
            pltpu.VMEM((PACK, width), bf16),
            pltpu.VMEM((3, width // 128, PACK + 16, 128), f32),
            pltpu.VMEM((width, rows), bf16),
        ],
        6 * count,
        after,
        order=loads,
    )
    return result[:count], result[count:]


def token_grad_kernel(ins, wait, outs, send):
    grad_one_ref, grad_refs, weight_refs = ins[0], ins[1:5], ins[5:9]
    (out_ref,) = outs
    rows = grad_one_ref.shape[0]
    for i in range(9):
        wait(i)
    weight = jnp.concatenate([w[...] for w in weight_refs], axis=1)
    for part in range(4):
        r = slice(part * rows // 4, (part + 1) * rows // 4)
        grad = jnp.concatenate([g[r] for g in grad_refs], axis=1)
        out_ref[r] = (grad_one_ref[r] + mm_t(grad, weight)).astype(bf16)
        send(0, part)


def run_token_grad(grad_one, grads, weights, after=()):
    (result,) = call_staged(
        token_grad_kernel, "token_grad", [grad_one, *grads, *weights], [shaped(grad_one.shape, bf16)], [], 4, after,
        out_parts={0: 4},
        megabytes=20,
    )
    return result


def merge_kernel(splits, unused, place_ref, *refs):
    count = len(splits)
    parts, refs = refs[: 2 * count], refs[2 * count + unused :]
    for item, split in enumerate(splits):
        total = (parts[2 * item][...].astype(f32) + parts[2 * item + 1][...].astype(f32)).astype(bf16)
        if split is None:
            refs[0][...] = total
            refs = refs[1:]
            continue
        keep_ref, send_ref = refs[:2]
        refs = refs[2:]
        half = total.shape[0] // 2
        second = place_ref[split] != 0
        keep_ref[...] = jnp.where(second, total[half:], total[:half])
        send_ref[...] = jnp.where(second, total[:half], total[half:])


def run_merge(place, items, splits, after=()):
    outs = []
    for (mine, _), split in zip(items, splits):
        rows, columns = mine.shape
        outs += [shaped((rows, columns), bf16)] if split is None else [shaped((rows // 2, columns), bf16)] * 2
    return pl.pallas_call(
        functools.partial(merge_kernel, splits, len(after)),
        in_specs=[smem] + [vmem] * (2 * len(items)) + [anywhere] * len(after),
        out_specs=[vmem] * len(outs),
        out_shape=outs,
        compiler_params=params(20),
        cost_estimate=cost(1),
        name="merge_parts",
    )(place, *[x for pair in items for x in pair], *after)


def run_join(index, mine, other, sizes, turns):
    rows, columns = mine.shape
    forms = {"plain": lambda s: (s, columns), "turned": lambda s: (columns, s), "slabs": lambda s: (columns // 128, s, 128)}
    shapes = [forms[turn](s) for s, turn in zip(sizes, turns)]
    return pl.pallas_call(
        functools.partial(join_kernel, turns),
        in_specs=[smem, vmem, vmem],
        out_specs=[vmem] * len(sizes),
        out_shape=[shaped(s, f32) for s in shapes],
        scratch_shapes=[pltpu.VMEM((2 * rows, columns), f32)],
        compiler_params=params(20),
        cost_estimate=cost(2),
        name="join_halves",
    )(index, mine, other)


def per_device(
    tokens, cotangent, shapes, head_mask, w_expand, w_depth, w_project, gain_conv, gain_attn, w_qkv, w_out,
    gain_mlp, w_up, w_down,
):
    rows, width = tokens.shape
    packs = rows // PACK
    channels = w_expand.shape[1]
    tensor_size = lax.axis_size("tensor")
    dp_size = lax.axis_size("dp")
    me_dp = lax.axis_index("dp")
    bits = [1 << b for b in range(dp_size.bit_length() - 1)]
    place = {bit: ((me_dp & bit) != 0).astype(jnp.int32) for bit in bits}

    def hold(x, after):
        return lax.optimization_barrier((x, after))[0]

    def swap_tensor(x, bit):
        return lax.ppermute(x, "tensor", [(i, i ^ bit) for i in range(tensor_size)])

    def swap_dp(x, bit):
        return lax.ppermute(x, "dp", [(i, i ^ bit) for i in range(dp_size)])

    def add(*parts):
        total = parts[0].astype(f32)
        for part in parts[1:]:
            total = total + part.astype(f32)
        return total.astype(bf16)

    def near_far(keep, pair):
        half = keep.shape[0] // 2
        return add(keep[:half], pair[:half]), add(keep[half:], pair[half:])

    def part(x, bit, mine):
        half = x.shape[0] // 2
        chosen = place[bit] if mine else 1 - place[bit]
        return lax.dynamic_slice_in_dim(x, chosen * half, half, 0)

    def halves(x, bit):
        send = part(x, bit, False)
        return part(x, bit, True), send, swap_dp(send, bit)

    def both(mine, other, bit):
        first = place[bit] == 0
        return jnp.concatenate([jnp.where(first, mine, other), jnp.where(first, other, mine)])

    def rest(x):
        for bit in bits[3:]:
            x = add(x, swap_dp(x, bit))
        return x

    other = jnp.concatenate(
        [
            w_project,
            w_depth,
            jnp.pad(head_mask.astype(bf16)[None, :], ((0, 6), (0, channels - head_mask.shape[0]))),
        ]
    )
    expand_w = [w_expand, swap_tensor(w_expand, 1)]
    other_w = [other, swap_tensor(other, 1)]
    far_expand, far_other = swap_tensor(w_expand, 2), swap_tensor(other, 2)
    project_w = [(w, 0, channels) for w in other_w]
    small_w = [(w, channels, 16) for w in other_w]
    exp_a, mix_a, act_a, (partial, mover, side, segment, segment_row) = run_conv_forward(
        tokens, shapes, shapes, expand_w, project_w, small_w, first=True
    )
    slabs, out_weight = hold((w_qkv, w_out), partial)
    slabs = slabs.transpose(1, 0, 2).reshape(-1, w_qkv.shape[2])
    slab_w = [slabs, swap_tensor(slabs, 1), swap_tensor(slabs, 2)]
    out_w = [out_weight, swap_tensor(out_weight, 1), swap_tensor(out_weight, 2)]
    far_expand, far_other = hold((far_expand, far_other), partial)
    expand_w += [far_expand, swap_tensor(far_expand, 1)]
    other_w += [far_other, swap_tensor(far_other, 1)]
    project_w = [(w, 0, channels) for w in other_w]
    small_w = [(w, channels, 16) for w in other_w]
    mlp = jnp.concatenate(hold([w_up, w_down], partial))
    mlp_w = [mlp, swap_tensor(mlp, 1), swap_tensor(mlp, 2)]
    exp_b, mix_b, act_b, (projected, residual_one, attn_low) = run_conv_forward(
        tokens, mover, side, expand_w[2:], project_w[2:], small_w[2:], partial, (gain_conv, gain_attn)
    )
    slab_w[2], out_w[2] = hold((slab_w[2], out_w[2]), attn_low)
    slab_w.append(swap_tensor(slab_w[2], 1))
    out_w.append(swap_tensor(out_w[2], 1))
    qkv, exps, inverse, merged, residual_two, mlp_low = run_attention_forward(
        attn_low, residual_one, segment, segment_row, gain_mlp, slab_w, out_w, small_w
    )
    mlp_w[2] = hold(mlp_w[2], mlp_low)
    mlp_w.append(swap_tensor(mlp_w[2], 1))
    (out_tokens, grad_two, gain_m), (mlp_0, mlp_1, mlp_2, mlp_3) = run_mlp(
        mlp_low, cotangent, residual_two, gain_mlp, mlp_w
    )
    mlp_far = add(mlp_2, swap_tensor(mlp_3, 1))
    mlp_cross = swap_tensor(mlp_far, 2)
    mlp_pair = swap_tensor(mlp_1, 1)
    grad_one, grad_projected, gain_a, gain_c, attn_0, attn_1, attn_2, attn_3 = run_attention_back(
        grad_two, qkv, exps, inverse, merged, out_w, small_w, attn_low, residual_one, projected, gain_attn, gain_conv,
        slab_w, [*act_a, *act_b], (mlp_far,),
    )
    gains = (gain_c, gain_a, gain_m)
    mlp_cross = hold(mlp_cross, grad_one)
    attn_pair_3 = swap_tensor(hold(attn_3, mlp_cross), 1)
    mlp_half, mlp_send, mlp_other = halves(add(mlp_0, mlp_pair, mlp_cross), 1)
    attn_far = add(attn_2, hold(attn_pair_3, mlp_half))
    attn_cross = swap_tensor(attn_far, 2)
    attn_pair_1 = swap_tensor(attn_1, 1)

    (grad_2, grad_3, grad_1), (conv_2, conv_3, conv_1) = run_conv_backward(
        grad_projected, tokens, mover, side, gains, [*project_w[2:], project_w[1]], [*small_w[2:], small_w[1]],
        [*exp_b, exp_a[1]], [*mix_b, mix_a[1]], (mlp_half, mlp_send, attn_far),
    )
    mlp_other = hold(mlp_other, conv_3)
    conv_pair_3 = swap_tensor(hold(conv_3, mlp_other), 1)
    conv_pair_1 = swap_tensor(hold(conv_1, mlp_other), 1)
    mlp_half, mlp_send, mlp_other = halves(add(mlp_half, mlp_other), 2)
    conv_far = add(conv_2, hold(conv_pair_3, mlp_half))
    conv_cross = swap_tensor(conv_far, 2)
    attn_half, attn_send, attn_other = halves(add(attn_0, attn_pair_1, hold(attn_cross, conv_far)), 1)

    (grad_0,), (conv_0,) = run_conv_backward(
        grad_projected, tokens, mover, side, gains, project_w[:1], small_w[:1], exp_a[:1], mix_a[:1],
        (mlp_half, mlp_send, conv_far, attn_half, attn_send),
    )
    grads_a, grads_b = [grad_0, grad_1], [grad_2, grad_3]
    places = jnp.stack([place[bit] for bit in bits[:2]])
    conv_near = add(conv_0, conv_pair_1, conv_cross)
    small = conv_near[width:]
    main = conv_near[:width]
    tail = jnp.concatenate([part(main, 1, True), small])
    tail_send = jnp.concatenate([part(main, 1, False), small])
    tail_other = swap_dp(tail_send, 1)
    attn_half, attn_send, mlp_half = run_merge(
        places, ((attn_half, attn_other), (mlp_half, mlp_other)), (1, None), (tail, tail_send)
    )
    attn_other = swap_dp(attn_send, 2)
    mlp_other = swap_dp(mlp_half, 4)
    (attn_half,) = run_merge(places, ((attn_half, attn_other),), (None,))
    attn_other = swap_dp(attn_half, 4)
    half = width // 2
    (tail,) = run_merge(places, ((tail, tail_other),), (None,), (attn_half,))
    main, small = tail[:half], tail[half:]
    tail_send = jnp.concatenate([part(main, 2, False), small])
    tail_other = swap_dp(tail_send, 2)
    tail = jnp.concatenate([part(main, 2, True), small])
    (mlp_half,) = run_merge(places, ((mlp_half, mlp_other),), (None,), (tail, tail_send))
    mlp_half = rest(mlp_half)
    mlp_other = swap_dp(mlp_half, 2)
    grad_tokens = run_token_grad(grad_one, [*grads_a, *grads_b], expand_w, (mlp_half,))
    (tail,) = run_merge(places, ((tail, tail_other),), (None,), (mlp_half,))
    tail_other = swap_dp(tail, 4)
    (attn_half,) = run_merge(places, ((attn_half, attn_other),), (None,), (tail,))
    attn_half = rest(attn_half)
    attn_other = swap_dp(attn_half, 2)
    mlp_half = both(mlp_half, mlp_other, 2)
    mlp_other = swap_dp(mlp_half, 1)
    (tail,) = run_merge(places, ((tail, tail_other),), (None,), (attn_half, mlp_half))
    tail = rest(tail)
    half = half // 2
    main, small = tail[:half], tail[half:].astype(f32)
    main_other = swap_dp(main, 2)
    attn_half = both(attn_half, attn_other, 2)
    attn_other = swap_dp(attn_half, 1)
    main = both(main, main_other, 2)
    main_other = swap_dp(main, 1)
    index = place[1][None]
    grad_up, grad_down = run_join(index, mlp_half, mlp_other, (width, width), ("plain", "turned"))
    grad_qkv, grad_out, grad_project = run_join(
        index, attn_half, attn_other, (width, w_out.shape[0], width), ("slabs", "plain", "turned")
    )
    (grad_expand,) = run_join(index, main, main_other, (width,), ("plain",))
    gain_sums = small[9:12] + small[12:15]
    return (
        out_tokens, grad_tokens, grad_expand, small[:9], grad_project, gain_sums[0], gain_sums[1],
        grad_qkv.transpose(1, 0, 2), grad_out, gain_sums[2], grad_up, grad_down,
    )


def solution(mesh):
    rows = P(("dp", "tensor"), None)
    cols = P(None, "tensor")
    down = P("tensor", None)
    return jax.shard_map(
        per_device,
        mesh=mesh,
        in_specs=(
            rows, rows, P("dp", None, None), P("tensor"), cols, cols, down, P(), P(), P(None, None, "tensor"), down,
            P(), cols, down,
        ),
        out_specs=(rows, rows, cols, cols, down, P(), P(), P(None, None, "tensor"), down, P(), cols, down),
        check_vma=False,
    )
```

```python
import functools
import jax
import jax.numpy as jnp
from jax import lax
from jax.experimental import pallas as pl
from jax.experimental.pallas import tpu as pltpu
from jax.sharding import PartitionSpec as P

HSZ = 64
PACK = 512
SPAN = 256
SPLIT = (0, 240, 480, 512)
UP_FROM = (0, 224, 256)
DOWN_FROM = (0, 240, 256)

epsilon = 1e-05
f32 = jnp.float32
bf16 = jnp.bfloat16


def mm(a, b):
    return jnp.dot(a, b, preferred_element_type=f32)


def mm_t(a, b):
    return lax.dot_general(a, b, (((1,), (1,)), ((), ())), preferred_element_type=f32)


def t_mm(a, b):
    return lax.dot_general(a, b, (((0,), (0,)), ((), ())), preferred_element_type=f32)


def standard(values):
    centred = values - jnp.mean(values, axis=-1, keepdims=True)
    inverse = lax.rsqrt(jnp.mean(centred * centred, axis=-1, keepdims=True) + epsilon)
    return centred * inverse, inverse


def standard_back(grad, unit, inverse):
    mean_grad = jnp.mean(grad, axis=-1, keepdims=True)
    mean_both = jnp.mean(grad * unit, axis=-1, keepdims=True)
    return (grad - mean_grad - unit * mean_both) * inverse


def geometry(pack, packs, shape_ref, mover_ref, side_ref, segment_ref, segment_row_ref, slot_ref):
    own = lax.axis_index("tensor") * packs + pack
    rows = slice(pack * PACK, (pack + 1) * PACK)
    slot_ref[...] = jnp.zeros_like(slot_ref)
    slot_ref[0:2, 0 : shape_ref.shape[2]] = shape_ref[own].astype(f32)
    sides = slot_ref[...]
    height_slots = sides[0:1]
    width_slots = sides[1:2]
    sizes = jnp.broadcast_to(height_slots * width_slots, (8, 128))
    before = lax.broadcasted_iota(jnp.int32, (128, 128), 0)
    after = lax.broadcasted_iota(jnp.int32, (128, 128), 1)
    ends = mm(sizes.astype(bf16), (before <= after).astype(bf16))[0:1]
    starts = ends - height_slots * width_slots
    places = lax.broadcasted_iota(jnp.int32, (PACK, 128), 0).astype(f32)
    here = ((starts <= places) & (places < ends)).astype(f32)
    image_start = jnp.sum(here * starts, axis=1, keepdims=True)
    height = jnp.sum(here * height_slots, axis=1, keepdims=True)
    width = jnp.sum(here * width_slots, axis=1, keepdims=True)
    place = places[:, 0:1]
    offset = place - image_start
    safe = jnp.maximum(width, 1.0)
    grid_row = jnp.floor((offset + 0.5) / safe)
    grid_col = offset - grid_row * safe
    above = jnp.where(grid_row >= 1.0, place - width, -1.0)
    below = jnp.where(grid_row + 1.0 < height, place + width, -1.0)
    lanes = lax.broadcasted_iota(jnp.int32, (1, SPAN), 1).astype(f32)
    for part in range(3):
        low, high = SPLIT[part], SPLIT[part + 1]
        for which, (target, origin) in enumerate(((above, UP_FROM[part]), (below, DOWN_FROM[part]))):
            hit = (target[low:high] == lanes + origin).astype(f32).astype(bf16)
            mover_ref[(2 * pack + which) * PACK + low : (2 * pack + which) * PACK + high] = hit
    side_ref[rows, 0:128] = jnp.broadcast_to((grid_col >= 1.0).astype(f32), (PACK, 128))
    side_ref[rows, 128:256] = jnp.broadcast_to((grid_col + 1.0 < width).astype(f32), (PACK, 128))
    segment = jnp.broadcast_to(image_start, (PACK, 128))
    segment_ref[rows] = segment
    segment_row_ref[pack] = segment.T[0:8]


def gelu_parts(values):
    cdf = 0.5 + 0.5 * lax.erf(values * 0.7071067811865476)
    bell = jnp.exp2(values * values * (-0.5 * 1.4426950408889634))
    return values * cdf, cdf + values * bell * 0.3989422804014327


def mlp_kernel(ins, wait, outs, send, act_ref, pre_ref, down_ref, up_ref, turned_ref, *buffers):
    mlp_ref, cotangent_ref, residual_ref, gain_ref = ins[:4]
    weight_refs = ins[4:]
    out_ref, grad_two_ref, gain_grad_ref = outs[:3]
    grad_refs = outs[3:]
    rows, width = mlp_ref.shape
    size = 256
    chunks = rows // size
    wait(0)
    turned_ref[0] = mlp_ref[...].T
    wait(1)
    turned_ref[1] = cotangent_ref[...].T

    def arrange(half, blocks):
        for side, block in enumerate(blocks):
            wait(4 + block)
            lanes = slice(side * width, (side + 1) * width)
            down_ref[half, lanes] = weight_refs[block][width:]
            up_ref[half, :, lanes] = weight_refs[block][0:width]

    arrange(0, (1, 3))
    arrange(1, (0, 2))

    def products(j, buffer):
        half = j // chunks
        r = pl.ds((j % chunks) * size, size)
        buffer[0] = mm(mlp_ref[r], up_ref[half])
        buffer[1] = mm_t(cotangent_ref[r], down_ref[half])

    def gates(j, buffer):
        half = j // chunks
        r = pl.ds((j % chunks) * size, size)
        act, slope = gelu_parts(buffer[0])
        act_ref[half, r] = act.astype(bf16)
        pre_ref[half, r] = (buffer[1] * slope).astype(bf16)

    products(0, buffers[0])

    def one(k, carry):
        products(2 * k + 1, buffers[1])
        gates(2 * k, buffers[0])
        products(jnp.minimum(2 * k + 2, 2 * chunks - 1), buffers[0])
        gates(2 * k + 1, buffers[1])
        return carry

    lax.fori_loop(0, chunks, one, 0, unroll=4)
    for half, blocks in enumerate(((1, 3), (0, 2))):
        grad_up = mm(turned_ref[0], pre_ref[half]).astype(bf16)
        grad_down = mm(turned_ref[1], act_ref[half]).astype(bf16)
        for place, block in enumerate(blocks):
            lanes = slice(place * width, (place + 1) * width)
            grad_refs[block][0:width] = grad_up[:, lanes]
            grad_refs[block][width:] = grad_down[:, lanes]
            send(3 + block)
    wait(2)
    wait(3)
    gain_grad_ref[...] = jnp.zeros_like(gain_grad_ref)

    def finish(c, carry):
        r = pl.ds(c * size, size)
        grad_in = mm_t(pre_ref[0, r], up_ref[0]) + mm_t(pre_ref[1, r], up_ref[1])
        residual = residual_ref[r]
        out = residual + (mm(act_ref[0, r], down_ref[0]) + mm(act_ref[1, r], down_ref[1]))
        out_ref[r] = out.astype(bf16)
        send(0, c)
        unit, inverse = standard(residual)
        gain_grad_ref[...] += jnp.sum((grad_in * unit).reshape(size // 8, 8, width), axis=0)
        grad_two_ref[r] = cotangent_ref[r].astype(f32) + standard_back(grad_in * gain_ref[...], unit, inverse)
        send(1, c)
        return carry

    lax.fori_loop(0, chunks, finish, 0, unroll=4)
    send(2)


def run_mlp(mlp, cotangent, residual, gain, weights):
    rows, width = mlp.shape
    channels = weights[0].shape[1]
    grads = shaped((2 * width, channels), bf16)
    wide = 2 * channels
    result = call_staged(
        mlp_kernel,
        "mlp_both",
        [mlp, cotangent, residual, gain, *weights],
        [shaped((rows, width), bf16), shaped((rows, width), f32), shaped((8, width), f32), *[grads] * 4],
        [
            pltpu.VMEM((2, rows, wide), bf16),
            pltpu.VMEM((2, rows, wide), bf16),
            pltpu.VMEM((2, wide, width), bf16),
            pltpu.VMEM((2, width, wide), bf16),
            pltpu.VMEM((2, width, rows), bf16),
            pltpu.VMEM((2, 256, wide), f32),
            pltpu.VMEM((2, 256, wide), f32),
        ],
        16,
        out_parts={0: rows // 256, 1: rows // 256},
        order=(0, 5, 7, 1, 4, 6, 2, 3),
    )
    return result[:3], result[3:]


HEADS_ON = 6


def list_heads(flag_refs, list_ref):
    count = jnp.int32(0)
    for head in range(2 * len(flag_refs)):
        on = flag(flag_refs[head // 2], head % 2)

        @pl.when(on)
        def _(count=count, head=head):
            list_ref[count] = jnp.int32(head)

        count = count + on.astype(jnp.int32)


def flag(flag_ref, side):
    return jnp.max(flag_ref[9:10, side : side + 1].astype(f32)) != 0


def lane_joined(weight_ref):
    rows = weight_ref.shape[0] // 3
    return jnp.concatenate([weight_ref[j * rows : (j + 1) * rows] for j in range(3)], axis=1)


def attention_forward_kernel(ins, wait, outs, send, list_ref, wide_ref):
    attn_ref, segment_ref, segment_row_ref, residual_ref, gain_ref = ins[:5]
    slab_refs, out_weight_refs, flag_refs = ins[5:9], ins[9:13], ins[13:17]
    qkv_ref, exps_ref, inverse_ref, merged_ref, residual_two_ref, mlp_ref = outs
    rows, width = attn_ref.shape
    for i in range(13, 17):
        wait(i)
    list_heads(flag_refs, list_ref)
    merged_ref[...] = jnp.zeros_like(merged_ref)
    inverse_ref[...] = jnp.zeros_like(inverse_ref)
    wait(5)
    wait(6)
    wait(0)
    for half in range(2):
        if half:
            wait(7)
            wait(8)
        for side in range(2):
            wide_ref[half, :, side * width : (side + 1) * width] = lane_joined(slab_refs[2 * half + side])
        projections = mm(attn_ref[...], wide_ref[half]).astype(bf16)
        for side in range(2):
            qkv_ref[2 * half + side] = projections[:, side * width : (side + 1) * width]
            send(0, 2 * half + side)
    wait(1)
    wait(2)
    lane = lax.broadcasted_iota(jnp.int32, (1, 128), 1)

    def one(i, carry):
        head = list_ref[i]
        pair = head // 2
        mine = (lane // HSZ) == (head % 2)
        scale = jnp.where(mine, HSZ**-0.5, 0.0).astype(bf16)
        for pack in range(rows // PACK):
            part = slice(pack * PACK, (pack + 1) * PACK)
            keys = qkv_ref[pair, part, 128:256]
            values = jnp.concatenate([qkv_ref[pair, part, 256:384], jnp.ones((PACK, 128), bf16)], axis=1)
            segment_row = segment_row_ref[pack, 0:1]
            for block in range(0, PACK, 256):
                r = slice(pack * PACK + block, pack * PACK + block + 256)
                scores = mm_t(qkv_ref[pair, r, 0:128] * scale, keys)
                segment = jnp.concatenate([segment_ref[r]] * (PACK // 128), axis=1)
                scores = jnp.where(segment == segment_row, scores, -1e30)
                exps = jnp.exp(scores - jnp.max(scores, axis=1, keepdims=True)).astype(bf16)
                exps_ref[i, r] = exps
                out = mm(exps, values)
                inverse = 1.0 / out[:, 128:256]
                merged_ref[pair, r] = jnp.where(mine, out[:, 0:128] * inverse, merged_ref[pair, r].astype(f32)).astype(bf16)
                inverse_ref[r] = jnp.where(lane == i, inverse, inverse_ref[r])
        send(1, i)
        return carry

    lax.fori_loop(0, HEADS_ON, one, 0, unroll=HEADS_ON)
    send(2)
    send(3)
    wait(3)
    wait(4)
    for pair in range(4):
        wait(9 + pair)
    out_weight = jnp.concatenate([w[...] for w in out_weight_refs], axis=0)
    for part in range(4):
        r = slice(part * rows // 4, (part + 1) * rows // 4)
        merged = jnp.concatenate([merged_ref[pair, r] for pair in range(4)], axis=1)
        total = residual_ref[r] + mm(merged, out_weight)
        residual_two_ref[r] = total
        send(4, part)
        unit, _ = standard(total)
        mlp_ref[r] = (unit * gain_ref[...]).astype(bf16)
        send(5, part)


def run_attention_forward(attn, residual, segment, segment_row, gain, slabs, out_weights, flags):
    rows, width = attn.shape
    outs = [
        shaped((4, rows, 384), bf16),
        shaped((HEADS_ON, rows, PACK), bf16),
        shaped((rows, 128), f32),
        shaped((4, rows, 128), bf16),
        shaped((rows, width), f32),
        shaped((rows, width), bf16),
    ]
    return call_staged(
        attention_forward_kernel,
        "attention_forward",
        [attn, segment, segment_row, residual, gain, *slabs, *out_weights, *flags],
        outs,
        [pltpu.SMEM((8,), jnp.int32), pltpu.VMEM((2, width, 768), bf16)],
        2,
        out_parts={0: 4, 1: HEADS_ON, 4: 4, 5: 4},
        order=(13, 14, 15, 16, 5, 6, 0, 7, 8, 1, 2, 9, 10, 11, 12, 4, 3),
    )


def attention_back_kernel(
    ins, wait, outs, send, list_ref, merged_grad_ref, score_ref, wide_ref, pair_ref, merged_wide_ref
):
    grad_two_ref, qkv_ref, exps_ref, inverse_ref, merged_ref = ins[:5]
    out_weight_refs, flag_refs = ins[5:9], ins[9:13]
    attn_ref, residual_ref, projected_ref, gain_attn_ref, gain_conv_ref = ins[13:18]
    slab_refs, acted_refs = ins[18:22], ins[22:26]
    grad_one_ref, grad_projected_ref, gain_attn_grad_ref, gain_conv_grad_ref = outs[:4]
    grad_refs = outs[4:]
    rows, width = grad_two_ref.shape
    for i in range(9, 13):
        wait(i)
    list_heads(flag_refs, list_ref)
    pair_ref[...] = jnp.zeros_like(pair_ref)
    gain_attn_grad_ref[...] = jnp.zeros_like(gain_attn_grad_ref)
    gain_conv_grad_ref[...] = jnp.zeros_like(gain_conv_grad_ref)
    wait(0)
    low = grad_two_ref[...].astype(bf16)
    for i in range(5, 9):
        wait(i)
    out_weight = jnp.concatenate([w[...] for w in out_weight_refs], axis=0)
    grad_merged = mm_t(low, out_weight).astype(bf16)
    for pair in range(4):
        merged_grad_ref[pair] = grad_merged[:, pair * 128 : pair * 128 + 128]
    wait(4)
    wait.more()
    for pair in range(4):
        merged_wide_ref[:, pair * 128 : pair * 128 + 128] = merged_ref[pair]
    grad_out = t_mm(merged_wide_ref[...], low).astype(bf16)
    for pair in range(4):
        grad_refs[pair][width : width + 128] = grad_out[pair * 128 : pair * 128 + 128]
    wait(1)
    wait(3)
    lane = lax.broadcasted_iota(jnp.int32, (1, 128), 1)

    def one(i, carry):
        head = list_ref[i]
        pair = head // 2
        half = head // 4
        mine = (lane // HSZ) == (head % 2)
        wait(2, i)
        for pack in range(rows // PACK):
            part = slice(pack * PACK, (pack + 1) * PACK)
            inverse = jnp.sum(jnp.where(lane == i, inverse_ref[part], 0.0), axis=1, keepdims=True)
            grad_heads = jnp.where(mine, merged_grad_ref[pair, part].astype(f32) * inverse, 0.0).astype(bf16)
            delta = jnp.sum(grad_heads.astype(f32) * merged_ref[pair, part].astype(f32), axis=1, keepdims=True)
            values = qkv_ref[pair, part, 256:384]
            for block in range(0, PACK, 256):
                r = slice(pack * PACK + block, pack * PACK + block + 256)
                b = slice(block, block + 256)
                grad_probs = mm_t(grad_heads[b], values)
                score_ref[pack, b] = (exps_ref[i, r].astype(f32) * (grad_probs - delta[b])).astype(bf16)
            grad_scores = score_ref[pack]
            grad_q = mm(grad_scores, qkv_ref[pair, part, 128:256]) * HSZ**-0.5
            grad_k = t_mm(grad_scores, qkv_ref[pair, part, 0:128]) * HSZ**-0.5
            grad_v = t_mm(exps_ref[i, part], grad_heads)
            for j, grad in enumerate((grad_q, grad_k, grad_v)):
                lanes = pl.ds(pl.multiple_of((pair % 2) * width + j * 128, 128), 128)
                pair_ref[half, part, lanes] = jnp.where(
                    mine, grad, pair_ref[half, part, lanes].astype(f32)
                ).astype(bf16)
        return carry

    lax.fori_loop(0, HEADS_ON, one, 0, unroll=3)
    for i in range(18, 22):
        wait(i)
    for half in range(2):
        for side in range(2):
            wide_ref[half, :, side * width : (side + 1) * width] = lane_joined(slab_refs[2 * half + side])
    for i in range(13, 18):
        wait(i)
    attn_t = attn_ref[...].T
    size = rows // 4
    for part in range(4):
        if part % 2:
            half = part // 2
            grad_qkv = mm(attn_t, pair_ref[half]).astype(bf16)
            for side in range(2):
                grad_refs[2 * half + side][0:width] = grad_qkv[:, side * width : (side + 1) * width]
        r = slice(part * size, (part + 1) * size)
        grad_in = mm_t(pair_ref[0, r], wide_ref[0]) + mm_t(pair_ref[1, r], wide_ref[1])
        unit, inverse = standard(residual_ref[r])
        gain_attn_grad_ref[...] += jnp.sum((grad_in * unit).reshape(size // 8, 8, width), axis=0)
        grad_one = grad_two_ref[r] + standard_back(grad_in * gain_attn_ref[...], unit, inverse)
        grad_one_ref[r] = grad_one
        unit, inverse = standard(projected_ref[r])
        gain_conv_grad_ref[...] += jnp.sum((grad_one * unit).reshape(size // 8, 8, width), axis=0)
        grad_projected_ref[r] = standard_back(grad_one * gain_conv_ref[...], unit, inverse).astype(bf16)
    for i in range(4):
        send(i)
    for i in range(22, 26):
        wait(i)
    projected_t = grad_projected_ref[...].T
    for half in (1, 0):
        acted = jnp.concatenate([acted_refs[2 * half][...], acted_refs[2 * half + 1][...]], axis=1)
        grad_project = mm(projected_t, acted).astype(bf16)
        for side in range(2):
            grad_refs[2 * half + side][width + 128 :] = grad_project[:, side * width : (side + 1) * width]
            send(4 + 2 * half + side)


def run_attention_back(
    grad_two, qkv, exps, inverse, merged, out_weights, flags, attn, residual, projected, gain_attn, gain_conv, slabs,
    acted, after=(),
):
    rows, width = grad_two.shape
    grads = shaped((2 * width + 128, 384), bf16)
    return call_staged(
        attention_back_kernel,
        "attention_back",
        [
            grad_two, qkv, exps, inverse, merged, *out_weights, *flags, attn, residual, projected, gain_attn, gain_conv,
            *slabs, *acted,
        ],
        [shaped((rows, width), f32), shaped((rows, width), bf16), *[shaped((8, width), f32)] * 2, *[grads] * 4],
        [
            pltpu.SMEM((8,), jnp.int32),
            pltpu.VMEM((4, rows, 128), bf16),
            pltpu.VMEM((rows // PACK, PACK, PACK), bf16),
            pltpu.VMEM((2, width, 2 * width), bf16),
            pltpu.VMEM((2, rows, 2 * width), bf16),
            pltpu.VMEM((rows, 512), bf16),
        ],
        24,
        after,
        in_parts={2: HEADS_ON},
        order=(9, 10, 11, 12, 5, 6, 7, 8, 0, 4, 1, 3, None, 2, *range(18, 22), *range(13, 18), *range(22, 26)),
    )


def small_rows(gain_refs, width):
    gains = jnp.concatenate([jnp.sum(ref[...], axis=0, keepdims=True) for ref in gain_refs], axis=0)
    high = gains.astype(bf16).astype(f32)
    return high, gains - high


def join_kernel(turns, index_ref, mine_ref, other_ref, *refs):
    out_refs = refs[:-1]
    whole_ref = refs[-1]
    first = index_ref[0] == 0
    rows = mine_ref.shape[0]
    mine = mine_ref[...].astype(f32)
    other = other_ref[...].astype(f32)
    whole_ref[0:rows] = jnp.where(first, mine, other)
    whole_ref[rows:] = jnp.where(first, other, mine)
    start = 0
    for out_ref, turn in zip(out_refs, turns):
        if turn == "slabs":
            rows = out_ref.shape[1]
            for j in range(out_ref.shape[0]):
                out_ref[j] = whole_ref[start : start + rows, j * 128 : j * 128 + 128]
        elif turn == "turned":
            rows = out_ref.shape[1]
            out_ref[...] = whole_ref[start : start + rows].T
        else:
            rows = out_ref.shape[0]
            out_ref[...] = whole_ref[start : start + rows]
        start += rows


def whole(shape):
    zeros = (0,) * len(shape)
    return pl.BlockSpec(shape, lambda p: zeros)


def params(megabytes=56):
    return pltpu.CompilerParams(vmem_limit_bytes=megabytes << 20)


def cost(microseconds):
    return pl.CostEstimate(
        flops=int(microseconds * 1.1e9), bytes_accessed=int(microseconds * 3.0e6), transcendentals=0
    )


smem = pl.BlockSpec(memory_space=pltpu.SMEM)


def shaped(shape, dtype):
    return jax.ShapeDtypeStruct(shape, dtype)


vmem = pl.BlockSpec(memory_space=pltpu.VMEM)
anywhere = pl.BlockSpec(memory_space=pl.ANY)


def call_staged(
    kernel, name, ins, outs, scratch, microseconds, after=(), in_parts=None, out_parts=None, order=None,
    megabytes=56,
):
    in_parts, out_parts = in_parts or {}, out_parts or {}
    n, m, skip = len(ins), len(outs), len(after)
    windows = {i: x[1:] for i, x in enumerate(ins) if isinstance(x, tuple)}
    ins = [x[0] if isinstance(x, tuple) else x for x in ins]
    sizes = [(windows[i][1], *x.shape[1:]) if i in windows else x.shape for i, x in enumerate(ins)]

    def body(*refs):
        in_hbm, refs = refs[:n], refs[n + skip :]
        out_hbm, refs = refs[:m], refs[m:]
        in_vmem, refs = refs[:n], refs[n:]
        out_vmem, refs = refs[:m], refs[m:]
        in_sems, refs = refs[:n], refs[n:]
        out_sems, refs = refs[:m], refs[m:]

        def copy(source, target, sem, parts, which):
            if parts == 1:
                return pltpu.make_async_copy(source, target, sem.at[0])
            size = source.shape[0] // parts
            rows = pl.ds(which * size, size)
            return pltpu.make_async_copy(source.at[rows], target.at[rows], sem.at[which])

        def load(i, which=0):
            source = in_hbm[i].at[pl.ds(*windows[i])] if i in windows else in_hbm[i]
            return copy(source, in_vmem[i], in_sems[i], in_parts.get(i, 1), which)

        def store(i, which=0):
            return copy(out_vmem[i], out_hbm[i], out_sems[i], out_parts.get(i, 1), which)

        queue = list(order or range(n))

        def more():
            while queue:
                i = queue.pop(0)
                if i is None:
                    return
                for which in range(in_parts.get(i, 1)):
                    load(i, which).start()

        def wait(i, which=0):
            load(i, which).wait()

        wait.more = more
        more()
        kernel(in_vmem, wait, out_vmem, lambda i, which=0: store(i, which).start(), *refs)
        for i in range(m):
            for which in range(out_parts.get(i, 1)):
                store(i, which).wait()

    return pl.pallas_call(
        body,
        in_specs=[anywhere] * (n + skip),
        out_specs=[anywhere] * m,
        out_shape=list(outs),
        scratch_shapes=[pltpu.VMEM(size, x.dtype) for size, x in zip(sizes, ins)]
        + [pltpu.VMEM(x.shape, x.dtype) for x in outs]
        + [pltpu.SemaphoreType.DMA((in_parts.get(i, 1),)) for i in range(n)]
        + [pltpu.SemaphoreType.DMA((out_parts.get(i, 1),)) for i in range(m)]
        + list(scratch),
        compiler_params=params(megabytes),
        cost_estimate=cost(microseconds),
        name=name,
    )(*ins, *after)


def conv_forward_kernel(
    count, first, has_partial, final, ins, wait, outs, send, raw_ref, up_ref, mid_ref, down_ref, slot_ref
):
    token_ref, mover_ref, side_ref = ins[:3]
    weight_refs, project_refs, small_refs = (ins[3 + j * count : 3 + (j + 1) * count] for j in range(3))
    extra = ins[3 + 3 * count :]
    expanded_refs, mixed_refs, acted_refs = outs[:count], outs[count : 2 * count], outs[2 * count : 3 * count]
    rows, width = token_ref.shape
    wide = count * width
    wait(0)
    for i in range(3, 3 + count):
        wait(i)
    weight = jnp.concatenate([w[...] for w in weight_refs], axis=1)
    for i in range(3 + count, 3 + 3 * count):
        wait(i)
    raw_ref[:, 0:8] = jnp.zeros((wide // 128, 8, 128), f32)
    raw_ref[:, 8 + PACK :] = jnp.zeros((wide // 128, 8, 128), f32)
    taps = jnp.concatenate([w[...] for w in small_refs], axis=1).astype(f32)
    project = jnp.concatenate([w[...] for w in project_refs], axis=0)
    total_ref = outs[3 * count]
    if first:
        shape_ref = mover_ref
        mover_ref, side_ref, segment_ref, segment_row_ref = outs[3 * count + 1 :]
        wait(1)
        wait(2)
        for pack in range(rows // PACK):
            geometry(pack, rows // PACK, shape_ref, mover_ref, side_ref, segment_ref, segment_row_ref, slot_ref)
        for i in range(3 * count + 1, 3 * count + 5):
            send(i)
    for pack in range(rows // PACK):
        base = pack * PACK
        expanded = mm(token_ref[base : base + PACK], weight)
        for tile in range(wide // 128):
            values = expanded[:, tile * 128 : tile * 128 + 128]
            raw_ref[tile, 8 : 8 + PACK] = values
            lanes = slice(tile % 3 * 128, tile % 3 * 128 + 128)
            expanded_refs[tile // 3][base : base + PACK, lanes] = values.astype(bf16)
        if pack == 0 and not first:
            wait(2)
        for tile in range(wide // 128):
            lanes = slice(tile * 128, tile * 128 + 128)
            kernel = [taps[k : k + 1, lanes] for k in range(9)]
            for start in range(0, PACK, 32):
                left = raw_ref[tile, 7 + start : 39 + start] * side_ref[base + start : base + start + 32, 0:128]
                mid = raw_ref[tile, 8 + start : 40 + start]
                right = raw_ref[tile, 9 + start : 41 + start] * side_ref[base + start : base + start + 32, 128:256]
                line = [left * kernel[3 * a] + mid * kernel[3 * a + 1] + right * kernel[3 * a + 2] for a in range(3)]
                up_ref[start : start + 32, lanes] = line[0].astype(bf16)
                mid_ref[start : start + 32, lanes] = line[1]
                down_ref[start : start + 32, lanes] = line[2].astype(bf16)
        if pack == 0 and not first:
            wait(1)
        for part in range(3):
            low, high = SPLIT[part], SPLIT[part + 1]
            hit = jnp.concatenate(
                [mover_ref[(2 * pack + which) * PACK + low : (2 * pack + which) * PACK + high] for which in range(2)], axis=1
            )
            source = jnp.concatenate(
                [
                    up_ref[UP_FROM[part] : UP_FROM[part] + SPAN],
                    down_ref[DOWN_FROM[part] : DOWN_FROM[part] + SPAN],
                ],
                axis=0,
            )
            mixed = mm(hit, source) + mid_ref[low:high]
            r = slice(base + low, base + high)
            acted = (mixed * jax.nn.sigmoid(mixed)).astype(bf16)
            mixed = mixed.astype(bf16)
            for block in range(count):
                lanes = slice(block * width, block * width + width)
                mixed_refs[block][r] = mixed[:, lanes]
                acted_refs[block][r] = acted[:, lanes]
        for i in range(3 * count):
            send(i, pack)
    for i in range(3 + 3 * count, len(ins)):
        wait(i)
    for part in range(4):
        r = slice(part * rows // 4, (part + 1) * rows // 4)
        total = mm(jnp.concatenate([a[r] for a in acted_refs], axis=1), project)
        if has_partial:
            total = total + extra[0][r]
        total_ref[r] = total
        send(3 * count, part)
        if final:
            residual_ref, attn_ref = outs[3 * count + 1 :]
            gain_conv_ref, gain_attn_ref = extra[1:]
            unit, _ = standard(total)
            residual = token_ref[r].astype(f32) + unit * gain_conv_ref[...]
            residual_ref[r] = residual
            send(3 * count + 1, part)
            unit, _ = standard(residual)
            attn_ref[r] = (unit * gain_attn_ref[...]).astype(bf16)
            send(3 * count + 2, part)


def run_conv_forward(tokens, mover, side, weights, projects, smalls, partial=None, gains=(), first=False):
    rows, width = tokens.shape
    count = len(weights)
    final = len(gains) > 0
    has_partial = partial is not None
    wide = count * width
    outs = [shaped((rows, width), bf16)] * (3 * count) + [shaped((rows, width), f32)]
    if final:
        outs += [shaped((rows, width), f32), shaped((rows, width), bf16)]
    out_parts = {i: rows // PACK if i < 3 * count else 4 for i in range(len(outs))}
    if first:
        packs = rows // PACK
        outs += [shaped((2 * rows, SPAN), bf16), shaped((rows, 256), f32), shaped((rows, 128), f32)]
        outs += [shaped((packs, 8, PACK), f32)]
    result = call_staged(
        functools.partial(conv_forward_kernel, count, first, has_partial, final),
        "conv_forward",
        [tokens, mover, side, *weights, *projects, *smalls, *([partial] if has_partial else []), *gains],
        outs,
        [
            pltpu.VMEM((wide // 128, PACK + 16, 128), f32),
            pltpu.VMEM((PACK, wide), bf16),
            pltpu.VMEM((PACK, wide), f32),
            pltpu.VMEM((PACK, wide), bf16),
            pltpu.VMEM((8, 128), f32),
        ],
        4 * count,
        out_parts=out_parts,
        order=(*((1,) if first else ()), 0, *range(3, 3 + 3 * count), 2, *(() if first else (1,)), *range(3 + 3 * count, 3 + 3 * count + has_partial + len(gains))),
    )
    return result[:count], result[count : 2 * count], result[2 * count : 3 * count], result[3 * count :]


def conv_backward_kernel(count, ins, wait, outs, send, acted_ref, low_ref, moved_ref, turned_ref):
    grad_projected_ref, mover_ref, side_ref, token_ref = ins[:4]
    gain_refs = ins[4:7]
    project_refs, mixed_refs, expanded_refs, small_refs = (ins[7 + j * count : 7 + (j + 1) * count] for j in range(4))
    grad_expanded_refs, grad_refs = outs[:count], outs[count:]
    rows, width = grad_projected_ref.shape
    tiles = width // 128
    moved_ref[:, :, 0:8] = jnp.zeros((3, tiles, 8, 128), f32)
    moved_ref[:, :, 8 + PACK :] = jnp.zeros((3, tiles, 8, 128), f32)
    wait(0)
    for block in range(count):
        mixed_ref, expanded_ref = mixed_refs[block], expanded_refs[block]
        grad_expanded_ref, grad_ref = grad_expanded_refs[block], grad_refs[block]
        wait(7 + block)
        wait(7 + 3 * count + block)
        project = project_refs[block][...]
        taps = small_refs[block][...].astype(f32)
        sums = [[jnp.zeros((8, 128), f32) for _ in range(9)] for _ in range(tiles)]
        for pack in range(rows // PACK):
            base = pack * PACK
            acted_ref[...] = mm_t(grad_projected_ref[base : base + PACK], project)
            if pack == 0:
                wait(7 + count + block)
            for tile in range(tiles):
                lanes = slice(tile * 128, tile * 128 + 128)
                for start in range(0, PACK, 64):
                    mixed = mixed_ref[base + start : base + start + 64, lanes].astype(f32)
                    gate = jax.nn.sigmoid(mixed)
                    grad = acted_ref[start : start + 64, lanes] * (gate * (1.0 + mixed * (1.0 - gate)))
                    moved_ref[1, tile, 8 + start : 72 + start] = grad
                    low_ref[start : start + 64, lanes] = grad.astype(bf16)
            if pack == 0 and block == 0:
                wait(1)
            for part in range(3):
                low, high = SPLIT[part], SPLIT[part + 1]
                for which, place, origin in ((0, 0, UP_FROM[part]), (1, 2, DOWN_FROM[part])):
                    hit = mover_ref[(2 * pack + which) * PACK + low : (2 * pack + which) * PACK + high]
                    moved = mm(hit, low_ref[origin : origin + SPAN])
                    for tile in range(tiles):
                        moved_ref[place, tile, 8 + low : 8 + high] = moved[:, tile * 128 : tile * 128 + 128]
            if pack == 0:
                if block == 0:
                    wait(2)
                wait(7 + 2 * count + block)
            for tile in range(tiles):
                lanes = slice(tile * 128, tile * 128 + 128)
                kernel = [taps[k : k + 1, lanes] for k in range(9)]
                for start in range(0, PACK, 32):
                    r = slice(base + start, base + start + 32)
                    left_mask, right_mask = side_ref[r, 0:128], side_ref[r, 128:256]
                    expanded = expanded_ref[r, lanes].astype(f32)
                    total = None
                    for a in range(3):
                        for b in range(3):
                            near = moved_ref[a, tile, 7 + b + start : 39 + b + start]
                            if b != 1:
                                near = near * (left_mask if b == 0 else right_mask)
                            tap = 8 - 3 * a - b
                            term = near * kernel[tap]
                            total = term if total is None else total + term
                            product = near * expanded
                            sums[tile][tap] = sums[tile][tap] + jnp.sum(product.reshape(4, 8, 128), axis=0)
                    grad_expanded_ref[r, lanes] = total.astype(bf16)
        send(block)
        if block == 0:
            for i in range(3, 7):
                wait(i)
            turned_ref[...] = token_ref[...].T
        grad_ref[0:width] = mm(turned_ref[...], grad_expanded_ref[...]).astype(bf16)
        depth = jnp.concatenate(
            [
                jnp.concatenate([jnp.sum(sums[tile][k], axis=0, keepdims=True) for k in range(9)], axis=0)
                for tile in range(tiles)
            ],
            axis=1,
        )
        high, rest = small_rows(gain_refs, width)
        grad_ref[width:] = jnp.concatenate([depth, high, rest, jnp.zeros((1, width), f32)], axis=0).astype(bf16)
        send(count + block)


def run_conv_backward(grad_projected, tokens, mover, side, gains, projects, smalls, expanded, mixed, after=()):
    rows, width = grad_projected.shape
    count = len(projects)
    loads = [0, 7, 7 + 3 * count, 7 + count, 1, 2, 7 + 2 * count, 3, 4, 5, 6]
    for block in range(1, count):
        loads += [7 + block, 7 + 3 * count + block, 7 + count + block, 7 + 2 * count + block]
    result = call_staged(
        functools.partial(conv_backward_kernel, count),
        "conv_backward",
        [grad_projected, mover, side, tokens, *gains, *projects, *mixed, *expanded, *smalls],
        [shaped((rows, width), bf16)] * count + [shaped((width + 16, width), bf16)] * count,
        [
            pltpu.VMEM((PACK, width), f32),
            pltpu.VMEM((PACK, width), bf16),
            pltpu.VMEM((3, width // 128, PACK + 16, 128), f32),
            pltpu.VMEM((width, rows), bf16),
        ],
        6 * count,
        after,
        order=loads,
    )
    return result[:count], result[count:]


def token_grad_kernel(ins, wait, outs, send):
    grad_one_ref, grad_refs, weight_refs = ins[0], ins[1:5], ins[5:9]
    (out_ref,) = outs
    rows = grad_one_ref.shape[0]
    for i in range(9):
        wait(i)
    weight = jnp.concatenate([w[...] for w in weight_refs], axis=1)
    for part in range(4):
        r = slice(part * rows // 4, (part + 1) * rows // 4)
        grad = jnp.concatenate([g[r] for g in grad_refs], axis=1)
        out_ref[r] = (grad_one_ref[r] + mm_t(grad, weight)).astype(bf16)
        send(0, part)


def run_token_grad(grad_one, grads, weights, after=()):
    (result,) = call_staged(
        token_grad_kernel, "token_grad", [grad_one, *grads, *weights], [shaped(grad_one.shape, bf16)], [], 4, after,
        out_parts={0: 4},
        megabytes=20,
    )
    return result


def merge_kernel(splits, unused, place_ref, *refs):
    count = len(splits)
    parts, refs = refs[: 2 * count], refs[2 * count + unused :]
    for item, split in enumerate(splits):
        total = (parts[2 * item][...].astype(f32) + parts[2 * item + 1][...].astype(f32)).astype(bf16)
        if split is None:
            refs[0][...] = total
            refs = refs[1:]
            continue
        keep_ref, send_ref = refs[:2]
        refs = refs[2:]
        half = total.shape[0] // 2
        second = place_ref[split] != 0
        keep_ref[...] = jnp.where(second, total[half:], total[:half])
        send_ref[...] = jnp.where(second, total[:half], total[half:])


def run_merge(place, items, splits, after=()):
    outs = []
    for (mine, _), split in zip(items, splits):
        rows, columns = mine.shape
        outs += [shaped((rows, columns), bf16)] if split is None else [shaped((rows // 2, columns), bf16)] * 2
    return pl.pallas_call(
        functools.partial(merge_kernel, splits, len(after)),
        in_specs=[smem] + [vmem] * (2 * len(items)) + [anywhere] * len(after),
        out_specs=[vmem] * len(outs),
        out_shape=outs,
        compiler_params=params(20),
        cost_estimate=cost(1),
        name="merge_parts",
    )(place, *[x for pair in items for x in pair], *after)


def run_join(index, mine, other, sizes, turns):
    rows, columns = mine.shape
    forms = {"plain": lambda s: (s, columns), "turned": lambda s: (columns, s), "slabs": lambda s: (columns // 128, s, 128)}
    shapes = [forms[turn](s) for s, turn in zip(sizes, turns)]
    return pl.pallas_call(
        functools.partial(join_kernel, turns),
        in_specs=[smem, vmem, vmem],
        out_specs=[vmem] * len(sizes),
        out_shape=[shaped(s, f32) for s in shapes],
        scratch_shapes=[pltpu.VMEM((2 * rows, columns), f32)],
        compiler_params=params(20),
        cost_estimate=cost(2),
        name="join_halves",
    )(index, mine, other)


def per_device(
    tokens, cotangent, shapes, head_mask, w_expand, w_depth, w_project, gain_conv, gain_attn, w_qkv, w_out,
    gain_mlp, w_up, w_down,
):
    rows, width = tokens.shape
    packs = rows // PACK
    channels = w_expand.shape[1]
    tensor_size = lax.axis_size("tensor")
    dp_size = lax.axis_size("dp")
    me_dp = lax.axis_index("dp")
    bits = [1 << b for b in range(dp_size.bit_length() - 1)]
    place = {bit: ((me_dp & bit) != 0).astype(jnp.int32) for bit in bits}

    def hold(x, after):
        return lax.optimization_barrier((x, after))[0]

    def swap_tensor(x, bit):
        return lax.ppermute(x, "tensor", [(i, i ^ bit) for i in range(tensor_size)])

    def swap_dp(x, bit):
        return lax.ppermute(x, "dp", [(i, i ^ bit) for i in range(dp_size)])

    def add(*parts):
        total = parts[0].astype(f32)
        for part in parts[1:]:
            total = total + part.astype(f32)
        return total.astype(bf16)

    def near_far(keep, pair):
        half = keep.shape[0] // 2
        return add(keep[:half], pair[:half]), add(keep[half:], pair[half:])

    def part(x, bit, mine):
        half = x.shape[0] // 2
        chosen = place[bit] if mine else 1 - place[bit]
        return lax.dynamic_slice_in_dim(x, chosen * half, half, 0)

    def halves(x, bit):
        send = part(x, bit, False)
        return part(x, bit, True), send, swap_dp(send, bit)

    def both(mine, other, bit):
        first = place[bit] == 0
        return jnp.concatenate([jnp.where(first, mine, other), jnp.where(first, other, mine)])

    def rest(x):
        for bit in bits[3:]:
            x = add(x, swap_dp(x, bit))
        return x

    other = jnp.concatenate(
        [
            w_project,
            w_depth,
            jnp.pad(head_mask.astype(bf16)[None, :], ((0, 6), (0, channels - head_mask.shape[0]))),
        ]
    )
    expand_w = [w_expand, swap_tensor(w_expand, 1)]
    other_w = [other, swap_tensor(other, 1)]
    far_expand, far_other = swap_tensor(w_expand, 2), swap_tensor(other, 2)
    project_w = [(w, 0, channels) for w in other_w]
    small_w = [(w, channels, 16) for w in other_w]
    exp_a, mix_a, act_a, (partial, mover, side, segment, segment_row) = run_conv_forward(
        tokens, shapes, shapes, expand_w, project_w, small_w, first=True
    )
    slabs, out_weight = hold((w_qkv, w_out), partial)
    slabs = slabs.transpose(1, 0, 2).reshape(-1, w_qkv.shape[2])
    slab_w = [slabs, swap_tensor(slabs, 1), swap_tensor(slabs, 2)]
    out_w = [out_weight, swap_tensor(out_weight, 1), swap_tensor(out_weight, 2)]
    far_expand, far_other = hold((far_expand, far_other), partial)
    expand_w += [far_expand, swap_tensor(far_expand, 1)]
    other_w += [far_other, swap_tensor(far_other, 1)]
    project_w = [(w, 0, channels) for w in other_w]
    small_w = [(w, channels, 16) for w in other_w]
    mlp = jnp.concatenate(hold([w_up, w_down], partial))
    mlp_w = [mlp, swap_tensor(mlp, 1), swap_tensor(mlp, 2)]
    exp_b, mix_b, act_b, (projected, residual_one, attn_low) = run_conv_forward(
        tokens, mover, side, expand_w[2:], project_w[2:], small_w[2:], partial, (gain_conv, gain_attn)
    )
    slab_w[2], out_w[2] = hold((slab_w[2], out_w[2]), attn_low)
    slab_w.append(swap_tensor(slab_w[2], 1))
    out_w.append(swap_tensor(out_w[2], 1))
    qkv, exps, inverse, merged, residual_two, mlp_low = run_attention_forward(
        attn_low, residual_one, segment, segment_row, gain_mlp, slab_w, out_w, small_w
    )
    mlp_w[2] = hold(mlp_w[2], mlp_low)
    mlp_w.append(swap_tensor(mlp_w[2], 1))
    (out_tokens, grad_two, gain_m), (mlp_0, mlp_1, mlp_2, mlp_3) = run_mlp(
        mlp_low, cotangent, residual_two, gain_mlp, mlp_w
    )
    mlp_far = add(mlp_2, swap_tensor(mlp_3, 1))
    mlp_cross = swap_tensor(mlp_far, 2)
    mlp_pair = swap_tensor(mlp_1, 1)
    grad_one, grad_projected, gain_a, gain_c, attn_0, attn_1, attn_2, attn_3 = run_attention_back(
        grad_two, qkv, exps, inverse, merged, out_w, small_w, attn_low, residual_one, projected, gain_attn, gain_conv,
        slab_w, [*act_a, *act_b], (mlp_far,),
    )
    gains = (gain_c, gain_a, gain_m)
    mlp_cross = hold(mlp_cross, grad_one)
    attn_pair_3 = swap_tensor(hold(attn_3, mlp_cross), 1)
    mlp_half, mlp_send, mlp_other = halves(add(mlp_0, mlp_pair, mlp_cross), 1)
    attn_far = add(attn_2, hold(attn_pair_3, mlp_half))
    attn_cross = swap_tensor(attn_far, 2)
    attn_pair_1 = swap_tensor(attn_1, 1)

    (grad_2, grad_3, grad_1), (conv_2, conv_3, conv_1) = run_conv_backward(
        grad_projected, tokens, mover, side, gains, [*project_w[2:], project_w[1]], [*small_w[2:], small_w[1]],
        [*exp_b, exp_a[1]], [*mix_b, mix_a[1]], (mlp_half, mlp_send, attn_far),
    )
    mlp_other = hold(mlp_other, conv_3)
    conv_pair_3 = swap_tensor(hold(conv_3, mlp_other), 1)
    conv_pair_1 = swap_tensor(hold(conv_1, mlp_other), 1)
    mlp_half, mlp_send, mlp_other = halves(add(mlp_half, mlp_other), 2)
    conv_far = add(conv_2, hold(conv_pair_3, mlp_half))
    conv_cross = swap_tensor(conv_far, 2)
    attn_half, attn_send, attn_other = halves(add(attn_0, attn_pair_1, hold(attn_cross, conv_far)), 1)

    (grad_0,), (conv_0,) = run_conv_backward(
        grad_projected, tokens, mover, side, gains, project_w[:1], small_w[:1], exp_a[:1], mix_a[:1],
        (mlp_half, mlp_send, conv_far, attn_half, attn_send),
    )
    grads_a, grads_b = [grad_0, grad_1], [grad_2, grad_3]
    places = jnp.stack([place[bit] for bit in bits[:2]])
    conv_near = add(conv_0, conv_pair_1, conv_cross)
    small = conv_near[width:]
    main = conv_near[:width]
    tail = jnp.concatenate([part(main, 1, True), small])
    tail_send = jnp.concatenate([part(main, 1, False), small])
    tail_other = swap_dp(tail_send, 1)
    attn_half, attn_send, mlp_half = run_merge(
        places, ((attn_half, attn_other), (mlp_half, mlp_other)), (1, None), (tail, tail_send)
    )
    attn_other = swap_dp(attn_send, 2)
    mlp_other = swap_dp(mlp_half, 4)
    (attn_half,) = run_merge(places, ((attn_half, attn_other),), (None,))
    attn_other = swap_dp(attn_half, 4)
    half = width // 2
    (tail,) = run_merge(places, ((tail, tail_other),), (None,), (attn_half,))
    main, small = tail[:half], tail[half:]
    tail_send = jnp.concatenate([part(main, 2, False), small])
    tail_other = swap_dp(tail_send, 2)
    tail = jnp.concatenate([part(main, 2, True), small])
    (mlp_half,) = run_merge(places, ((mlp_half, mlp_other),), (None,), (tail, tail_send))
    mlp_half = rest(mlp_half)
    mlp_other = swap_dp(mlp_half, 2)
    grad_tokens = run_token_grad(grad_one, [*grads_a, *grads_b], expand_w, (mlp_half,))
    (tail,) = run_merge(places, ((tail, tail_other),), (None,), (mlp_half,))
    tail_other = swap_dp(tail, 4)
    (attn_half,) = run_merge(places, ((attn_half, attn_other),), (None,), (tail,))
    attn_half = rest(attn_half)
    attn_other = swap_dp(attn_half, 2)
    mlp_half = both(mlp_half, mlp_other, 2)
    mlp_other = swap_dp(mlp_half, 1)
    (tail,) = run_merge(places, ((tail, tail_other),), (None,), (attn_half, mlp_half))
    tail = rest(tail)
    half = half // 2
    main, small = tail[:half], tail[half:].astype(f32)
    main_other = swap_dp(main, 2)
    attn_half = both(attn_half, attn_other, 2)
    attn_other = swap_dp(attn_half, 1)
    main = both(main, main_other, 2)
    main_other = swap_dp(main, 1)
    index = place[1][None]
    grad_up, grad_down = run_join(index, mlp_half, mlp_other, (width, width), ("plain", "turned"))
    grad_qkv, grad_out, grad_project = run_join(
        index, attn_half, attn_other, (width, w_out.shape[0], width), ("slabs", "plain", "turned")
    )
    (grad_expand,) = run_join(index, main, main_other, (width,), ("plain",))
    gain_sums = small[9:12] + small[12:15]
    return (
        out_tokens, grad_tokens, grad_expand, small[:9], grad_project, gain_sums[0], gain_sums[1],
        grad_qkv.transpose(1, 0, 2), grad_out, gain_sums[2], grad_up, grad_down,
    )


def solution(mesh):
    rows = P(("dp", "tensor"), None)
    cols = P(None, "tensor")
    down = P("tensor", None)
    return jax.shard_map(
        per_device,
        mesh=mesh,
        in_specs=(
            rows, rows, P("dp", None, None), P("tensor"), cols, cols, down, P(), P(), P(None, None, "tensor"), down,
            P(), cols, down,
        ),
        out_specs=(rows, rows, cols, cols, down, P(), P(), P(None, None, "tensor"), down, P(), cols, down),
        check_vma=False,
    )
```
